32 devices in a mesh: rows: 8 (over z, x), seq: 4 (over y, core).
Axes of the slice: x: 2, y: 2, z: 4, core: 2. Of those that a mesh axis runs over, the one named last changes fastest.
Arguments:
- layer_input: bfloat16 [32, 576, 768], P('rows', 'seq'), may hold values from -6 to 6
- first_gain: bfloat16 [768], replicated, may hold values from 0.25 to 1.75
- first_shift: bfloat16 [768], replicated, may hold values from -4 to 4
- input_weight: bfloat16 [768, 2304], replicated, may hold values from -0.21875 to 0.21875
- query_bias: bfloat16 [768], replicated, may hold values from -4 to 4
- value_bias: bfloat16 [768], replicated, may hold values from -4 to 4
- bias_table: bfloat16 [2209, 12], replicated, may hold values from -4 to 4
- output_weight: bfloat16 [768, 768], replicated, may hold values from -0.875 to 0.875
- output_bias: bfloat16 [768], replicated, may hold values from -4 to 4
- attention_scale: bfloat16 [768], replicated, may hold values from 0.5 to 2
- second_gain: bfloat16 [768], replicated, may hold values from 0.25 to 1.75
- second_shift: bfloat16 [768], replicated, may hold values from -4 to 4
- up_weight: bfloat16 [768, 3072], replicated, may hold values from -0.21875 to 0.21875
- up_bias: bfloat16 [3072], replicated, may hold values from -4 to 4
- down_weight: bfloat16 [3072, 768], replicated, may hold values from -0.21875 to 0.21875
- down_bias: bfloat16 [768], replicated, may hold values from -4 to 4
- feed_scale: bfloat16 [768], replicated, may hold values from 0.5 to 2
- upstream: bfloat16 [32, 576, 768], P('rows', 'seq'), may hold values from -6 to 6
- grid_heights: int32 [32, 4], P('rows'), may hold values from 1 to 23, as said below
- grid_widths: int32 [32, 4], P('rows'), may hold values from 1 to 23, as said below
- packing_order: int32 [32, 4], P('rows'), may hold values from 0 to 3, each once within a row
Outputs:
- layer_output: bfloat16 [32, 576, 768], P('rows', 'seq')
- input_gradient: float32 [32, 576, 768], P('rows', 'seq')
- first_gain_gradient: float32 [768], replicated
- first_shift_gradient: float32 [768], replicated
- input_weight_gradient: float32 [768, 2304], P('rows', 'seq')
- query_bias_gradient: float32 [768], replicated
- value_bias_gradient: float32 [768], replicated
- bias_table_gradient: float32 [2209, 12], replicated
- output_weight_gradient: float32 [768, 768], P('rows', 'seq')
- output_bias_gradient: float32 [768], replicated
- attention_scale_gradient: float32 [768], replicated
- second_gain_gradient: float32 [768], replicated
- second_shift_gradient: float32 [768], replicated
- up_weight_gradient: float32 [768, 3072], P('rows', 'seq')
- up_bias_gradient: float32 [3072], replicated
- down_weight_gradient: float32 [3072, 768], P('rows', 'seq')
- down_bias_gradient: float32 [768], replicated
- feed_scale_gradient: float32 [768], replicated
The draws below stay inside these ranges and needn't reach their ends.
Inputs may be any that keep to these rules, and one draw needn't show every extreme that they name: `grid_heights`: column 0 of each packed row is its large image, with height and width at least 21; the other images have sides of at most 3; a row's images together fill at most 576 slots. `grid_widths`: as for grid_heights, column by column.
All inputs are finite; a program needn't handle non-finite values.
Results may differ from the reference program's by a relative error of at most 0.019.
Values may be sent and summed in bfloat16 or wider, within the bound.
A program may use at most 384 MiB of HBM per device.

```python
import math
import jax
import jax.numpy as jnp
from jax import lax

D = 768
HEADS = 12
HEAD = 64
FF = 3072
GRID = 24
IMGS = 4
ROWS_DEV = 4
SLOTS = 576
ROWS = 32
RELATIVE = 2209
N_ROWS = 8


def grid_sides(key):
    first, rest = jax.random.split(key)
    large = jax.random.randint(first, (ROWS, 1), GRID - GRID // 8, GRID, dtype=jnp.int32)
    small = jax.random.randint(rest, (ROWS, IMGS - 1), 1, 4, dtype=jnp.int32)
    return jnp.concatenate([large, small], axis=1)


def draw_grid_heights(key, part):
    key = jax.random.fold_in(key, 11)
    return grid_sides(key)


def draw_grid_widths(key, part):
    key = jax.random.fold_in(key, 12)
    return grid_sides(key)


def block_scale(key, extent, cuts, low, largest):
    loudness, own = 1.0, jax.random.fold_in(key, 6)
    for position, shards_of in cuts:
        steps = jnp.exp(jax.random.uniform(jax.random.fold_in(own, position), (shards_of,), jnp.float32, low / len(cuts), largest / len(cuts)))
        loudness = loudness * jnp.repeat(steps, extent[position] // shards_of).reshape([-1 if axis == position else 1 for axis in range(len(extent))])
    return loudness


def normal_values(rng, dims, deviation, most, cuts=(), kind=jnp.bfloat16):
    values = jax.random.normal(rng, dims, jnp.float32) * deviation
    if len(cuts) > 0:
        values = block_scale(rng, dims, cuts, -0.22, 0.18) * values
    return jnp.clip(values, min=-most, max=most).astype(kind)


def setup_inputs(seed: int = 0) -> dict:
    arg_keys = jax.random.split(jax.random.key(seed), 22)
    return {
        "layer_input": normal_values(arg_keys[0], (ROWS, SLOTS, D), 1.0, 6.0, ((0, 8), (1, 4))),
        "first_gain": jnp.clip(1.0 + 0.15 * jax.random.normal(arg_keys[1], (D,), jnp.float32), 0.25, 1.75).astype(jnp.bfloat16),
        "first_shift": normal_values(arg_keys[2], (D,), 0.3, 4.0),
        "input_weight": normal_values(arg_keys[3], (D, 3 * D), D ** -0.5, 0.21875),
        "query_bias": normal_values(arg_keys[4], (D,), 0.5, 4.0),
        "value_bias": normal_values(arg_keys[5], (D,), 0.5, 4.0),
        "bias_table": normal_values(arg_keys[6], (RELATIVE, HEADS), 1.0, 4.0),
        "output_weight": normal_values(arg_keys[7], (D, D), (D // 16) ** -0.5, 0.875),
        "output_bias": normal_values(arg_keys[8], (D,), 0.3, 4.0),
        "attention_scale": jnp.clip(jnp.exp(jax.random.uniform(arg_keys[9], (D,), jnp.float32, math.log(0.5), math.log(2.0))), 0.5, 2.0).astype(jnp.bfloat16),
        "second_gain": jnp.clip(1.0 + 0.15 * jax.random.normal(arg_keys[10], (D,), jnp.float32), 0.25, 1.75).astype(jnp.bfloat16),
        "second_shift": normal_values(arg_keys[11], (D,), 0.3, 4.0),
        "up_weight": normal_values(arg_keys[12], (D, FF), D ** -0.5, 0.21875),
        "up_bias": normal_values(arg_keys[13], (FF,), 0.3, 4.0),
        "down_weight": normal_values(arg_keys[14], (FF, D), (FF // 4) ** -0.5, 0.21875),
        "down_bias": normal_values(arg_keys[15], (D,), 0.3, 4.0),
        "feed_scale": jnp.clip(jnp.exp(jax.random.uniform(arg_keys[16], (D,), jnp.float32, math.log(0.5), math.log(2.0))), 0.5, 2.0).astype(jnp.bfloat16),
        "upstream": normal_values(arg_keys[17], (ROWS, SLOTS, D), 1.0, 6.0, ((0, 8), (1, 4))),
        "grid_heights": draw_grid_heights(jax.random.fold_in(arg_keys[21], 71), 0),
        "grid_widths": draw_grid_widths(jax.random.fold_in(arg_keys[21], 71), 0),
        "packing_order": jax.vmap(lambda own: jax.random.permutation(own, IMGS))(jax.random.split(arg_keys[20], ROWS)).reshape((ROWS, IMGS)).astype(jnp.int32),
    }


EPS = 1e-06
NEGATIVE = -1e+30
HIGHEST = lax.Precision.HIGHEST

@jax.custom_vjp
def low(v):
    return lax.optimization_barrier(v.astype(jnp.bfloat16)).astype(jnp.float32)

@jax.custom_vjp
def low_back(v):
    return v

def low_keep(v):
    return (low(v), None)

def low_pass(kept, grad):
    return (grad,)

def back_keep(v):
    return (v, None)

def back_low(kept, grad):
    return (low(grad),)
low.defvjp(low_keep, low_pass)
low_back.defvjp(back_keep, back_low)

def arrange(heights, widths, order, count):
    images = heights.shape[-1]
    numbers = jnp.arange(images, dtype=jnp.int32)
    picked = order[:, :, None] == numbers[None, None, :]
    sizes = lax.optimization_barrier(jnp.sum(jnp.where(picked, (heights * widths)[:, None, :], 0), -1)).astype(jnp.int32)
    breadth = lax.optimization_barrier(jnp.sum(jnp.where(picked, widths[:, None, :], 0), -1)).astype(jnp.int32)
    finish = jnp.cumsum(sizes, -1).astype(jnp.int32)
    begin = finish - sizes
    places = jnp.arange(count, dtype=jnp.int32)[None, :, None]
    inside = (places >= begin[:, None, :]) & (places < finish[:, None, :])
    offset = places - begin[:, None, :]
    across = breadth[:, None, :]
    segment = jnp.where(jnp.any(inside, -1), lax.optimization_barrier(jnp.sum(jnp.where(inside, numbers, 0), -1)), images)
    row_number = lax.optimization_barrier(jnp.sum(jnp.where(inside, offset // across, 0), -1))
    column_number = lax.optimization_barrier(jnp.sum(jnp.where(inside, offset % across, 0), -1))
    return (segment.astype(jnp.int32), row_number.astype(jnp.int32), column_number.astype(jnp.int32))

def normalize(values, gain, shift):
    center = values - lax.optimization_barrier(jnp.mean(values, -1, keepdims=True))
    spread = lax.rsqrt(lax.optimization_barrier(jnp.mean(center * center, -1, keepdims=True)) + EPS)
    return center * spread * gain + shift

def product(left, right, form):
    return jnp.einsum(form, left, right, precision=HIGHEST)

def row_attention(items, table_heads):
    query, keys, values, segment, row_number, column_number = items
    same = segment[:, None] == segment[None, :]
    index = (row_number[:, None] - row_number[None, :] + GRID - 1) * (2 * GRID - 1) + column_number[:, None] - column_number[None, :] + GRID - 1
    score = low_back(product(query, keys, 'qhd,khd->hqk') + jnp.take(table_heads, index, axis=1))
    score = jnp.where(same[None], score, NEGATIVE)
    top = lax.optimization_barrier(jnp.max(score, -1, keepdims=True))
    weight = jnp.exp(score - top)
    total = lax.optimization_barrier(jnp.sum(weight, -1))
    mixed = product(low(weight), values, 'hqk,khd->qhd')
    return mixed / jnp.transpose(total)[..., None]

def layer(inputs, params, layout):
    first_gain, first_shift, input_weight, query_bias, value_bias, bias_table, output_weight, output_bias, attention_scale, second_gain, second_shift, up_weight, up_bias, down_weight, down_bias, feed_scale = params
    segment, row_number, column_number = layout
    first = low(normalize(inputs, first_gain, first_shift))
    mixed = product(first, input_weight, 'rsd,de->rse')
    query = low(low_back((mixed[..., :D] + query_bias) * HEAD ** (-0.5)))
    keys = low(low_back(mixed[..., D:2 * D]))
    values = low(low_back(mixed[..., 2 * D:] + value_bias))
    shape_heads = inputs.shape[:2] + (HEADS, HEAD)
    table_heads = bias_table.T

    def attend_row(items):
        return row_attention(items, table_heads)
    attended = lax.map(jax.checkpoint(attend_row), (query.reshape(shape_heads), keys.reshape(shape_heads), values.reshape(shape_heads), segment, row_number, column_number))
    attended = low(low_back(attended.reshape(inputs.shape)))
    branch = low_back(product(attended, output_weight, 'rsd,de->rse') + output_bias)
    middle = inputs + attention_scale * branch
    second = low(normalize(middle, second_gain, second_shift))
    hidden = low_back(product(second, up_weight, 'rsd,df->rsf') + up_bias)
    active = low(jax.nn.gelu(hidden, approximate=False))
    outcome = low_back(product(active, down_weight, 'rsf,fd->rsd') + down_bias)
    return middle + feed_scale * outcome

def reference(layer_input, first_gain, first_shift, input_weight, query_bias, value_bias, bias_table, output_weight, output_bias, attention_scale, second_gain, second_shift, up_weight, up_bias, down_weight, down_bias, feed_scale, upstream, grid_heights, grid_widths, packing_order):
    params = tuple((item.astype(jnp.float32) for item in (first_gain, first_shift, input_weight, query_bias, value_bias, bias_table, output_weight, output_bias, attention_scale, second_gain, second_shift, up_weight, up_bias, down_weight, down_bias, feed_scale)))
    layout = arrange(grid_heights, grid_widths, packing_order, SLOTS)

    def regroup(item):
        return item.reshape((N_ROWS, ROWS_DEV) + item.shape[1:])

    def visit(summed, items):
        block, change, segment, row_number, column_number = items

        def forward(inputs, weights):
            return layer(inputs, weights, (segment, row_number, column_number))
        result, pull = jax.vjp(forward, block.astype(jnp.float32), params)
        input_change, weight_change = pull(change.astype(jnp.float32))
        return (jax.tree.map(jnp.add, summed, weight_change), (result.astype(jnp.bfloat16), input_change))
    start = jax.tree.map(jnp.zeros_like, params)
    summed, outputs = lax.scan(visit, start, (regroup(layer_input), regroup(upstream), regroup(layout[0]), regroup(layout[1]), regroup(layout[2])))
    results, changes = outputs
    return (results.reshape(layer_input.shape), changes.reshape(layer_input.shape), summed[0], summed[1], summed[2], summed[3], summed[4], summed[5], summed[6], summed[7], summed[8], summed[9], summed[10], summed[11], summed[12], summed[13], summed[14], summed[15])
```

```python
import functools
import math

import jax
import jax.numpy as jnp
from jax import lax
from jax.experimental import pallas as pl
from jax.experimental.pallas import tpu as pltpu
from jax.sharding import PartitionSpec as P

HEADS = 12
HEAD = 64
GRID = 24
SPAN = 2 * GRID - 1
SLOTS = 576
PADDED = 640
MODEL = 768
PAIRS = HEADS // 2
WIDE = 1152
STRIP = 128
BASE = 489
COMPACT = 32
IMGS = 4
EPS = 1e-06
NEGATIVE = -1e30
CHUNK = 32
F32 = jnp.float32
BF16 = jnp.bfloat16
VMEM_LIMIT = 62 * 2**20


def dot(left, right):
    return lax.dot_general(left, right, (((1,), (0,)), ((), ())), preferred_element_type=F32)


def dot_nt(left, right):
    return lax.dot_general(left, right, (((1,), (1,)), ((), ())), preferred_element_type=F32)


def dot_tn(left, right):
    return lax.dot_general(left, right, (((0,), (0,)), ((), ())), preferred_element_type=F32)


def chunks(body):
    def step(index, carry):
        body(pl.ds(pl.multiple_of(index * CHUNK, CHUNK), CHUNK))
        return carry

    lax.fori_loop(0, SLOTS // CHUNK, step, 0)


def fold(value):
    return jnp.sum(value.reshape(value.shape[0] // 8, 8, value.shape[1]), 0)


def normal_of(values):
    center = values - jnp.mean(values, -1, keepdims=True)
    spread = lax.rsqrt(jnp.mean(center * center, -1, keepdims=True) + EPS)
    return center * spread, spread


def normal_back(change, normal, spread, gain):
    scaled = change * gain
    inner = (
        scaled
        - jnp.mean(scaled, -1, keepdims=True)
        - normal * jnp.mean(scaled * normal, -1, keepdims=True)
    )
    return inner * spread


def row_scalars(heights, widths, order, row):
    sizes, breadths, large = [], [], []
    for place in range(IMGS):
        picked = order[row, place]
        size, breadth = jnp.int32(0), jnp.int32(0)
        for image in range(IMGS):
            hit = picked == image
            size = size + jnp.where(hit, heights[row, image] * widths[row, image], 0)
            breadth = breadth + jnp.where(hit, widths[row, image], 0)
        sizes.append(size)
        breadths.append(breadth)
        large.append(jnp.where(picked == 0, 1, 0))
    begins = [jnp.int32(0)]
    for place in range(IMGS - 1):
        begins.append(begins[-1] + sizes[place])
    large_begin = sum(begins[p] * large[p] for p in range(IMGS))
    return dict(
        sizes=sizes,
        breadths=breadths,
        large=large,
        begins=begins,
        large_begin=large_begin,
        large_size=heights[row, 0] * widths[row, 0],
        large_width=widths[row, 0],
    )


def place_info(info, slot):
    segment = jnp.full(slot.shape, IMGS, jnp.int32)
    across = jnp.zeros(slot.shape, jnp.int32)
    down = jnp.zeros(slot.shape, jnp.int32)
    large = jnp.zeros(slot.shape, jnp.int32)
    for place in range(IMGS):
        offset = slot - info["begins"][place]
        inside = (offset >= 0) & (offset < info["sizes"][place])
        breadth = jnp.full(slot.shape, info["breadths"][place], jnp.int32)
        line = ((offset.astype(F32) + 0.5) / breadth.astype(F32)).astype(jnp.int32)
        segment = jnp.where(inside, place, segment)
        down = jnp.where(inside, line, down)
        across = jnp.where(inside, offset - line * breadth, across)
        large = jnp.where(inside, info["large"][place], large)
    return segment, down, across, large


def compact_index(info):
    found = []
    for axis in (0, 1):
        number = lax.broadcasted_iota(jnp.int32, (COMPACT, 128), axis)
        slot = number + jnp.where(number >= info["large_begin"], info["large_size"], 0)
        segment, down, across, large = place_info(info, slot)
        small = (segment < IMGS) & (large == 0) & (number < COMPACT)
        found.append((jnp.where(small, segment, -1 - axis), down, across))
    same = found[0][0] == found[1][0]
    row_step = found[0][1] - found[1][1] + 2
    column_step = found[0][2] - found[1][2] + 2
    return jnp.where(same, row_step * 5 + column_step, -1)


def shift_of(info, line):
    shift = BASE - (line - (GRID - 1)) * info["large_width"]
    return jnp.where(shift < 0, shift + WIDE, shift)


def prepare(info, reversed_table, near_table, picks, query_codes, key_code, bands, near):
    def rows(index, carry):
        start = pl.multiple_of(index * 64, 64)
        slot = lax.broadcasted_iota(jnp.int32, (64, 128), 0) + start
        lane = lax.broadcasted_iota(jnp.int32, (64, 128), 1)
        segment, _, across, large = place_info(info, slot)
        rank = slot - jnp.where(slot >= info["large_begin"], info["large_size"], 0)
        small = (segment < IMGS) & (large == 0)
        target = jnp.where(small, rank, -1)
        pick = (lane == target) | (lane == segment + COMPACT)
        picks[pl.ds(start, 64), :] = jnp.where(pick, 1.0, 0.0).astype(BF16)
        code = across.astype(F32)
        query_codes[0, pl.ds(start, 64), :] = jnp.where(large == 1, code, -1e9)
        query_codes[1, pl.ds(start, 64), :] = jnp.where(large == 1, code, 1e9)
        return carry

    lax.fori_loop(0, SLOTS // 64, rows, 0)
    slot = lax.broadcasted_iota(jnp.int32, (8, PADDED), 1)
    key_code[...] = place_info(info, slot)[2].astype(F32)

    lanes = lax.broadcasted_iota(jnp.int32, (16, WIDE), 1)
    width = info["large_width"]

    def line_step(line, carry):
        low, high = carry
        shift = shift_of(info, line)
        wide = jnp.concatenate([reversed_table[line], jnp.zeros((16, WIDE - 128), F32)], 1)
        rolled = pltpu.roll(wide, shift, 1)
        entry = lanes - shift
        entry = jnp.where(entry < 0, entry + WIDE, entry)
        low = jnp.where((entry >= GRID - width) & (entry <= GRID - 1), rolled, low)
        high = jnp.where((entry >= GRID) & (entry <= GRID - 2 + width), rolled, high)
        return low, high

    zero = jnp.zeros((16, WIDE), F32)
    low, high = lax.fori_loop(0, SPAN, line_step, (zero, zero))
    for head in range(HEADS):
        bands[head, 0] = jnp.broadcast_to(low[head : head + 1], (8, WIDE))
        bands[head, 1] = jnp.broadcast_to(high[head : head + 1], (8, WIDE))

    index = compact_index(info)
    across = lax.broadcasted_iota(jnp.int32, (128 - COMPACT, 128), 1) - COMPACT
    down = lax.broadcasted_iota(jnp.int32, (128 - COMPACT, 128), 0)
    inside = (across >= 0) & (across <= IMGS) & (down <= IMGS)
    for head in range(HEADS):
        value = jnp.zeros((COMPACT, 128), F32)
        for entry in range(25):
            value = jnp.where(index == entry, near_table[entry, head], value)
        near[head, 0:COMPACT, :] = value.astype(BF16)
        own = jnp.where(down == IMGS, near_table[12, head], 0.0)
        lower = jnp.where(inside, jnp.where(across == down, own, NEGATIVE), 0.0)
        near[head, COMPACT:128, :] = lower.astype(BF16)


def project_in(tokens, gain, shift, weight, query_bias, value_bias, first, query, keys, values):
    def norm(rows):
        normal, _ = normal_of(tokens[rows, :].astype(F32))
        first[rows, :] = (normal * gain[...] + shift[...]).astype(BF16)

    chunks(norm)
    step = 256
    for part, out in enumerate((query, keys, values)):
        for block in range(MODEL // step):
            lanes = slice(block * step, (block + 1) * step)
            columns = slice(part * MODEL + block * step, part * MODEL + (block + 1) * step)
            mixed = dot(first[...], weight[:, columns])
            if part == 0:
                mixed = (mixed + query_bias[:, lanes]) * HEAD**-0.5
            if part == 2:
                mixed = mixed + value_bias[:, lanes]
            out[:, lanes] = mixed.astype(BF16)


def half_mask(half):
    lane = lax.broadcasted_iota(jnp.int32, (SLOTS, 128), 1)
    return (lane < HEAD) if half == 0 else (lane >= HEAD)


def keep(mask, value):
    return jnp.where(mask, value, jnp.zeros_like(value))


def attend(query, keys, values, picks, query_codes, key_code, bands, near, chance, attended, inverse, score, low_strip, high_strip):
    def pair_step(pair, carry):
        lanes = pl.ds(pl.multiple_of(pair * 128, 128), 128)
        key_side = jnp.concatenate([keys[:, lanes], picks[...]], 1)
        result = jnp.zeros((SLOTS, 256), F32)
        for half in range(2):
            head = pair * 2 + half
            mask = half_mask(half)
            near_side = dot(picks[...], near[head]).astype(BF16)
            query_side = jnp.concatenate([keep(mask, query[:, lanes]), near_side], 1)
            score[...] = dot_nt(query_side, key_side)
            for which, strip in enumerate((low_strip, high_strip)):
                band = jnp.concatenate([bands[head, which]] * (STRIP // 8), 0)
                strip[...] = pltpu.roll(band, 0, 1, stride=1, stride_axis=0)
            for block in range(SLOTS // 64):
                rows = slice(block * 64, (block + 1) * 64)
                strip_rows = slice(block % 2 * 64, block % 2 * 64 + 64)
                start = 512 - block // 2 * 128
                strip_lanes = slice(start, start + SLOTS)
                code = key_code[0:1, 0:SLOTS]
                low_hit = query_codes[0, rows, 0:1] >= code
                high_hit = code > query_codes[1, rows, 0:1]
                bias = jnp.where(
                    low_hit,
                    low_strip[strip_rows, strip_lanes],
                    jnp.where(high_hit, high_strip[strip_rows, strip_lanes], 0.0),
                )
                part = score[rows, :] + bias
                top = jnp.max(part, -1, keepdims=True)
                chance[head, rows, 0:SLOTS] = jnp.exp(part - top).astype(BF16)
            chance[head, :, SLOTS:] = jnp.zeros((SLOTS, PADDED - SLOTS), BF16)
            value_side = jnp.concatenate(
                [keep(mask, values[:, lanes]), keep(mask, jnp.ones((SLOTS, 128), BF16))], 1
            )
            result = result + dot(chance[head, :, 0:SLOTS], value_side)
        scale = 1.0 / result[:, 128:]
        inverse[:, lanes] = scale
        attended[:, lanes] = result[:, :128] * scale
        return carry

    lax.fori_loop(0, PAIRS, pair_step, 0)


def project_out(tokens, attended, weight, bias, scale, gain, shift, branch, middle, second, attended_low):
    attended_low[...] = attended[...].astype(BF16)
    step = 256
    for block in range(MODEL // step):
        lanes = slice(block * step, (block + 1) * step)
        branch[:, lanes] = dot(attended_low[...], weight[:, lanes]) + bias[:, lanes]

    def norm(rows):
        value = tokens[rows, :].astype(F32) + scale[...] * branch[rows, :]
        middle[rows, :] = value
        normal, _ = normal_of(value)
        second[rows, :] = (normal * gain[...] + shift[...]).astype(BF16)

    chunks(norm)


def gelu_parts(value):
    square = value * value
    bell = jnp.exp(square * -0.5)
    base = 1.0 + (0.3275911 / math.sqrt(2.0)) * jnp.abs(value)
    guess = pl.reciprocal(base, approx=True)
    inner = guess * (2.0 - base * guess)
    poly = 1.061405429
    for coefficient in (-1.453152027, 1.421413741, -0.284496736, 0.254829592):
        poly = poly * inner + coefficient
    tail = 0.5 * poly * inner * bell
    share = jnp.where(value >= 0.0, 1.0 - tail, tail)
    return value * share, share + value * bell * (1.0 / math.sqrt(2.0 * math.pi))


def feed_tile(second, outcome_change, up, up_bias, down, active, slope, hidden, change):
    hidden[...] = dot(second[...], up[...]) + up_bias
    change[...] = dot_nt(outcome_change[...], down[...])

    def body(rows):
        value, gradient = gelu_parts(hidden[rows, :])
        active[rows, :] = value.astype(BF16)
        slope[rows, :] = (change[rows, :] * gradient).astype(BF16)

    chunks(body)


def feed_kernel(second, middle, upstream, up, up_bias, down, down_bias, feed_scale, output, second_change, up_unit, down_unit, up_sum, feed_sums, outcome_change, outcome, active, slope, hidden, change):
    tile = pl.program_id(0)

    @pl.when(tile == 0)
    def _():
        feed_sums[...] = jnp.zeros_like(feed_sums)

        def body(rows):
            value = (upstream[rows, :].astype(F32) * feed_scale[...]).astype(BF16)
            outcome_change[rows, :] = value
            feed_sums[1] += fold(value.astype(F32))

        chunks(body)

    feed_tile(second, outcome_change, up, up_bias[...], down, active, slope, hidden, change)
    up_unit[0] = dot_tn(second[...], slope[...]).astype(BF16)
    turned = dot_tn(outcome_change[...], active[...]).astype(BF16)
    for part in range(4):
        for half in range(2):
            down_unit[part, half] = turned[part * 192 : part * 192 + 192, half * 384 : half * 384 + 384]
    result = dot(active[...], down[...])
    back = dot_nt(slope[...], up[...])

    @pl.when(tile == 0)
    def _():
        outcome[...] = result
        second_change[...] = back

    @pl.when(tile > 0)
    def _():
        outcome[...] += result
        second_change[...] += back

    up_sum[...] = jnp.zeros_like(up_sum)

    def sums(rows):
        up_sum[0] += fold(slope[rows, :].astype(F32))

    chunks(sums)

    @pl.when(tile == pl.num_programs(0) - 1)
    def _():
        def body(rows):
            value = outcome[rows, :] + down_bias[...]
            output[rows, :] = (middle[rows, :] + feed_scale[...] * value).astype(BF16)
            feed_sums[0] += fold(upstream[rows, :].astype(F32) * value)

        chunks(body)


def attend_back(query, keys, values, picks, query_codes, key_code, chance, change_low, attended, inverse, joined, band_sums, near_sums, weight_change, score_change):
    def pair_step(pair, carry):
        lanes = pl.ds(pl.multiple_of(pair * 128, 128), 128)
        key_lanes = pl.ds(pl.multiple_of(pair * 128 + MODEL, 128), 128)
        value_lanes = pl.ds(pl.multiple_of(pair * 128 + 2 * MODEL, 128), 128)
        lane = lax.broadcasted_iota(jnp.int32, (SLOTS, 128), 1)
        own_change = change_low[:, lanes].astype(F32)
        scale = inverse[:, lanes]
        terms = own_change * attended[:, lanes]
        high = terms.astype(BF16)
        low = (terms - high.astype(F32)).astype(BF16)
        block_row = lax.broadcasted_iota(jnp.int32, (128, 128), 0) // HEAD
        block_lane = lax.broadcasted_iota(jnp.int32, (128, 128), 1) // HEAD
        block = jnp.where(block_row == block_lane, 1.0, 0.0).astype(BF16)
        delta = (dot(high, block) + dot(low, block)) * -scale
        delta_high = delta.astype(BF16)
        delta_low = (delta - delta_high.astype(F32)).astype(BF16)
        scaled = (own_change * scale).astype(BF16)
        value_side = jnp.concatenate([values[:, lanes], jnp.ones((SLOTS, 128), BF16)], 1)
        query_total = jnp.zeros((SLOTS, 128), F32)
        key_total = jnp.zeros((SLOTS, 128), F32)
        value_total = jnp.zeros((SLOTS, 128), F32)
        for half in range(2):
            head = pair * 2 + half
            mask = half_mask(half)
            extra = jnp.where(
                lane == half * HEAD,
                delta_high,
                jnp.where(lane == half * HEAD + 1, delta_low, jnp.zeros_like(delta_low)),
            )
            own_scaled = keep(mask, scaled)
            weight_change[:, 0:SLOTS] = dot_nt(jnp.concatenate([own_scaled, extra], 1), value_side)
            kinds = [jnp.zeros((16, WIDE), F32), jnp.zeros((16, WIDE), F32)]
            for group in range(STRIP // 16 - 1, -1, -1):
                tiles = [[jnp.zeros((16, 128), F32)] * (WIDE // 128) for _ in range(2)]
                for major in range(-(-SLOTS // STRIP)):
                    start = major * STRIP + group * 16
                    if start >= SLOTS:
                        continue
                    rows = slice(start, start + 16)
                    low_code = query_codes[0, rows, :]
                    high_code = query_codes[1, rows, :]
                    for column in range(-(-SLOTS // 128)):
                        span = slice(column * 128, column * 128 + 128)
                        value = chance[head, rows, span].astype(F32) * weight_change[rows, span]
                        code = jnp.broadcast_to(key_code[0:1, span], (16, 128))
                        if column * 128 + 128 > SLOTS:
                            inside = lax.broadcasted_iota(jnp.int32, (16, 128), 1) < SLOTS - column * 128
                            value = jnp.where(inside, value, 0.0)
                        score_change[rows, span] = value.astype(BF16)
                        place = 4 - major + column
                        tiles[0][place] = tiles[0][place] + jnp.where(low_code >= code, value, 0.0)
                        tiles[1][place] = tiles[1][place] + jnp.where(code > high_code, value, 0.0)
                for which in range(2):
                    fresh = jnp.concatenate(tiles[which], 1)
                    if group == STRIP // 16 - 1:
                        kinds[which] = fresh
                    else:
                        kinds[which] = pltpu.roll(kinds[which], WIDE - 16, 1) + fresh
            for which in range(2):
                band_sums[head, which] = kinds[which][0:8] + pltpu.roll(kinds[which][8:16], WIDE - 8, 1)
            own_score = score_change[:, 0:SLOTS]
            key_side = jnp.concatenate([keep(mask, keys[:, lanes]), picks[...]], 1)
            both = dot(own_score, key_side)
            query_total = query_total + both[:, :128]
            near_sums[head] = dot_tn(picks[...], both[:, 128:].astype(BF16))
            key_total = key_total + dot_tn(own_score, keep(mask, query[:, lanes]))
            value_total = value_total + dot_tn(chance[head, :, 0:SLOTS], own_scaled)
        joined[:, lanes] = (query_total.astype(BF16).astype(F32) * HEAD**-0.5).astype(BF16)
        joined[:, key_lanes] = key_total.astype(BF16)
        joined[:, value_lanes] = value_total.astype(BF16)
        return carry

    lax.fori_loop(0, PAIRS, pair_step, 0)


def table_back(info, band_sums, near_sums, table_sum):
    kinds = []
    for which in range(2):
        total = jnp.zeros((16, WIDE), F32)
        for step in range(8):
            rows = jnp.concatenate(
                [band_sums[head, which, step : step + 1, :] for head in range(HEADS)]
                + [jnp.zeros((16 - HEADS, WIDE), F32)],
                0,
            )
            total = total + (rows if step == 0 else pltpu.roll(rows, WIDE - step, 1))
        kinds.append(total)
    low, high = kinds
    width = info["large_width"]
    entry = lax.broadcasted_iota(jnp.int32, (16, 128), 1)
    low_hit = (entry >= GRID - width) & (entry <= GRID - 1)
    high_hit = (entry >= GRID) & (entry <= GRID - 2 + width)

    def line_step(line, carry):
        back = WIDE - shift_of(info, line)
        low_part = pltpu.roll(low, back, 1)[:, :128]
        high_part = pltpu.roll(high, back, 1)[:, :128]
        table_sum[line] = jnp.where(low_hit, low_part, jnp.where(high_hit, high_part, 0.0))
        return carry

    lax.fori_loop(0, SPAN, line_step, 0)
    index = compact_index(info)
    head_row = lax.broadcasted_iota(jnp.int32, (16, 128), 0)
    for row_step in range(5):
        addition = jnp.zeros((16, 128), F32)
        for column_step in range(5):
            hit = index == row_step * 5 + column_step
            column = jnp.zeros((16, 128), F32)
            for head in range(HEADS):
                part = jnp.sum(jnp.where(hit, near_sums[head, 0:COMPACT, :], 0.0), 0, keepdims=True)
                column = jnp.where(head_row == head, part, column)
            total = jnp.sum(column, 1, keepdims=True)
            addition = addition + jnp.where(entry == GRID + 1 - column_step, total, 0.0)
        if row_step == 2:
            corner = jnp.zeros((16, 128), F32)
            for head in range(HEADS):
                at = COMPACT + IMGS
                own = near_sums[head, at : at + 1, :]
                corner = jnp.where(head_row == head, own, corner)
            own = jnp.sum(jnp.where(entry == COMPACT + IMGS, corner, 0.0), 1, keepdims=True)
            addition = addition + jnp.where(entry == GRID - 1, own, 0.0)
        table_sum[GRID - 3 + row_step] += addition


def forward_kernel(heights, widths, order, near_table, reversed_table, tokens, first_gain, first_shift, input_weight, query_bias, value_bias, output_weight, output_bias, attention_scale, second_gain, second_shift, first, query, keys, values, chance, attended, inverse, branch, middle, second, attended_low, picks, query_codes, key_code, bands, near, score, low_strip, high_strip):
    info = row_scalars(heights, widths, order, lax.axis_index("seq"))
    prepare(info, reversed_table, near_table, picks, query_codes, key_code, bands, near)
    project_in(tokens, first_gain, first_shift, input_weight, query_bias, value_bias, first, query, keys, values)
    attend(query, keys, values, picks, query_codes, key_code, bands, near, chance, attended, inverse, score, low_strip, high_strip)
    project_out(tokens, attended, output_weight, output_bias, attention_scale, second_gain, second_shift, branch, middle, second, attended_low)


def backward_kernel(heights, widths, order, tokens, upstream, middle, branch, second_change, attended, attended_low, inverse, first, query, keys, values, chance, picks, query_codes, key_code, input_weight, output_weight, attention_scale, second_gain, first_gain, gradient, input_unit, output_unit, table_sum, sums, middle_change, branch_change, change_low, joined, band_sums, near_sums, weight_change, score_change, first_change):
    info = row_scalars(heights, widths, order, lax.axis_index("seq"))
    sums[...] = jnp.zeros_like(sums)

    def norm(rows):
        normal, spread = normal_of(middle[rows, :])
        change = second_change[rows, :]
        sums[6] += fold(change * normal)
        sums[7] += fold(change)
        value = upstream[rows, :].astype(F32) + normal_back(change, normal, spread, second_gain[...])
        middle_change[rows, :] = value
        sums[5] += fold(value * branch[rows, :])
        low = (value * attention_scale[...]).astype(BF16)
        branch_change[rows, :] = low
        sums[4] += fold(low.astype(F32))

    chunks(norm)
    for part in range(4):
        output_unit[part] = dot_tn(attended_low[...], branch_change[:, part * 192 : part * 192 + 192]).astype(BF16)
    change_low[...] = dot_nt(branch_change[...], output_weight[...]).astype(BF16)
    attend_back(query, keys, values, picks, query_codes, key_code, chance, change_low, attended, inverse, joined, band_sums, near_sums, weight_change, score_change)
    table_back(info, band_sums, near_sums, table_sum)
    for part in range(4):
        input_unit[part] = dot_tn(first[...], joined[:, part * 576 : part * 576 + 576]).astype(BF16)
    first_change[...] = dot_nt(joined[...], input_weight[...])

    def norm_first(rows):
        normal, spread = normal_of(tokens[rows, :].astype(F32))
        change = first_change[rows, :]
        sums[0] += fold(change * normal)
        sums[1] += fold(change)
        sums[2] += fold(joined[rows, 0:MODEL].astype(F32))
        sums[3] += fold(joined[rows, 2 * MODEL : 3 * MODEL].astype(F32))
        value = middle_change[rows, :] + normal_back(change, normal, spread, first_gain[...])
        gradient[rows, :] = value.astype(BF16)

    chunks(norm_first)


def remote(source, target, send, receive, device):
    return pltpu.make_async_remote_copy(
        src_ref=source,
        dst_ref=target,
        send_sem=send,
        recv_sem=receive,
        device_id=device,
        device_id_type=pl.DeviceIdType.MESH,
    )


def greet(devices):
    barrier = pltpu.get_barrier_semaphore()
    for device in devices:
        pl.semaphore_signal(barrier, inc=1, device_id=device, device_id_type=pl.DeviceIdType.MESH)
    pl.semaphore_wait(barrier, len(devices))


def spread_kernel(parts, tokens, upstream, full_tokens, full_upstream, send, receive, local):
    row, me = lax.axis_index("rows"), lax.axis_index("seq")
    peers = [lax.rem(me + step, parts) for step in range(1, parts)]
    greet([(row, peer) for peer in peers])
    slots = tokens.shape[1]
    mine = pl.ds(pl.multiple_of(me * slots, slots), slots)
    copies = []
    for which, (source, target) in enumerate(((tokens, full_tokens), (upstream, full_upstream))):
        for step, peer in enumerate(peers):
            copies.append(remote(source.at[peer], target.at[mine], send.at[which, step], receive.at[which, step], (row, peer)))
        copies.append(pltpu.make_async_copy(source.at[me], target.at[mine], local.at[which]))
    for copy in copies:
        copy.start()
    for copy in copies:
        copy.wait()


def gather_kernel(parts, output, gradient, own_output, own_gradient, send, receive, local):
    row, me = lax.axis_index("rows"), lax.axis_index("seq")
    peers = [lax.rem(me + step, parts) for step in range(1, parts)]
    greet([(row, peer) for peer in peers])
    slots = own_output.shape[1]
    copies = []
    for which, (source, target) in enumerate(((output, own_output), (gradient, own_gradient))):
        for step, peer in enumerate(peers):
            theirs = pl.ds(pl.multiple_of(peer * slots, slots), slots)
            copies.append(remote(source.at[theirs], target.at[me], send.at[which, step], receive.at[which, step], (row, peer)))
        mine = pl.ds(pl.multiple_of(me * slots, slots), slots)
        copies.append(pltpu.make_async_copy(source.at[mine], target.at[me], local.at[which]))
    for copy in copies:
        copy.start()
    for copy in copies:
        copy.wait()


UNITS = ((96, 576), (96, 192), (96, 768), (192, 384))
SMALL_ROWS = 512


def reduce_kernel(*refs):
    count = len(UNITS)
    units, small = refs[:count], refs[count]
    outs, small_out = refs[count + 1 : 2 * count + 1], refs[2 * count + 1]
    scratch = refs[2 * count + 2 :]
    core_in, x_in, y_in, late, line_in = (scratch[i * count : (i + 1) * count] for i in range(5))
    small_core, small_plane, small_line, small_part, send, receive, small_send, small_receive = scratch[5 * count :]
    rows, seq = lax.axis_index("rows"), lax.axis_index("seq")
    z, x = rows // 2, rows % 2
    y, core = seq // 2, seq % 2
    core_peer = (rows, y * 2 + 1 - core)
    x_peer = (z * 2 + 1 - x, seq)
    y_peer = (rows, (1 - y) * 2 + core)
    diagonal = (z * 2 + 1 - x, (1 - y) * 2 + core)
    z_peers = [(lax.rem(z + step, 4) * 2 + x, seq) for step in range(1, 4)]
    greet([core_peer, x_peer, y_peer, diagonal] + z_peers)

    small_core_copy = remote(small.at[1 - core], small_core, small_send.at[0], small_receive.at[0], core_peer)
    small_core_copy.start()
    core_copies = []
    for unit in range(count):
        for part in range(2):
            copy = remote(
                units[unit].at[part * 2 + 1 - core], core_in[unit].at[part],
                send.at[unit, part], receive.at[unit, part], core_peer,
            )
            copy.start()
            core_copies.append(copy)

    small_core_copy.wait()
    small_core[...] += small[core]
    plane = x * 2 + y
    plane_peers = ((x_peer, lax.rem(plane + 2, 4)), (y_peer, plane + 1 - 2 * y), (diagonal, 3 - plane))
    small_plane_copies = []
    for step, (peer, index) in enumerate(plane_peers):
        copy = remote(small_core.at[index], small_plane.at[step], small_send.at[1 + step], small_receive.at[1 + step], peer)
        copy.start()
        small_plane_copies.append(copy)

    first_copies = []
    for unit in range(count):
        half = UNITS[unit][0] // 2
        for part in range(2):
            core_copies[unit * 2 + part].wait()
        held = core_in[unit]

        def add(index, carry, held=held, unit=unit):
            line = index // 2
            for part in range(2):
                held[part, line, index % 2] = (
                    held[part, line, index % 2].astype(F32)
                    + units[unit][part * 2 + core, line, index % 2].astype(F32)
                ).astype(BF16)
            return carry

        lax.fori_loop(0, 8, add, 0)
        copy_x = remote(
            held.at[:, :, 1 - x, 0:half], x_in[unit], send.at[unit, 2], receive.at[unit, 2], x_peer
        )
        copy_y = remote(
            held.at[1 - y, :, :, half:], y_in[unit], send.at[unit, 3], receive.at[unit, 3], y_peer
        )
        copy_x.start()
        copy_y.start()
        first_copies.append((copy_x, copy_y))

    for copy in small_plane_copies:
        copy.wait()
    small_part[...] = small_core[plane] + small_plane[0] + small_plane[1] + small_plane[2]
    small_line_copies = []
    for step, peer in enumerate(z_peers):
        index = lax.rem(z + step + 1, 4)
        copy = remote(small_part.at[index], small_line.at[step], small_send.at[4 + step], small_receive.at[4 + step], peer)
        copy.start()
        small_line_copies.append(copy)

    second_copies = []
    for unit in range(count):
        half = UNITS[unit][0] // 2
        copy_x, copy_y = first_copies[unit]
        copy_x.wait()
        for part in range(2):
            for line in range(4):
                x_in[unit][part, line] = (
                    x_in[unit][part, line].astype(F32) + core_in[unit][part, line, x, 0:half].astype(F32)
                ).astype(BF16)
        again_y = remote(
            x_in[unit].at[1 - y], late[unit].at[:, 0:half], send.at[unit, 4], receive.at[unit, 4], y_peer
        )
        again_y.start()
        copy_y.wait()
        for line in range(4):
            for side in range(2):
                y_in[unit][line, side] = (
                    y_in[unit][line, side].astype(F32) + core_in[unit][y, line, side, half:].astype(F32)
                ).astype(BF16)
        again_x = remote(
            y_in[unit].at[:, 1 - x], late[unit].at[:, half:], send.at[unit, 5], receive.at[unit, 5], x_peer
        )
        again_x.start()
        second_copies.append((again_y, again_x))

    for copy in small_line_copies:
        copy.wait()
    own = small_part[z] + small_line[0] + small_line[1] + small_line[2]
    small_out[core, plane, z] = own
    gather = []
    for step, peer in enumerate(z_peers):
        copy = remote(
            small_out.at[core, plane, z], small_out.at[core, plane, z], small_send.at[7 + step], small_receive.at[7 + step], peer
        )
        copy.start()
        gather.append(copy)

    line_copies = []
    for unit in range(count):
        half = UNITS[unit][0] // 2
        again_y, again_x = second_copies[unit]
        again_y.wait()
        again_x.wait()
        for line in range(4):
            late[unit][line, 0:half] = (
                late[unit][line, 0:half].astype(F32) + x_in[unit][y, line].astype(F32)
            ).astype(BF16)
            late[unit][line, half:] = (
                late[unit][line, half:].astype(F32) + y_in[unit][line, x].astype(F32)
            ).astype(BF16)
        copies = []
        for step, peer in enumerate(z_peers):
            copy = remote(
                late[unit].at[lax.rem(z + step + 1, 4)], line_in[unit].at[step],
                send.at[unit, 6 + step], receive.at[unit, 6 + step], peer,
            )
            copy.start()
            copies.append(copy)
        line_copies.append(copies)

    for copy in gather:
        copy.wait()
    plane_gather = []
    for step, (peer, _) in enumerate(plane_peers):
        copy = remote(
            small_out.at[core, plane], small_out.at[core, plane], small_send.at[10 + step], small_receive.at[10 + step], peer
        )
        copy.start()
        plane_gather.append(copy)
    for copy in plane_gather:
        copy.wait()
    last = remote(small_out.at[core], small_out.at[core], small_send.at[13], small_receive.at[13], core_peer)
    last.start()

    for unit in range(count):
        for copy in line_copies[unit]:
            copy.wait()
        total = late[unit][z].astype(F32)
        for step in range(3):
            total = total + line_in[unit][step].astype(F32)
        outs[unit][...] = total
    last.wait()


def reduce_small_mesh(units, small):
    count = len(UNITS)
    scratch = []
    for shape in (
        lambda r, c: (2, 4, 2, r, c),
        lambda r, c: (2, 4, r // 2, c),
        lambda r, c: (4, 2, r // 2, c),
        lambda r, c: (4, r, c),
        lambda r, c: (3, r, c),
    ):
        scratch += [pltpu.VMEM(shape(*unit), BF16) for unit in UNITS]
    scratch += [
        pltpu.VMEM((4, 4, 16, 128), F32),
        pltpu.VMEM((3, 4, 16, 128), F32),
        pltpu.VMEM((3, 16, 128), F32),
        pltpu.VMEM((4, 16, 128), F32),
        pltpu.SemaphoreType.DMA((count, 9)),
        pltpu.SemaphoreType.DMA((count, 9)),
        pltpu.SemaphoreType.DMA((14,)),
        pltpu.SemaphoreType.DMA((14,)),
    ]
    shaped = [item.reshape((4, 4, 2) + unit) for item, unit in zip(units, UNITS)]
    results = pl.pallas_call(
        reduce_kernel,
        out_shape=[jax.ShapeDtypeStruct(unit, F32) for unit in UNITS]
        + [jax.ShapeDtypeStruct((2, 4, 4, 16, 128), F32)],
        in_specs=[whole()] * (count + 1),
        out_specs=[whole()] * (count + 1),
        scratch_shapes=scratch,
        compiler_params=pltpu.CompilerParams(
            collective_id=2, has_side_effects=True, vmem_limit_bytes=VMEM_LIMIT
        ),
        name="reduce",
    )(*shaped, small.reshape(2, 4, 4, 16, 128))
    return list(results[:count]), results[count].reshape(SMALL_ROWS, 128)


def reduce_any_mesh(units, small):
    done = []
    for item in units:
        part = lax.psum_scatter(item.reshape((4, -1) + item.shape[-2:]), "seq", scatter_dimension=0, tiled=True)
        part = part.reshape(part.shape[1:])
        count = lax.axis_size("rows")
        part = part.reshape((count, -1, part.shape[-1]))
        part = lax.psum_scatter(part, "rows", scatter_dimension=0, tiled=True)
        done.append(part.reshape(part.shape[1:]).astype(F32))
    return done, lax.psum(small, ("rows", "seq"))


def whole():
    return pl.BlockSpec(memory_space=pltpu.VMEM)


def scalars():
    return pl.BlockSpec(memory_space=pltpu.SMEM)


def on_device(layer_input, first_gain, first_shift, input_weight, query_bias, value_bias, bias_table, output_weight, output_bias, attention_scale, second_gain, second_shift, up_weight, up_bias, down_weight, down_bias, feed_scale, upstream, grid_heights, grid_widths, packing_order):
    parts = lax.axis_size("seq")
    slots = layer_input.shape[1]
    hidden_units = up_weight.shape[1]

    def line(item):
        return item.reshape(1, -1)

    def shape(*dims, dtype=F32):
        return jax.ShapeDtypeStruct(dims, dtype)

    table = bias_table.reshape(SPAN, SPAN, HEADS)
    reversed_table = jnp.pad(
        jnp.transpose(table[:, ::-1, :], (0, 2, 1)).astype(F32),
        ((0, 0), (0, 16 - HEADS), (0, 128 - SPAN)),
    )
    near_table = table[GRID - 3 : GRID + 2, GRID - 3 : GRID + 2].reshape(25, HEADS).astype(F32)

    tokens, own_upstream = pl.pallas_call(
        functools.partial(spread_kernel, parts),
        out_shape=[shape(SLOTS, MODEL, dtype=BF16)] * 2,
        in_specs=[whole()] * 2,
        out_specs=[whole()] * 2,
        scratch_shapes=[
            pltpu.SemaphoreType.DMA((2, parts - 1)),
            pltpu.SemaphoreType.DMA((2, parts - 1)),
            pltpu.SemaphoreType.DMA((2,)),
        ],
        compiler_params=pltpu.CompilerParams(collective_id=0, has_side_effects=True, vmem_limit_bytes=VMEM_LIMIT),
        name="spread",
    )(layer_input, upstream)

    full = (SLOTS, MODEL)
    first, query, keys, values, chance, attended, inverse, branch, middle, second, attended_low, picks, query_codes, key_code = pl.pallas_call(
        forward_kernel,
        out_shape=[shape(*full, dtype=BF16)] * 4
        + [shape(HEADS, SLOTS, PADDED, dtype=BF16)]
        + [shape(*full)] * 4
        + [shape(*full, dtype=BF16)] * 2
        + [shape(SLOTS, 128, dtype=BF16), shape(2, SLOTS, 128), shape(8, PADDED)],
        in_specs=[scalars()] * 4 + [whole()] * 12,
        out_specs=[whole()] * 14,
        scratch_shapes=[
            pltpu.VMEM((HEADS, 2, 8, WIDE), F32),
            pltpu.VMEM((HEADS, 128, 128), BF16),
            pltpu.VMEM((SLOTS, SLOTS), F32),
            pltpu.VMEM((STRIP, WIDE), F32),
            pltpu.VMEM((STRIP, WIDE), F32),
        ],
        compiler_params=pltpu.CompilerParams(vmem_limit_bytes=VMEM_LIMIT),
        name="forward",
    )(
        grid_heights, grid_widths, packing_order, near_table, reversed_table, tokens,
        line(first_gain), line(first_shift), input_weight, line(query_bias), line(value_bias),
        output_weight, line(output_bias), line(attention_scale), line(second_gain), line(second_shift),
    )

    tiles = hidden_units // MODEL

    def fixed(*dims):
        return pl.BlockSpec(dims, lambda tile: (0,) * len(dims))

    output, second_change, up_unit, down_unit, up_sum, feed_sums = pl.pallas_call(
        feed_kernel,
        grid=(tiles,),
        out_shape=[
            shape(*full, dtype=BF16),
            shape(*full),
            shape(4, MODEL, MODEL, dtype=BF16),
            shape(4, 8, 192, 384, dtype=BF16),
            shape(tiles, 8, MODEL),
            shape(2, 8, MODEL),
        ],
        in_specs=[
            fixed(*full),
            fixed(*full),
            fixed(*full),
            pl.BlockSpec((MODEL, MODEL), lambda tile: (0, tile)),
            pl.BlockSpec((1, MODEL), lambda tile: (0, tile)),
            pl.BlockSpec((MODEL, MODEL), lambda tile: (tile, 0)),
            fixed(1, MODEL),
            fixed(1, MODEL),
        ],
        out_specs=[
            fixed(*full),
            fixed(*full),
            pl.BlockSpec((1, MODEL, MODEL), lambda tile: (tile, 0, 0)),
            pl.BlockSpec((4, 2, 192, 384), lambda tile: (0, tile, 0, 0)),
            pl.BlockSpec((1, 8, MODEL), lambda tile: (tile, 0, 0)),
            fixed(2, 8, MODEL),
        ],
        scratch_shapes=[
            pltpu.VMEM(full, BF16),
            pltpu.VMEM(full, F32),
            pltpu.VMEM(full, BF16),
            pltpu.VMEM(full, BF16),
            pltpu.VMEM(full, F32),
            pltpu.VMEM(full, F32),
        ],
        compiler_params=pltpu.CompilerParams(vmem_limit_bytes=VMEM_LIMIT),
        name="feed",
    )(second, middle, own_upstream, up_weight, line(up_bias), down_weight, line(down_bias), line(feed_scale))

    gradient, input_unit, output_unit, table_sum, sums = pl.pallas_call(
        backward_kernel,
        out_shape=[
            shape(*full, dtype=BF16),
            shape(4, MODEL, 576, dtype=BF16),
            shape(4, MODEL, 192, dtype=BF16),
            shape(SPAN, 16, 128),
            shape(8, 8, MODEL),
        ],
        in_specs=[scalars()] * 3 + [whole()] * 21,
        out_specs=[whole()] * 5,
        scratch_shapes=[
            pltpu.VMEM(full, F32),
            pltpu.VMEM(full, BF16),
            pltpu.VMEM(full, BF16),
            pltpu.VMEM((SLOTS, 3 * MODEL), BF16),
            pltpu.VMEM((HEADS, 2, 8, WIDE), F32),
            pltpu.VMEM((HEADS, 128, 128), F32),
            pltpu.VMEM((SLOTS, PADDED), F32),
            pltpu.VMEM((SLOTS, PADDED), BF16),
            pltpu.VMEM(full, F32),
        ],
        input_output_aliases={},
        compiler_params=pltpu.CompilerParams(vmem_limit_bytes=VMEM_LIMIT),
        name="backward",
    )(
        grid_heights, grid_widths, packing_order, tokens, own_upstream, middle, branch, second_change,
        attended, attended_low, inverse, first, query, keys, values, chance, picks, query_codes, key_code,
        input_weight, output_weight, line(attention_scale), line(second_gain), line(first_gain),
    )

    own_output, own_gradient = pl.pallas_call(
        functools.partial(gather_kernel, parts),
        out_shape=[shape(parts, slots, MODEL, dtype=BF16)] * 2,
        in_specs=[whole()] * 2,
        out_specs=[whole()] * 2,
        scratch_shapes=[
            pltpu.SemaphoreType.DMA((2, parts - 1)),
            pltpu.SemaphoreType.DMA((2, parts - 1)),
            pltpu.SemaphoreType.DMA((2,)),
        ],
        compiler_params=pltpu.CompilerParams(collective_id=1, has_side_effects=True, vmem_limit_bytes=VMEM_LIMIT),
        name="gather",
    )(output, gradient)

    vectors = jnp.concatenate([jnp.sum(sums, 1), jnp.sum(feed_sums, 1), jnp.sum(up_sum, 1)], 0)
    table_flat = jnp.concatenate([table_sum[:, :HEADS, :64], jnp.zeros((1, HEADS, 64), F32)], 0)
    table_flat = table_flat.reshape(-1, 128)
    vector_flat = vectors.reshape(-1, 128)
    used = table_flat.shape[0] + vector_flat.shape[0]
    small = jnp.concatenate([table_flat, vector_flat, jnp.zeros((SMALL_ROWS - used, 128), F32)], 0)
    units = (input_unit, output_unit, up_unit, down_unit)
    if (lax.axis_size("rows"), parts) == (8, 4):
        done, small = reduce_small_mesh(units, small)
        done[3] = done[3].T
    else:
        done, small = reduce_any_mesh(units[:3] + (jnp.transpose(down_unit, (0, 1, 3, 2)),), small)
    table_done = small[: table_flat.shape[0]].reshape(SPAN + 1, HEADS, 64)[:SPAN, :, :SPAN]
    table_done = jnp.transpose(table_done[:, :, ::-1], (0, 2, 1)).reshape(-1, HEADS)
    vectors = small[table_flat.shape[0] : used].reshape(-1, MODEL)
    return (
        own_output,
        own_gradient.astype(F32),
        vectors[0],
        vectors[1],
        done[0],
        vectors[2],
        vectors[3],
        table_done,
        done[1],
        vectors[4],
        vectors[5],
        vectors[6],
        vectors[7],
        done[2],
        vectors[10:].reshape(-1),
        done[3],
        vectors[9],
        vectors[8],
    )


def solution(mesh):
    split = P("rows", "seq", None)
    lines = P("rows", None)
    block = P("rows", "seq")
    in_specs = (split,) + (P(),) * 16 + (split, lines, lines, lines)
    out_specs = (split, split, P(), P(), block, P(), P(), P(), block, P(), P(), P(), P(), block, P(), block, P(), P())
    return jax.shard_map(on_device, mesh=mesh, in_specs=in_specs, out_specs=out_specs, check_vma=False)
```

```python
import functools
import math

import jax
import jax.numpy as jnp
from jax import lax
from jax.experimental import pallas as pl
from jax.experimental.pallas import tpu as pltpu
from jax.sharding import PartitionSpec as P

HEADS = 12
HEAD = 64
GRID = 24
SPAN = 2 * GRID - 1
SLOTS = 576
PADDED = 640
MODEL = 768
PAIRS = HEADS // 2
WIDE = 1152
STRIP = 128
BASE = 489
COMPACT = 32
IMGS = 4
EPS = 1e-06
NEGATIVE = -1e30
CHUNK = 32
PARTS = 4
BLOCKS = 8
TILES = 3
F32 = jnp.float32
BF16 = jnp.bfloat16
VMEM_LIMIT = 63 * 2**20


def dot(left, right):
    return lax.dot_general(left, right, (((1,), (0,)), ((), ())), preferred_element_type=F32)


def dot_nt(left, right):
    return lax.dot_general(left, right, (((1,), (1,)), ((), ())), preferred_element_type=F32)


def dot_tn(left, right):
    return lax.dot_general(left, right, (((0,), (0,)), ((), ())), preferred_element_type=F32)


def chunks(body):
    def step(index, carry):
        body(pl.ds(pl.multiple_of(index * CHUNK, CHUNK), CHUNK))
        return carry

    lax.fori_loop(0, SLOTS // CHUNK, step, 0)


def fold(value):
    return jnp.sum(value.reshape(value.shape[0] // 8, 8, value.shape[1]), 0)


def normal_of(values):
    center = values - jnp.mean(values, -1, keepdims=True)
    spread = lax.rsqrt(jnp.mean(center * center, -1, keepdims=True) + EPS)
    return center * spread, spread


def normal_back(change, normal, spread, gain):
    scaled = change * gain
    inner = (
        scaled
        - jnp.mean(scaled, -1, keepdims=True)
        - normal * jnp.mean(scaled * normal, -1, keepdims=True)
    )
    return inner * spread


def row_scalars(heights, widths, order, row):
    sizes, breadths, large = [], [], []
    for place in range(IMGS):
        picked = order[row, place]
        size, breadth = jnp.int32(0), jnp.int32(0)
        for image in range(IMGS):
            hit = picked == image
            size = size + jnp.where(hit, heights[row, image] * widths[row, image], 0)
            breadth = breadth + jnp.where(hit, widths[row, image], 0)
        sizes.append(size)
        breadths.append(breadth)
        large.append(jnp.where(picked == 0, 1, 0))
    begins = [jnp.int32(0)]
    for place in range(IMGS - 1):
        begins.append(begins[-1] + sizes[place])
    large_begin = sum(begins[p] * large[p] for p in range(IMGS))
    return dict(
        sizes=sizes,
        breadths=breadths,
        large=large,
        begins=begins,
        large_begin=large_begin,
        large_size=heights[row, 0] * widths[row, 0],
        large_width=widths[row, 0],
    )


def place_info(info, slot):
    segment = jnp.full(slot.shape, IMGS, jnp.int32)
    across = jnp.zeros(slot.shape, jnp.int32)
    down = jnp.zeros(slot.shape, jnp.int32)
    large = jnp.zeros(slot.shape, jnp.int32)
    for place in range(IMGS):
        offset = slot - info["begins"][place]
        inside = (offset >= 0) & (offset < info["sizes"][place])
        breadth = jnp.full(slot.shape, info["breadths"][place], jnp.int32)
        line = ((offset.astype(F32) + 0.5) / breadth.astype(F32)).astype(jnp.int32)
        segment = jnp.where(inside, place, segment)
        down = jnp.where(inside, line, down)
        across = jnp.where(inside, offset - line * breadth, across)
        large = jnp.where(inside, info["large"][place], large)
    return segment, down, across, large


def compact_index(info):
    found = []
    for axis in (0, 1):
        number = lax.broadcasted_iota(jnp.int32, (COMPACT, 128), axis)
        slot = number + jnp.where(number >= info["large_begin"], info["large_size"], 0)
        segment, down, across, large = place_info(info, slot)
        small = (segment < IMGS) & (large == 0) & (number < COMPACT)
        found.append((jnp.where(small, segment, -1 - axis), down, across))
    same = found[0][0] == found[1][0]
    row_step = found[0][1] - found[1][1] + 2
    column_step = found[0][2] - found[1][2] + 2
    return jnp.where(same, row_step * 5 + column_step, -1)


def shift_of(info, line):
    shift = BASE - (line - (GRID - 1)) * info["large_width"]
    return jnp.where(shift < 0, shift + WIDE, shift)


def prepare(info, reversed_table, near_table, picks, query_codes, key_code, bands, near):
    def rows(index, carry):
        start = pl.multiple_of(index * 64, 64)
        slot = lax.broadcasted_iota(jnp.int32, (64, 128), 0) + start
        lane = lax.broadcasted_iota(jnp.int32, (64, 128), 1)
        segment, _, across, large = place_info(info, slot)
        rank = slot - jnp.where(slot >= info["large_begin"], info["large_size"], 0)
        small = (segment < IMGS) & (large == 0)
        target = jnp.where(small, rank, -1)
        pick = (lane == target) | (lane == segment + COMPACT)
        picks[pl.ds(start, 64), :] = jnp.where(pick, 1.0, 0.0).astype(BF16)
        code = across.astype(F32)
        query_codes[0, pl.ds(start, 64), :] = jnp.where(large == 1, code, -1e9)
        query_codes[1, pl.ds(start, 64), :] = jnp.where(large == 1, code, 1e9)
        return carry

    lax.fori_loop(0, SLOTS // 64, rows, 0)
    slot = lax.broadcasted_iota(jnp.int32, (8, PADDED), 1)
    key_code[...] = place_info(info, slot)[2].astype(F32)

    lanes = lax.broadcasted_iota(jnp.int32, (16, WIDE), 1)
    width = info["large_width"]

    def line_step(line, carry):
        low, high = carry
        shift = shift_of(info, line)
        wide = jnp.concatenate([reversed_table[line], jnp.zeros((16, WIDE - 128), F32)], 1)
        rolled = pltpu.roll(wide, shift, 1)
        entry = lanes - shift
        entry = jnp.where(entry < 0, entry + WIDE, entry)
        low = jnp.where((entry >= GRID - width) & (entry <= GRID - 1), rolled, low)
        high = jnp.where((entry >= GRID) & (entry <= GRID - 2 + width), rolled, high)
        return low, high

    zero = jnp.zeros((16, WIDE), F32)
    low, high = lax.fori_loop(0, SPAN, line_step, (zero, zero))
    for head in range(HEADS):
        bands[head, 0] = jnp.broadcast_to(low[head : head + 1], (8, WIDE))
        bands[head, 1] = jnp.broadcast_to(high[head : head + 1], (8, WIDE))

    index = compact_index(info)
    across = lax.broadcasted_iota(jnp.int32, (128 - COMPACT, 128), 1) - COMPACT
    down = lax.broadcasted_iota(jnp.int32, (128 - COMPACT, 128), 0)
    inside = (across >= 0) & (across <= IMGS) & (down <= IMGS)
    for head in range(HEADS):
        value = jnp.zeros((COMPACT, 128), F32)
        for entry in range(25):
            value = jnp.where(index == entry, near_table[entry, head], value)
        near[head, 0:COMPACT, :] = value.astype(BF16)
        own = jnp.where(down == IMGS, near_table[12, head], 0.0)
        lower = jnp.where(inside, jnp.where(across == down, own, NEGATIVE), 0.0)
        near[head, COMPACT:128, :] = lower.astype(BF16)


def project_in(tokens, gain, shift, weight, query_bias, value_bias, first, query, keys, values):
    def norm(rows):
        normal, _ = normal_of(tokens[rows, :].astype(F32))
        first[rows, :] = (normal * gain[...] + shift[...]).astype(BF16)

    chunks(norm)
    step = 256
    for part, out in enumerate((query, keys, values)):
        for block in range(MODEL // step):
            lanes = slice(block * step, (block + 1) * step)
            columns = slice(part * MODEL + block * step, part * MODEL + (block + 1) * step)
            mixed = dot(first[...], weight[:, columns])
            if part == 0:
                mixed = (mixed + query_bias[:, lanes]) * HEAD**-0.5
            if part == 2:
                mixed = mixed + value_bias[:, lanes]
            out[:, lanes] = mixed.astype(BF16)


def half_mask(half):
    lane = lax.broadcasted_iota(jnp.int32, (SLOTS, 128), 1)
    return (lane < HEAD) if half == 0 else (lane >= HEAD)


def keep(mask, value):
    return jnp.where(mask, value, jnp.zeros_like(value))


def attend(query, keys, values, picks, query_codes, key_code, bands, near, chance, attended, inverse, score, low_strip, high_strip):
    def pair_step(pair, carry):
        lanes = pl.ds(pl.multiple_of(pair * 128, 128), 128)
        key_side = jnp.concatenate([keys[:, lanes], picks[...]], 1)
        result = jnp.zeros((SLOTS, 256), F32)
        for half in range(2):
            head = pair * 2 + half
            mask = half_mask(half)
            near_side = dot(picks[...], near[head]).astype(BF16)
            query_side = jnp.concatenate([keep(mask, query[:, lanes]), near_side], 1)
            score[...] = dot_nt(query_side, key_side)
            for which, strip in enumerate((low_strip, high_strip)):
                band = jnp.concatenate([bands[head, which]] * (STRIP // 8), 0)
                strip[...] = pltpu.roll(band, 0, 1, stride=1, stride_axis=0)
            for block in range(SLOTS // 64):
                rows = slice(block * 64, (block + 1) * 64)
                strip_rows = slice(block % 2 * 64, block % 2 * 64 + 64)
                start = 512 - block // 2 * 128
                strip_lanes = slice(start, start + SLOTS)
                code = key_code[0:1, 0:SLOTS]
                low_hit = query_codes[0, rows, 0:1] >= code
                high_hit = code > query_codes[1, rows, 0:1]
                bias = jnp.where(
                    low_hit,
                    low_strip[strip_rows, strip_lanes],
                    jnp.where(high_hit, high_strip[strip_rows, strip_lanes], 0.0),
                )
                part = score[rows, :] + bias
                top = jnp.max(part, -1, keepdims=True)
                chance[head, rows, 0:SLOTS] = jnp.exp(part - top).astype(BF16)
            chance[head, :, SLOTS:] = jnp.zeros((SLOTS, PADDED - SLOTS), BF16)
            value_side = jnp.concatenate(
                [keep(mask, values[:, lanes]), keep(mask, jnp.ones((SLOTS, 128), BF16))], 1
            )
            result = result + dot(chance[head, :, 0:SLOTS], value_side)
        scale = 1.0 / result[:, 128:]
        inverse[:, lanes] = scale
        attended[:, lanes] = result[:, :128] * scale
        return carry

    lax.fori_loop(0, PAIRS, pair_step, 0)


def project_out(tokens, attended, weight, bias, scale, gain, shift, branch, middle, second, attended_low):
    attended_low[...] = attended[...].astype(BF16)
    step = 256
    for block in range(MODEL // step):
        lanes = slice(block * step, (block + 1) * step)
        branch[:, lanes] = dot(attended_low[...], weight[:, lanes]) + bias[:, lanes]

    def norm(rows):
        value = tokens[rows, :].astype(F32) + scale[...] * branch[rows, :]
        middle[rows, :] = value
        normal, _ = normal_of(value)
        second[rows, :] = (normal * gain[...] + shift[...]).astype(BF16)

    chunks(norm)


def gelu_parts(value):
    square = value * value
    bell = jnp.exp(square * -0.5)
    base = 1.0 + (0.3275911 / math.sqrt(2.0)) * jnp.abs(value)
    guess = pl.reciprocal(base, approx=True)
    inner = guess * (2.0 - base * guess)
    poly = 1.061405429
    for coefficient in (-1.453152027, 1.421413741, -0.284496736, 0.254829592):
        poly = poly * inner + coefficient
    tail = 0.5 * poly * inner * bell
    share = jnp.where(value >= 0.0, 1.0 - tail, tail)
    return value * share, share + value * bell * (1.0 / math.sqrt(2.0 * math.pi))


def feed(second, upstream, up, up_bias, down, down_bias, feed_scale, middle, output, second_change, unit_of, up_sum, feed_sums, outcome_change, outcome, active, slope, hidden, change, up_tile, down_tile, sems, after=None):
    def loads(tile):
        slot = tile % 2
        copies = []
        for block in range(BLOCKS):
            start = 3 * 128 * block + 128 * tile
            inside = slice(block * 128, block * 128 + 128)
            copies.append(
                pltpu.make_async_copy(
                    up.at[:, start : start + 128], up_tile.at[slot, :, inside], sems.at[slot, 0, block]
                )
            )
            copies.append(
                pltpu.make_async_copy(
                    down.at[start : start + 128], down_tile.at[slot, inside], sems.at[slot, 1, block]
                )
            )
        return copies

    for copy in loads(0):
        copy.start()
    feed_sums[...] = jnp.zeros_like(feed_sums)

    def begin(rows):
        value = (upstream[rows, :].astype(F32) * feed_scale[...]).astype(BF16)
        outcome_change[rows, :] = value
        feed_sums[1] += fold(value.astype(F32))

    chunks(begin)
    for tile in range(TILES):
        slot = tile % 2
        if tile + 1 < TILES:
            for copy in loads(tile + 1):
                copy.start()
        for copy in loads(tile):
            copy.wait()
        starts = [3 * 128 * block + 128 * tile for block in range(BLOCKS)]
        bias = jnp.concatenate([up_bias[:, start : start + 128] for start in starts], 1)
        hidden[...] = dot(second[...], up_tile[slot]) + bias
        change[...] = dot_nt(outcome_change[...], down_tile[slot])

        def body(rows):
            value, gradient = gelu_parts(hidden[rows, :])
            active[rows, :] = value.astype(BF16)
            low = (change[rows, :] * gradient).astype(BF16)
            slope[rows, :] = low

        chunks(body)
        result = dot(active[...], down_tile[slot])
        back = dot_nt(slope[...], up_tile[slot])
        if tile == 0:
            outcome[...] = result
            second_change[...] = back
        else:
            outcome[...] += result
            second_change[...] += back
        unit = unit_of(tile)
        ones = jnp.ones((8, SLOTS), BF16)
        total = dot(ones, slope[...])
        for block in range(BLOCKS):
            inside = slice(block * 128, block * 128 + 128)
            up_sum[:, starts[block] : starts[block] + 128] = total[:, inside]
        turned = dot_tn(second[...], slope[...]).astype(BF16)
        for block in range(BLOCKS):
            inside = slice(block * 128, block * 128 + 128)
            part, half = block // 2, block % 2
            unit[part, :, :, half * 128 : half * 128 + 128] = turned[:, inside].reshape(BLOCKS, 96, 128)
        turned = dot_tn(outcome_change[...], active[...]).astype(BF16)
        for block in range(BLOCKS):
            inside = slice(block * 128, block * 128 + 128)
            for part in range(PARTS):
                for half in range(2):
                    start = part * 192 + half * 96
                    unit[part, block, :, 256 + half * 128 : 384 + half * 128] = turned[start : start + 96, inside]
        if after is not None:
            after(tile)

    def end(rows):
        value = outcome[rows, :] + down_bias[...]
        output[rows, :] = (middle[rows, :] + feed_scale[...] * value).astype(BF16)
        feed_sums[0] += fold(upstream[rows, :].astype(F32) * value)

    chunks(end)


def attend_back(query, keys, values, picks, query_codes, key_code, chance_of, change_low, attended, inverse, joined, band_sums, near_sums, weight_change, score_change, event):
    def pair_step(pair, carry):
        event(pair)
        chance = chance_of(pair)
        lanes = pl.ds(pl.multiple_of(pair * 128, 128), 128)
        key_lanes = pl.ds(pl.multiple_of(pair * 128 + MODEL, 128), 128)
        value_lanes = pl.ds(pl.multiple_of(pair * 128 + 2 * MODEL, 128), 128)
        lane = lax.broadcasted_iota(jnp.int32, (SLOTS, 128), 1)
        own_change = change_low[:, lanes].astype(F32)
        scale = inverse[:, lanes]
        terms = own_change * attended[:, lanes]
        high = terms.astype(BF16)
        low = (terms - high.astype(F32)).astype(BF16)
        block_row = lax.broadcasted_iota(jnp.int32, (128, 128), 0) // HEAD
        block_lane = lax.broadcasted_iota(jnp.int32, (128, 128), 1) // HEAD
        block = jnp.where(block_row == block_lane, 1.0, 0.0).astype(BF16)
        delta = (dot(high, block) + dot(low, block)) * -scale
        delta_high = delta.astype(BF16)
        delta_low = (delta - delta_high.astype(F32)).astype(BF16)
        scaled = (own_change * scale).astype(BF16)
        value_side = jnp.concatenate([values[:, lanes], jnp.ones((SLOTS, 128), BF16)], 1)
        query_total = jnp.zeros((SLOTS, 128), F32)
        key_total = jnp.zeros((SLOTS, 128), F32)
        value_total = jnp.zeros((SLOTS, 128), F32)
        for half in range(2):
            head = pair * 2 + half
            mask = half_mask(half)
            extra = jnp.where(
                lane == half * HEAD,
                delta_high,
                jnp.where(lane == half * HEAD + 1, delta_low, jnp.zeros_like(delta_low)),
            )
            own_scaled = keep(mask, scaled)
            weight_change[:, 0:SLOTS] = dot_nt(jnp.concatenate([own_scaled, extra], 1), value_side)
            kinds = [jnp.zeros((16, WIDE), F32), jnp.zeros((16, WIDE), F32)]
            for group in range(STRIP // 16 - 1, -1, -1):
                tiles = [[jnp.zeros((16, 128), F32)] * (WIDE // 128) for _ in range(2)]
                for major in range(-(-SLOTS // STRIP)):
                    start = major * STRIP + group * 16
                    if start >= SLOTS:
                        continue
                    rows = slice(start, start + 16)
                    low_code = query_codes[0, rows, :]
                    high_code = query_codes[1, rows, :]
                    for column in range(-(-SLOTS // 128)):
                        span = slice(column * 128, column * 128 + 128)
                        value = chance[half, rows, span].astype(F32) * weight_change[rows, span]
                        code = jnp.broadcast_to(key_code[0:1, span], (16, 128))
                        if column * 128 + 128 > SLOTS:
                            inside = lax.broadcasted_iota(jnp.int32, (16, 128), 1) < SLOTS - column * 128
                            value = jnp.where(inside, value, 0.0)
                        score_change[rows, span] = value.astype(BF16)
                        place = 4 - major + column
                        tiles[0][place] = tiles[0][place] + jnp.where(low_code >= code, value, 0.0)
                        tiles[1][place] = tiles[1][place] + jnp.where(code > high_code, value, 0.0)
                for which in range(2):
                    fresh = jnp.concatenate(tiles[which], 1)
                    if group == STRIP // 16 - 1:
                        kinds[which] = fresh
                    else:
                        kinds[which] = pltpu.roll(kinds[which], WIDE - 16, 1) + fresh
            for which in range(2):
                band_sums[head, which] = kinds[which][0:8] + pltpu.roll(kinds[which][8:16], WIDE - 8, 1)
            own_score = score_change[:, 0:SLOTS]
            key_side = jnp.concatenate([keep(mask, keys[:, lanes]), picks[...]], 1)
            both = dot(own_score, key_side)
            query_total = query_total + both[:, :128]
            near_sums[head] = dot_tn(picks[...], both[:, 128:].astype(BF16))
            key_total = key_total + dot_tn(own_score, keep(mask, query[:, lanes]))
            value_total = value_total + dot_tn(chance[half, :, 0:SLOTS], own_scaled)
        joined[:, lanes] = (query_total.astype(BF16).astype(F32) * HEAD**-0.5).astype(BF16)
        joined[:, key_lanes] = key_total.astype(BF16)
        joined[:, value_lanes] = value_total.astype(BF16)
        return carry

    lax.fori_loop(0, PAIRS, pair_step, 0)


def table_back(info, band_sums, near_sums, table_sum):
    kinds = []
    for which in range(2):
        total = jnp.zeros((16, WIDE), F32)
        for step in range(8):
            rows = jnp.concatenate(
                [band_sums[head, which, step : step + 1, :] for head in range(HEADS)]
                + [jnp.zeros((16 - HEADS, WIDE), F32)],
                0,
            )
            total = total + (rows if step == 0 else pltpu.roll(rows, WIDE - step, 1))
        kinds.append(total)
    low, high = kinds
    width = info["large_width"]
    entry = lax.broadcasted_iota(jnp.int32, (16, 128), 1)
    low_hit = (entry >= GRID - width) & (entry <= GRID - 1)
    high_hit = (entry >= GRID) & (entry <= GRID - 2 + width)

    def line_step(line, carry):
        back = WIDE - shift_of(info, line)
        low_part = pltpu.roll(low, back, 1)[:, :128]
        high_part = pltpu.roll(high, back, 1)[:, :128]
        table_sum[line] = jnp.where(low_hit, low_part, jnp.where(high_hit, high_part, 0.0))
        return carry

    lax.fori_loop(0, SPAN, line_step, 0)
    index = compact_index(info)
    head_row = lax.broadcasted_iota(jnp.int32, (16, 128), 0)
    for row_step in range(5):
        addition = jnp.zeros((16, 128), F32)
        for column_step in range(5):
            hit = index == row_step * 5 + column_step
            column = jnp.zeros((16, 128), F32)
            for head in range(HEADS):
                part = jnp.sum(jnp.where(hit, near_sums[head, 0:COMPACT, :], 0.0), 0, keepdims=True)
                column = jnp.where(head_row == head, part, column)
            total = jnp.sum(column, 1, keepdims=True)
            addition = addition + jnp.where(entry == GRID + 1 - column_step, total, 0.0)
        if row_step == 2:
            corner = jnp.zeros((16, 128), F32)
            for head in range(HEADS):
                at = COMPACT + IMGS
                own = near_sums[head, at : at + 1, :]
                corner = jnp.where(head_row == head, own, corner)
            own = jnp.sum(jnp.where(entry == COMPACT + IMGS, corner, 0.0), 1, keepdims=True)
            addition = addition + jnp.where(entry == GRID - 1, own, 0.0)
        table_sum[GRID - 3 + row_step] += addition


def feed_kernel(second, middle, upstream, up, up_bias, down, down_bias, feed_scale, output, second_change, units, up_sum, feed_sums, outcome_change, outcome, active, slope, hidden, change, up_tile, down_tile, sems):
    feed(second, upstream, up, up_bias, down, down_bias, feed_scale, middle, output, second_change, lambda tile: units.at[tile], up_sum, feed_sums, outcome_change, outcome, active, slope, hidden, change, up_tile, down_tile, sems)


def remote(source, target, send, receive, device):
    return pltpu.make_async_remote_copy(
        src_ref=source,
        dst_ref=target,
        send_sem=send,
        recv_sem=receive,
        device_id=device,
        device_id_type=pl.DeviceIdType.MESH,
    )


def greet(devices):
    barrier = pltpu.get_barrier_semaphore()
    for device in devices:
        pl.semaphore_signal(barrier, inc=1, device_id=device, device_id_type=pl.DeviceIdType.MESH)
    pl.semaphore_wait(barrier, len(devices))


def group_peers(parts):
    row, me = lax.axis_index("rows"), lax.axis_index("seq")
    return row, me, [lax.rem(me + step, parts) for step in range(1, parts)]


def block_of(index, size):
    return pl.ds(pl.multiple_of(index * size, size), size)


def forward_kernel(heights, widths, order, near_table, reversed_table, own_tokens, own_upstream, first_gain, first_shift, input_weight, query_bias, value_bias, output_weight, output_bias, attention_scale, second_gain, second_shift, tokens, upstream, first, query, keys, values, chance, attended, inverse, branch, middle, second, attended_low, picks, query_codes, key_code, bands, near, score, low_strip, high_strip, send, receive, local):
    parts, slots = own_tokens.shape[0], own_tokens.shape[1]
    row, me, peers = group_peers(parts)
    greet([(row, peer) for peer in peers])

    def exchange(which, source, target):
        mine = block_of(me, slots)
        copies = [
            remote(source.at[peer], target.at[mine], send.at[which, step], receive.at[which, step], (row, peer))
            for step, peer in enumerate(peers)
        ]
        return copies + [pltpu.make_async_copy(source.at[me], target.at[mine], local.at[which])]

    token_copies = exchange(0, own_tokens, tokens)
    upstream_copies = exchange(1, own_upstream, upstream)
    for copy in token_copies:
        copy.start()
    info = row_scalars(heights, widths, order, me)
    prepare(info, reversed_table, near_table, picks, query_codes, key_code, bands, near)
    for copy in token_copies:
        copy.wait()
    for copy in upstream_copies:
        copy.start()
    project_in(tokens, first_gain, first_shift, input_weight, query_bias, value_bias, first, query, keys, values)
    attend(query, keys, values, picks, query_codes, key_code, bands, near, chance, attended, inverse, score, low_strip, high_strip)
    project_out(tokens, attended, output_weight, output_bias, attention_scale, second_gain, second_shift, branch, middle, second, attended_low)
    for copy in upstream_copies:
        copy.wait()


WIDTHS = (512, 512, 512, 384, 384)


class Reduction:
    def __init__(self, sources, results, owns, core_in, x_in, y_in, late, line_in, send, receive, local):
        self.sources, self.results, self.owns = sources, results, owns
        self.core_in, self.x_in, self.y_in, self.late, self.line_in = core_in, x_in, y_in, late, line_in
        self.send, self.receive, self.local = send, receive, local
        rows, seq = lax.axis_index("rows"), lax.axis_index("seq")
        self.z, self.x, self.y, self.core = rows // 2, rows % 2, seq // 2, seq % 2
        z, x, y, core = self.z, self.x, self.y, self.core
        self.core_peer = (rows, y * 2 + 1 - core)
        self.x_peer = (z * 2 + 1 - x, seq)
        self.y_peer = (rows, (1 - y) * 2 + core)
        self.diagonal = (z * 2 + 1 - x, (1 - y) * 2 + core)
        self.z_peers = [(lax.rem(z + step, 4) * 2 + x, seq) for step in range(1, 4)]

    def peers(self):
        return [self.core_peer, self.x_peer, self.y_peer, self.diagonal] + self.z_peers

    def copy(self, unit, number, source, target, peer):
        return remote(source, target, self.send.at[unit, number], self.receive.at[unit, number], peer)

    def core_copies(self, unit):
        return [
            self.copy(unit, part, self.sources[unit].at[part * 2 + 1 - self.core], self.core_in[unit].at[part], self.core_peer)
            for part in range(2)
        ]

    def own_copies(self, unit):
        if self.owns[unit] is None:
            return []
        return [
            pltpu.make_async_copy(self.sources[unit].at[part * 2 + self.core], self.owns[unit].at[part], self.local.at[unit, part])
            for part in range(2)
        ]

    def x_copy(self, unit):
        return self.copy(unit, 2, self.core_in[unit].at[:, :, 1 - self.x, 0:48], self.x_in[unit], self.x_peer)

    def y_copy(self, unit):
        return self.copy(unit, 3, self.core_in[unit].at[1 - self.y, :, :, 48:96], self.y_in[unit], self.y_peer)

    def again_y(self, unit):
        return self.copy(unit, 4, self.x_in[unit].at[1 - self.y], self.late[unit].at[:, 0:48], self.y_peer)

    def again_x(self, unit):
        return self.copy(unit, 5, self.y_in[unit].at[:, 1 - self.x], self.late[unit].at[:, 48:96], self.x_peer)

    def line_copies(self, unit):
        return [
            self.copy(unit, 6 + step, self.late[unit].at[lax.rem(self.z + step + 1, 4)], self.line_in[unit].at[step], peer)
            for step, peer in enumerate(self.z_peers)
        ]

    def begin(self, unit):
        for copy in self.core_copies(unit):
            copy.start()

    def fetch(self, unit):
        for copy in self.own_copies(unit):
            copy.start()

    def first(self, unit):
        for copy in self.core_copies(unit) + self.own_copies(unit):
            copy.wait()
        held, own = self.core_in[unit], self.owns[unit]

        def add(line, carry):
            for part in range(2):
                for side in range(2):
                    if own is None:
                        term = self.sources[unit][part * 2 + self.core, line, side]
                    else:
                        term = own[part, line, side]
                    held[part, line, side] = held[part, line, side] + term
            return carry

        lax.fori_loop(0, 4, add, 0)
        self.x_copy(unit).start()
        self.y_copy(unit).start()

    def second(self, unit):
        x_in, y_in, held = self.x_in[unit], self.y_in[unit], self.core_in[unit]
        self.x_copy(unit).wait()

        def add_x(line, carry):
            for part in range(2):
                x_in[part, line] = x_in[part, line] + held[part, line, self.x, 0:48]
            return carry

        lax.fori_loop(0, 4, add_x, 0)
        self.again_y(unit).start()
        self.y_copy(unit).wait()

        def add_y(line, carry):
            for side in range(2):
                y_in[line, side] = y_in[line, side] + held[self.y, line, side, 48:96]
            return carry

        lax.fori_loop(0, 4, add_y, 0)
        self.again_x(unit).start()

    def third(self, unit):
        late, x_in, y_in = self.late[unit], self.x_in[unit], self.y_in[unit]
        self.again_y(unit).wait()
        self.again_x(unit).wait()

        def add(line, carry):
            late[line, 0:48] = late[line, 0:48] + x_in[self.y, line]
            late[line, 48:96] = late[line, 48:96] + y_in[line, self.x]
            return carry

        lax.fori_loop(0, 4, add, 0)
        for copy in self.line_copies(unit):
            copy.start()

    def fourth(self, unit):
        for copy in self.line_copies(unit):
            copy.wait()
        total = self.late[unit][self.z].astype(F32)
        for step in range(3):
            total = total + self.line_in[unit][step].astype(F32)
        self.results[unit](total)


class SmallSum:
    def __init__(self, link, small, out, core_in, plane_in, line_in, part, send, receive):
        self.link, self.small, self.out = link, small, out
        self.core_in, self.plane_in, self.line_in, self.part = core_in, plane_in, line_in, part
        self.send, self.receive = send, receive
        plane = link.x * 2 + link.y
        self.plane = plane
        self.plane_peers = (
            (link.x_peer, lax.rem(plane + 2, 4)),
            (link.y_peer, plane + 1 - 2 * link.y),
            (link.diagonal, 3 - plane),
        )

    def copy(self, number, source, target, peer):
        return remote(source, target, self.send.at[number], self.receive.at[number], peer)

    def core_copy(self):
        return self.copy(0, self.small.at[1 - self.link.core], self.core_in, self.link.core_peer)

    def plane_copies(self):
        return [
            self.copy(1 + step, self.core_in.at[index], self.plane_in.at[step], peer)
            for step, (peer, index) in enumerate(self.plane_peers)
        ]

    def line_copies(self):
        return [
            self.copy(4 + step, self.part.at[lax.rem(self.link.z + step + 1, 4)], self.line_in.at[step], peer)
            for step, peer in enumerate(self.link.z_peers)
        ]

    def line_back(self):
        mine = self.out.at[self.link.core, self.plane, self.link.z]
        return [self.copy(7 + step, mine, mine, peer) for step, peer in enumerate(self.link.z_peers)]

    def plane_back(self):
        mine = self.out.at[self.link.core, self.plane]
        return [self.copy(10 + step, mine, mine, peer) for step, (peer, _) in enumerate(self.plane_peers)]

    def core_back(self):
        mine = self.out.at[self.link.core]
        return self.copy(13, mine, mine, self.link.core_peer)

    def steps(self):
        def one():
            self.core_copy().start()

        def two():
            self.core_copy().wait()
            self.core_in[...] += self.small[self.link.core]
            for copy in self.plane_copies():
                copy.start()

        def three():
            for copy in self.plane_copies():
                copy.wait()
            self.part[...] = self.core_in[self.plane] + self.plane_in[0] + self.plane_in[1] + self.plane_in[2]
            for copy in self.line_copies():
                copy.start()

        def four():
            for copy in self.line_copies():
                copy.wait()
            self.out[self.link.core, self.plane, self.link.z] = (
                self.part[self.link.z] + self.line_in[0] + self.line_in[1] + self.line_in[2]
            )
            for copy in self.line_back():
                copy.start()

        def five():
            for copy in self.line_back():
                copy.wait()
            for copy in self.plane_back():
                copy.start()

        def six():
            for copy in self.plane_back():
                copy.wait()
            self.core_back().start()

        def seven():
            self.core_back().wait()

        return [one, two, three, four, five, six, seven]


def pack_small(table_sum, sums, feed_sums, up_sum, vectors, small):
    lane = lax.broadcasted_iota(jnp.int32, (16, 128), 1)
    for block in range(32):
        where = (block // 16, block // 4 % 4, block % 4)
        if block < 24:
            value = table_sum[2 * block]
            if 2 * block + 1 < SPAN:
                other = pltpu.roll(table_sum[2 * block + 1], 64, 1)
                value = jnp.where(lane < 64, value, other)
            small[where] = value
        elif block >= 30:
            small[where] = jnp.zeros((16, 128), F32)
    vectors[...] = jnp.zeros_like(vectors)
    for number in range(8):
        vectors[number : number + 1, :] = jnp.sum(sums[number], 0, keepdims=True)
    for number in range(2):
        vectors[8 + number : 9 + number, :] = jnp.sum(feed_sums[number], 0, keepdims=True)
    for number in range(PARTS):
        vectors[10 + number : 11 + number, :] = up_sum[0:1, number * MODEL : (number + 1) * MODEL]
    for block in range(24, 30):
        where = (block // 16, block // 4 % 4, block % 4)
        small[where] = vectors[:, (block - 24) * 128 : (block - 23) * 128]


def backward_kernel(paired, heights, widths, order, own_upstream, middle, branch, second_change, attended_low, picks, query_codes, key_code, output_weight, attention_scale, second_gain, first_gain, feed_sums, up_sum, output, feed_units, tokens_far, first_far, query_far, keys_far, values_far, attended_far, inverse_far, chance_far, weight_far, *rest):
    if paired:
        outs, rest = rest[:6], rest[6:]
        own_output, own_gradient, up_result, down_result, late_result, small_out = outs
    else:
        outs, rest = rest[:4], rest[4:]
        own_output, own_gradient, late_unit, small = outs
    (tokens, first, query, keys, values, attended, inverse, input_weight, chance, middle_change, branch_change, change_low, joined, band_sums, near_sums, weight_change, score_change, table_sum, sums, vectors, load_sems, chance_sems, send, receive, local), rest = rest[:25], rest[25:]
    first_change, gradient = attended, change_low
    parts, slots = own_output.shape[0], own_output.shape[1]
    row, me, peers = group_peers(parts)
    if paired:
        (late_unit, small), rest = rest[:2], rest[2:]
        own_block, rest = rest[0], rest[1:]
        count = len(WIDTHS)
        stages = [rest[i * count : (i + 1) * count] for i in range(5)]
        rest = rest[5 * count :]
        unit_send, unit_receive, unit_local = rest[:3]
        sources = [feed_units.at[tile] for tile in range(TILES)]
        sources += [late_unit.at[:, :, :, :, half * 384 : half * 384 + 384] for half in range(2)]

        def feed_result(tile):
            def put(total):
                for half in range(2):
                    columns = slice(half * 384 + tile * 128, half * 384 + tile * 128 + 128)
                    up_result[:, columns] = total[:, half * 128 : half * 128 + 128]
                    lines = slice(half * 96, half * 96 + 96)
                    down_result[lines, tile * 128 : tile * 128 + 128] = total[:, 256 + half * 128 : 384 + half * 128]

            return put

        def late_put(half):
            def put(total):
                late_result[:, half * 384 : half * 384 + 384] = total

            return put

        results = [feed_result(tile) for tile in range(TILES)] + [late_put(half) for half in range(2)]
        owns = [own_block] * TILES + [None, None]
        link = Reduction(sources, results, owns, *stages, unit_send, unit_receive, unit_local)
        small_sum = SmallSum(link, small, small_out, *rest[3:])
        others = link.peers() + [(row, (1 - link.y) * 2 + 1 - link.core)]
        greet(others)
    else:
        greet([(row, peer) for peer in peers])

    def give_back(which, source, target):
        copies = [
            remote(source.at[block_of(peer, slots)], target.at[me], send.at[which, step], receive.at[which, step], (row, peer))
            for step, peer in enumerate(peers)
        ]
        return copies + [pltpu.make_async_copy(source.at[block_of(me, slots)], target.at[me], local.at[which])]

    output_copies = give_back(0, output, own_output)
    gradient_copies = give_back(1, gradient, own_gradient)

    loads = [
        pltpu.make_async_copy(source, target, load_sems.at[number])
        for number, (source, target) in enumerate(
            (
                (query_far, query),
                (keys_far, keys),
                (values_far, values),
                (attended_far, attended),
                (inverse_far, inverse),
                (first_far, first),
                (tokens_far, tokens),
                (weight_far, input_weight),
            )
        )
    ]

    def chance_copy(pair):
        slot = lax.rem(pair, 2)
        return pltpu.make_async_copy(chance_far.at[pl.ds(pair * 2, 2)], chance.at[slot], chance_sems.at[slot])

    if paired:
        for unit in range(TILES):
            link.begin(unit)
        link.fetch(0)
    for copy in loads:
        copy.start()
    chance_copy(0).start()
    info = row_scalars(heights, widths, order, me)
    sums[...] = jnp.zeros_like(sums)

    def norm(rows):
        normal, spread = normal_of(middle[rows, :])
        change = second_change[rows, :]
        sums[6] += fold(change * normal)
        sums[7] += fold(change)
        value = own_upstream[rows, :].astype(F32) + normal_back(change, normal, spread, second_gain[...])
        middle_change[rows, :] = value
        sums[5] += fold(value * branch[rows, :])
        low = (value * attention_scale[...]).astype(BF16)
        branch_change[rows, :] = low
        sums[4] += fold(low.astype(F32))

    chunks(norm)
    change_low[...] = dot_nt(branch_change[...], output_weight[...]).astype(BF16)
    if paired:
        link.first(0)
        link.fetch(1)
    for copy in output_copies:
        copy.start()
    for copy in loads[:5]:
        copy.wait()

    def event(pair):
        @pl.when(pair + 1 < PAIRS)
        def _():
            chance_copy(pair + 1).start()

        chance_copy(pair).wait()
        if not paired:
            return

        @pl.when(pair == 1)
        def _():
            link.first(1)
            link.fetch(2)

        @pl.when(pair == 2)
        def _():
            link.second(0)

        @pl.when(pair == 3)
        def _():
            link.first(2)

        @pl.when(pair == 4)
        def _():
            link.second(1)
            link.third(0)

    attend_back(query, keys, values, picks, query_codes, key_code, lambda pair: chance.at[lax.rem(pair, 2)], change_low, attended, inverse, joined, band_sums, near_sums, weight_change, score_change, event)
    for copy in loads[5:]:
        copy.wait()

    def late_parts(half):
        for part in range(PARTS):
            base = part * 576 + half * 384
            if half == 0:
                value = dot_tn(first[...], joined[:, base : base + 384])
            else:
                value = jnp.concatenate(
                    [
                        dot_tn(first[...], joined[:, base : base + 192]),
                        dot_tn(attended_low[...], branch_change[:, part * 192 : part * 192 + 192]),
                    ],
                    1,
                )
            late_unit[part, :, :, :, half * 384 : half * 384 + 384] = value.astype(BF16).reshape(4, 2, 96, 384)

    late_parts(0)
    if paired:
        link.begin(3)
    late_parts(1)
    if paired:
        link.begin(4)
        link.second(2)
        link.first(3)
        link.third(1)
    first_change[...] = dot_nt(joined[...], input_weight[...])

    def norm_first(rows):
        normal, spread = normal_of(tokens[rows, :].astype(F32))
        change = first_change[rows, :]
        sums[0] += fold(change * normal)
        sums[1] += fold(change)
        sums[2] += fold(joined[rows, 0:MODEL].astype(F32))
        sums[3] += fold(joined[rows, 2 * MODEL : 3 * MODEL].astype(F32))
        value = middle_change[rows, :] + normal_back(change, normal, spread, first_gain[...])
        gradient[rows, :] = value.astype(BF16)

    chunks(norm_first)
    for copy in gradient_copies:
        copy.start()
    if paired:
        link.first(4)
        link.fourth(0)
    table_back(info, band_sums, near_sums, table_sum)
    pack_small(table_sum, sums, feed_sums, up_sum, vectors, small)
    if paired:
        step = small_sum.steps()
        step[0]()
        link.second(3)
        link.third(2)
        step[1]()
        link.second(4)
        step[2]()
        link.third(3)
        link.fourth(1)
        step[3]()
        link.third(4)
        step[4]()
        link.fourth(2)
        link.fourth(3)
        step[5]()
        link.fourth(4)
        step[6]()
    for copy in output_copies + gradient_copies:
        copy.wait()


def whole():
    return pl.BlockSpec(memory_space=pltpu.VMEM)


def far():
    return pl.BlockSpec(memory_space=pl.ANY)


def scalars():
    return pl.BlockSpec(memory_space=pltpu.SMEM)


def shape(*dims, dtype=F32):
    return jax.ShapeDtypeStruct(dims, dtype)


def on_device(layer_input, first_gain, first_shift, input_weight, query_bias, value_bias, bias_table, output_weight, output_bias, attention_scale, second_gain, second_shift, up_weight, up_bias, down_weight, down_bias, feed_scale, upstream, grid_heights, grid_widths, packing_order):
    parts = lax.axis_size("seq")
    paired = (lax.axis_size("rows"), parts) == (8, 4)
    slots = layer_input.shape[1]
    hidden_units = up_weight.shape[1]

    def line(item):
        return item.reshape(1, -1)

    table = bias_table.reshape(SPAN, SPAN, HEADS)
    reversed_table = jnp.pad(
        jnp.transpose(table[:, ::-1, :], (0, 2, 1)).astype(F32),
        ((0, 0), (0, 16 - HEADS), (0, 128 - SPAN)),
    )
    near_table = table[GRID - 3 : GRID + 2, GRID - 3 : GRID + 2].reshape(25, HEADS).astype(F32)
    full = (SLOTS, MODEL)
    dma = pltpu.SemaphoreType.DMA
    exchange_sems = [dma((2, parts - 1)), dma((2, parts - 1)), dma((2,))]
    tokens, own_upstream, first, query, keys, values, chance, attended, inverse, branch, middle, second, attended_low, picks, query_codes, key_code = pl.pallas_call(
        forward_kernel,
        out_shape=[shape(*full, dtype=BF16)] * 6
        + [shape(HEADS, SLOTS, PADDED, dtype=BF16)]
        + [shape(*full)] * 4
        + [shape(*full, dtype=BF16)] * 2
        + [shape(SLOTS, 128, dtype=BF16), shape(2, SLOTS, 128), shape(8, PADDED)],
        in_specs=[scalars()] * 4 + [whole()] * 13,
        out_specs=[whole()] * 16,
        scratch_shapes=[
            pltpu.VMEM((HEADS, 2, 8, WIDE), F32),
            pltpu.VMEM((HEADS, 128, 128), BF16),
            pltpu.VMEM((SLOTS, SLOTS), F32),
            pltpu.VMEM((STRIP, WIDE), F32),
            pltpu.VMEM((STRIP, WIDE), F32),
        ]
        + exchange_sems,
        compiler_params=pltpu.CompilerParams(collective_id=0, has_side_effects=True, vmem_limit_bytes=VMEM_LIMIT),
        name="forward",
    )(
        grid_heights, grid_widths, packing_order, near_table, reversed_table, layer_input, upstream,
        line(first_gain), line(first_shift), input_weight, line(query_bias), line(value_bias),
        output_weight, line(output_bias), line(attention_scale), line(second_gain), line(second_shift),
    )

    output, second_change, feed_units, up_sum, feed_sums = pl.pallas_call(
        feed_kernel,
        out_shape=[
            shape(*full, dtype=BF16),
            shape(*full),
            shape(TILES, PARTS, BLOCKS, 96, 512, dtype=BF16),
            shape(8, hidden_units),
            shape(2, 8, MODEL),
        ],
        in_specs=[whole()] * 3 + [far(), whole(), far(), whole(), whole()],
        out_specs=[whole()] * 5,
        scratch_shapes=[
            pltpu.VMEM(full, BF16),
            pltpu.VMEM(full, F32),
            pltpu.VMEM((SLOTS, 1024), BF16),
            pltpu.VMEM((SLOTS, 1024), BF16),
            pltpu.VMEM((SLOTS, 1024), F32),
            pltpu.VMEM((SLOTS, 1024), F32),
            pltpu.VMEM((2, MODEL, 1024), BF16),
            pltpu.VMEM((2, 1024, MODEL), BF16),
            dma((2, 2, BLOCKS)),
        ],
        compiler_params=pltpu.CompilerParams(vmem_limit_bytes=VMEM_LIMIT),
        name="feed",
    )(second, middle, own_upstream, up_weight, line(up_bias), down_weight, line(down_bias), line(feed_scale))

    outs = [(shape(parts, slots, MODEL, dtype=BF16), far())] * 2
    scratch = [
        pltpu.VMEM(full, BF16),
        pltpu.VMEM(full, BF16),
        pltpu.VMEM(full, BF16),
        pltpu.VMEM(full, BF16),
        pltpu.VMEM(full, BF16),
        pltpu.VMEM(full, F32),
        pltpu.VMEM(full, F32),
        pltpu.VMEM((MODEL, 3 * MODEL), BF16),
        pltpu.VMEM((2, 2, SLOTS, PADDED), BF16),
        pltpu.VMEM(full, F32),
        pltpu.VMEM(full, BF16),
        pltpu.VMEM(full, BF16),
        pltpu.VMEM((SLOTS, 3 * MODEL), BF16),
        pltpu.VMEM((HEADS, 2, 8, WIDE), F32),
        pltpu.VMEM((HEADS, 128, 128), F32),
        pltpu.VMEM((SLOTS, PADDED), F32),
        pltpu.VMEM((SLOTS, PADDED), BF16),
        pltpu.VMEM((SPAN, 16, 128), F32),
        pltpu.VMEM((8, 8, MODEL), F32),
        pltpu.VMEM((16, MODEL), F32),
        dma((8,)),
        dma((2,)),
    ] + exchange_sems
    late_shape, small_shape = (4, 4, 2, 96, 768), (2, 4, 4, 16, 128)
    if paired:
        outs += [
            (shape(96, 768), whole()),
            (shape(192, 384), whole()),
            (shape(96, 768), whole()),
            (shape(*small_shape), whole()),
        ]
        scratch += [pltpu.VMEM(late_shape, BF16), pltpu.VMEM(small_shape, F32)]
        scratch += [pltpu.VMEM((2, 4, 2, 96, 512), BF16)]
        for dims in (
            lambda c: (2, 4, 2, 96, c),
            lambda c: (2, 4, 48, c),
            lambda c: (4, 2, 48, c),
            lambda c: (4, 96, c),
            lambda c: (3, 96, c),
        ):
            scratch += [pltpu.VMEM(dims(width), BF16) for width in WIDTHS]
        count = len(WIDTHS)
        scratch += [dma((count, 9)), dma((count, 9)), dma((count, 2))]
        scratch += [
            pltpu.VMEM((4, 4, 16, 128), F32),
            pltpu.VMEM((3, 4, 16, 128), F32),
            pltpu.VMEM((3, 16, 128), F32),
            pltpu.VMEM((4, 16, 128), F32),
            dma((14,)),
            dma((14,)),
        ]
    else:
        outs += [(shape(*late_shape, dtype=BF16), whole()), (shape(*small_shape), whole())]
    results = pl.pallas_call(
        functools.partial(backward_kernel, paired),
        out_shape=[item[0] for item in outs],
        in_specs=[scalars()] * 3 + [whole()] * 14 + [far()] * 11,
        out_specs=[item[1] for item in outs],
        scratch_shapes=scratch,
        compiler_params=pltpu.CompilerParams(collective_id=1, has_side_effects=True, vmem_limit_bytes=VMEM_LIMIT),
        name="backward",
    )(
        grid_heights, grid_widths, packing_order, own_upstream, middle, branch, second_change,
        attended_low, picks, query_codes, key_code, output_weight, line(attention_scale), line(second_gain),
        line(first_gain), feed_sums, up_sum, output, feed_units.reshape(TILES, PARTS, 4, 2, 96, 512),
        tokens, first, query, keys, values, attended, inverse, chance, input_weight,
    )
    own_output, own_gradient = results[:2]
    if paired:
        up_result, down_result, late_result, small = results[2:]
    else:
        late_unit, small = results[2:]
        late_result = reduce_any_mesh(late_unit.reshape(PARTS, MODEL, MODEL))
        up_unit, down_unit = restore_feed(feed_units)
        up_result, down_result = reduce_any_mesh(up_unit), reduce_any_mesh(down_unit)
        small = lax.psum(small, ("rows", "seq"))
    return finish(parts, own_output, own_gradient, up_result, down_result, late_result, small)


def finish(parts, own_output, own_gradient, up_result, down_result, late_result, small):
    blocks = small.reshape(32, 16, 128)
    vectors = jnp.transpose(blocks[24:30], (1, 0, 2)).reshape(16, MODEL)
    table = jnp.transpose(blocks[:24].reshape(24, 16, 2, 64), (0, 2, 1, 3)).reshape(48, 16, 64)
    table = jnp.transpose(table[:SPAN, :HEADS, SPAN - 1 :: -1], (0, 2, 1)).reshape(-1, HEADS)
    return (
        own_output,
        own_gradient.astype(F32),
        vectors[0],
        vectors[1],
        late_result[:, :576],
        vectors[2],
        vectors[3],
        table,
        late_result[:, 576:],
        vectors[4],
        vectors[5],
        vectors[6],
        vectors[7],
        up_result,
        vectors[10:14].reshape(-1),
        down_result if down_result.shape[1] == 192 else down_result.T,
        vectors[9],
        vectors[8],
    )


def restore_feed(units):
    up = units[..., :256].reshape(TILES, PARTS, BLOCKS, 96, 2, 128)
    up = jnp.transpose(up, (1, 2, 3, 4, 0, 5)).reshape(PARTS, MODEL, MODEL)
    down = units[..., 256:].reshape(TILES, PARTS, BLOCKS, 96, 2, 128)
    down = jnp.transpose(down, (1, 2, 0, 5, 4, 3)).reshape(PARTS, BLOCKS * TILES * 128, 192)
    return up, down


def reduce_any_mesh(item):
    part = lax.psum_scatter(item, "seq", scatter_dimension=0, tiled=True)
    part = lax.psum_scatter(part.reshape(part.shape[1:]), "rows", scatter_dimension=0, tiled=True)
    return part.astype(F32)


def solution(mesh):
    split = P("rows", "seq", None)
    lines = P("rows", None)
    block = P("rows", "seq")
    in_specs = (split,) + (P(),) * 16 + (split, lines, lines, lines)
    out_specs = (split, split, P(), P(), block, P(), P(), P(), block, P(), P(), P(), P(), block, P(), block, P(), P())
    return jax.shard_map(on_device, mesh=mesh, in_specs=in_specs, out_specs=out_specs, check_vma=False)
```

```python
import functools
import math

import jax
import jax.numpy as jnp
from jax import lax
from jax.experimental import pallas as pl
from jax.experimental.pallas import tpu as pltpu
from jax.sharding import PartitionSpec as P

HEADS = 12
HEAD = 64
GRID = 24
SPAN = 2 * GRID - 1
SLOTS = 576
PADDED = 640
MODEL = 768
PAIRS = HEADS // 2
WIDE = 1152
STRIP = 128
BASE = 489
COMPACT = 32
LINES = 2304 // 128
IMGS = 4
EPS = 1e-06
NEGATIVE = -1e30
CHUNK = 32
PARTS = 4
BLOCKS = 8
TILES = 3
F32 = jnp.float32
BF16 = jnp.bfloat16
VMEM_LIMIT = 63 * 2**20
FIRST_GAIN, FIRST_SHIFT, QUERY_BIAS, VALUE_BIAS, OUTPUT_BIAS, ATTENTION_SCALE = range(6)
SECOND_GAIN, SECOND_SHIFT, DOWN_BIAS, FEED_SCALE, UP_BIAS = range(6, 11)


def dot(left, right):
    return lax.dot_general(left, right, (((1,), (0,)), ((), ())), preferred_element_type=F32)


def dot_nt(left, right):
    return lax.dot_general(left, right, (((1,), (1,)), ((), ())), preferred_element_type=F32)


def dot_tn(left, right):
    return lax.dot_general(left, right, (((0,), (0,)), ((), ())), preferred_element_type=F32)


def chunks(body):
    def step(index, carry):
        body(pl.ds(pl.multiple_of(index * CHUNK, CHUNK), CHUNK))
        return carry

    lax.fori_loop(0, SLOTS // CHUNK, step, 0)


def fold(value):
    return jnp.sum(value.reshape(value.shape[0] // 8, 8, value.shape[1]), 0)


def normal_of(values):
    center = values - jnp.mean(values, -1, keepdims=True)
    spread = lax.rsqrt(jnp.mean(center * center, -1, keepdims=True) + EPS)
    return center * spread, spread


def normal_back(change, normal, spread, gain):
    scaled = change * gain
    inner = (
        scaled
        - jnp.mean(scaled, -1, keepdims=True)
        - normal * jnp.mean(scaled * normal, -1, keepdims=True)
    )
    return inner * spread


def row_scalars(heights, widths, order, row):
    sizes, breadths, large = [], [], []
    for place in range(IMGS):
        picked = order[row, place]
        size, breadth = jnp.int32(0), jnp.int32(0)
        for image in range(IMGS):
            hit = picked == image
            size = size + jnp.where(hit, heights[row, image] * widths[row, image], 0)
            breadth = breadth + jnp.where(hit, widths[row, image], 0)
        sizes.append(size)
        breadths.append(breadth)
        large.append(jnp.where(picked == 0, 1, 0))
    begins = [jnp.int32(0)]
    for place in range(IMGS - 1):
        begins.append(begins[-1] + sizes[place])
    large_begin = sum(begins[p] * large[p] for p in range(IMGS))
    return dict(
        sizes=sizes,
        breadths=breadths,
        large=large,
        begins=begins,
        large_begin=large_begin,
        large_size=heights[row, 0] * widths[row, 0],
        large_width=widths[row, 0],
    )


def place_info(info, slot):
    segment = jnp.full(slot.shape, IMGS, jnp.int32)
    across = jnp.zeros(slot.shape, jnp.int32)
    down = jnp.zeros(slot.shape, jnp.int32)
    large = jnp.zeros(slot.shape, jnp.int32)
    for place in range(IMGS):
        offset = slot - info["begins"][place]
        inside = (offset >= 0) & (offset < info["sizes"][place])
        breadth = jnp.full(slot.shape, info["breadths"][place], jnp.int32)
        line = ((offset.astype(F32) + 0.5) / breadth.astype(F32)).astype(jnp.int32)
        segment = jnp.where(inside, place, segment)
        down = jnp.where(inside, line, down)
        across = jnp.where(inside, offset - line * breadth, across)
        large = jnp.where(inside, info["large"][place], large)
    return segment, down, across, large


def compact_index(info):
    found = []
    for axis in (0, 1):
        number = lax.broadcasted_iota(jnp.int32, (COMPACT, 128), axis)
        slot = number + jnp.where(number >= info["large_begin"], info["large_size"], 0)
        segment, down, across, large = place_info(info, slot)
        small = (segment < IMGS) & (large == 0) & (number < COMPACT)
        found.append((jnp.where(small, segment, -1 - axis), down, across))
    same = found[0][0] == found[1][0]
    row_step = found[0][1] - found[1][1] + 2
    column_step = found[0][2] - found[1][2] + 2
    return jnp.where(same, row_step * 5 + column_step, -1)


def shift_of(info, line):
    shift = BASE - (line - (GRID - 1)) * info["large_width"]
    return jnp.where(shift < 0, shift + WIDE, shift)


def flip():
    down = lax.broadcasted_iota(jnp.int32, (128, 128), 0)
    across = lax.broadcasted_iota(jnp.int32, (128, 128), 1)
    return jnp.where(down + across == 127, 1.0, 0.0).astype(BF16)


def line_place(line):
    start = LINES * 128 - SPAN - SPAN * line
    return start // 128, lax.rem(start, 128)


def prepare(info, table, flat, turned, columns, picks, query_codes, key_code, bands, near):
    flat[...] = jnp.zeros_like(flat)
    flat[0:HEADS, 0 : SPAN * SPAN] = table[...].astype(F32)
    turned[LINES] = jnp.zeros((16, 128), F32)
    for block in range(LINES):
        turned[LINES - 1 - block] = dot(flat[:, block * 128 : block * 128 + 128].astype(BF16), flip())
    for entry in range(25):
        at = (GRID - 3 + entry // 5) * SPAN + GRID - 3 + entry % 5
        columns[entry] = jnp.broadcast_to(flat[:, at : at + 1], (16, 128))

    def rows(index, carry):
        start = pl.multiple_of(index * 64, 64)
        slot = lax.broadcasted_iota(jnp.int32, (64, 128), 0) + start
        lane = lax.broadcasted_iota(jnp.int32, (64, 128), 1)
        segment, _, across, large = place_info(info, slot)
        rank = slot - jnp.where(slot >= info["large_begin"], info["large_size"], 0)
        small = (segment < IMGS) & (large == 0)
        target = jnp.where(small, rank, -1)
        pick = (lane == target) | (lane == segment + COMPACT)
        picks[pl.ds(start, 64), :] = jnp.where(pick, 1.0, 0.0).astype(BF16)
        code = across.astype(F32)
        query_codes[0, pl.ds(start, 64), :] = jnp.where(large == 1, code, -1e9)
        query_codes[1, pl.ds(start, 64), :] = jnp.where(large == 1, code, 1e9)
        return carry

    lax.fori_loop(0, SLOTS // 64, rows, 0)
    slot = lax.broadcasted_iota(jnp.int32, (8, PADDED), 1)
    key_code[...] = place_info(info, slot)[2].astype(F32)

    lanes = lax.broadcasted_iota(jnp.int32, (16, WIDE), 1)
    width = info["large_width"]

    def line_step(line, carry):
        low, high = carry
        shift = shift_of(info, line)
        block, lane = line_place(line)
        wide = jnp.concatenate([turned[block], turned[block + 1], jnp.zeros((16, WIDE - 256), F32)], 1)
        move = shift - lane
        rolled = pltpu.roll(wide, jnp.where(move < 0, move + WIDE, move), 1)
        entry = lanes - shift
        entry = jnp.where(entry < 0, entry + WIDE, entry)
        low = jnp.where((entry >= GRID - width) & (entry <= GRID - 1), rolled, low)
        high = jnp.where((entry >= GRID) & (entry <= GRID - 2 + width), rolled, high)
        return low, high

    zero = jnp.zeros((16, WIDE), F32)
    low, high = lax.fori_loop(0, SPAN, line_step, (zero, zero))
    for head in range(HEADS):
        bands[head, 0] = jnp.broadcast_to(low[head : head + 1], (8, WIDE))
        bands[head, 1] = jnp.broadcast_to(high[head : head + 1], (8, WIDE))

    index = compact_index(info)
    across = lax.broadcasted_iota(jnp.int32, (128 - COMPACT, 128), 1) - COMPACT
    down = lax.broadcasted_iota(jnp.int32, (128 - COMPACT, 128), 0)
    inside = (across >= 0) & (across <= IMGS) & (down <= IMGS)
    for head in range(HEADS):
        value = jnp.zeros((COMPACT, 128), F32)
        for entry in range(25):
            value = jnp.where(index == entry, columns[entry, head : head + 1, :], value)
        near[head, 0:COMPACT, :] = value.astype(BF16)
        own = jnp.where(down == IMGS, columns[12, head : head + 1, :], 0.0)
        lower = jnp.where(inside, jnp.where(across == down, own, NEGATIVE), 0.0)
        near[head, COMPACT:128, :] = lower.astype(BF16)


def project_in(tokens, vec, weight, first, query, keys, values):
    gain, shift = vec[FIRST_GAIN : FIRST_GAIN + 1, :], vec[FIRST_SHIFT : FIRST_SHIFT + 1, :]

    def norm(rows):
        normal, _ = normal_of(tokens[rows, :].astype(F32))
        first[rows, :] = (normal * gain + shift).astype(BF16)

    chunks(norm)
    step = 256
    for part, out in enumerate((query, keys, values)):
        for block in range(MODEL // step):
            lanes = slice(block * step, (block + 1) * step)
            columns = slice(part * MODEL + block * step, part * MODEL + (block + 1) * step)
            mixed = dot(first[...], weight[:, columns])
            if part == 0:
                mixed = (mixed + vec[QUERY_BIAS : QUERY_BIAS + 1, lanes]) * HEAD**-0.5
            if part == 2:
                mixed = mixed + vec[VALUE_BIAS : VALUE_BIAS + 1, lanes]
            out[:, lanes] = mixed.astype(BF16)


def half_mask(half):
    lane = lax.broadcasted_iota(jnp.int32, (SLOTS, 128), 1)
    return (lane < HEAD) if half == 0 else (lane >= HEAD)


def keep(mask, value):
    return jnp.where(mask, value, jnp.zeros_like(value))


def attend(query, keys, values, picks, query_codes, key_code, bands, near, chance_of, attended, inverse, scores, strips, done):
    def pair_step(pair, carry):
        chance = chance_of(pair)
        lanes = pl.ds(pl.multiple_of(pair * 128, 128), 128)
        key_side = jnp.concatenate([keys[:, lanes], picks[...]], 1)
        result = jnp.zeros((SLOTS, 256), F32)
        for half in range(2):
            head = pair * 2 + half
            mask = half_mask(half)
            near_side = dot(picks[...], near[head]).astype(BF16)
            query_side = jnp.concatenate([keep(mask, query[:, lanes]), near_side], 1)
            score = scores[half]
            low_strip, high_strip = strips[half]
            score[...] = dot_nt(query_side, key_side)
            for which, strip in enumerate((low_strip, high_strip)):
                band = jnp.concatenate([bands[head, which]] * (STRIP // 8), 0)
                strip[...] = pltpu.roll(band, 0, 1, stride=1, stride_axis=0)
            for block in range(SLOTS // 64):
                rows = slice(block * 64, (block + 1) * 64)
                strip_rows = slice(block % 2 * 64, block % 2 * 64 + 64)
                start = 512 - block // 2 * 128
                strip_lanes = slice(start, start + SLOTS)
                code = key_code[0:1, 0:SLOTS]
                low_hit = query_codes[0, rows, 0:1] >= code
                high_hit = code > query_codes[1, rows, 0:1]
                bias = jnp.where(
                    low_hit,
                    low_strip[strip_rows, strip_lanes],
                    jnp.where(high_hit, high_strip[strip_rows, strip_lanes], 0.0),
                )
                part = score[rows, :] + bias
                top = jnp.max(part, -1, keepdims=True)
                chance[half, rows, 0:SLOTS] = jnp.exp(part - top).astype(BF16)
            chance[half, :, SLOTS:] = jnp.zeros((SLOTS, PADDED - SLOTS), BF16)
            value_side = jnp.concatenate(
                [keep(mask, values[:, lanes]), keep(mask, jnp.ones((SLOTS, 128), BF16))], 1
            )
            result = result + dot(chance[half, :, 0:SLOTS], value_side)
        scale = 1.0 / result[:, 128:]
        inverse[:, lanes] = scale
        attended[:, lanes] = result[:, :128] * scale
        done(pair)
        return carry

    lax.fori_loop(0, PAIRS, pair_step, 0)


def project_out(tokens, attended, weight, vec, branch, middle, second, attended_low):
    attended_low[...] = attended[...].astype(BF16)
    step = 256
    for block in range(MODEL // step):
        lanes = slice(block * step, (block + 1) * step)
        branch[:, lanes] = dot(attended_low[...], weight[:, lanes]) + vec[OUTPUT_BIAS : OUTPUT_BIAS + 1, lanes]
    scale = vec[ATTENTION_SCALE : ATTENTION_SCALE + 1, :]
    gain, shift = vec[SECOND_GAIN : SECOND_GAIN + 1, :], vec[SECOND_SHIFT : SECOND_SHIFT + 1, :]

    def norm(rows):
        value = tokens[rows, :].astype(F32) + scale * branch[rows, :]
        middle[rows, :] = value
        normal, _ = normal_of(value)
        second[rows, :] = (normal * gain + shift).astype(BF16)

    chunks(norm)


def gelu_parts(value):
    bell = jnp.exp2(value * value * (-0.5 * math.log2(math.e)))
    base = 1.0 + (0.3275911 / math.sqrt(2.0)) * jnp.abs(value)
    guess = pl.reciprocal(base, approx=True)
    inner = guess * (2.0 - base * guess)
    poly = 0.5 * 1.061405429
    for coefficient in (-1.453152027, 1.421413741, -0.284496736, 0.254829592):
        poly = poly * inner + 0.5 * coefficient
    tail = poly * inner * bell
    share = jnp.where(value >= 0.0, 1.0 - tail, tail)
    return value * share, share + value * bell * (1.0 / math.sqrt(2.0 * math.pi))


def feed(second, upstream, up, down, vec, second_change, unit, up_sum, feed_sums, outcome_change, outcome, active, slope, up_tile, down_tile, sems, before, after):
    def loads(tile):
        slot = tile % 2
        copies = []
        for block in range(BLOCKS):
            start = 3 * 128 * block + 128 * tile
            inside = slice(block * 128, block * 128 + 128)
            copies.append(
                pltpu.make_async_copy(
                    up.at[:, start : start + 128], up_tile.at[slot, :, inside], sems.at[slot, 0, block]
                )
            )
            copies.append(
                pltpu.make_async_copy(
                    down.at[start : start + 128], down_tile.at[slot, inside], sems.at[slot, 1, block]
                )
            )
        return copies

    for copy in loads(0):
        copy.start()
    feed_sums[...] = jnp.zeros_like(feed_sums)
    scale = vec[FEED_SCALE : FEED_SCALE + 1, :]

    def begin(rows):
        value = (upstream[rows, :].astype(F32) * scale).astype(BF16)
        outcome_change[rows, :] = value
        feed_sums[1] += fold(value.astype(F32))

    chunks(begin)
    for tile in range(TILES):
        slot = tile % 2
        if tile + 1 < TILES:
            for copy in loads(tile + 1):
                copy.start()
        for copy in loads(tile):
            copy.wait()
        for pair in range(BLOCKS // 2):
            wide = slice(pair * 256, pair * 256 + 256)
            line = slice(UP_BIAS + pair, UP_BIAS + pair + 1)
            ends = [slice(start + 128 * tile, start + 128 * tile + 128) for start in (0, 384)]
            bias = jnp.concatenate([vec[line, end] for end in ends], 1)
            for start in range(0, SLOTS, 192):
                rows = slice(start, start + 192)
                value, gradient = gelu_parts(dot(second[rows, :], up_tile[slot, :, wide]) + bias)
                active[rows, wide] = value.astype(BF16)
                back = dot_nt(outcome_change[rows, :], down_tile[slot, wide, :])
                slope[rows, wide] = (back * gradient).astype(BF16)
            before(tile, pair)
        for start in range(0, MODEL, 256):
            lanes = slice(start, start + 256)
            result = dot(active[...], down_tile[slot, :, lanes])
            back = dot_nt(slope[...], up_tile[slot, lanes, :])
            if tile == 0:
                outcome[:, lanes] = result
                second_change[:, lanes] = back
            else:
                outcome[:, lanes] += result
                second_change[:, lanes] += back
        total = dot(jnp.ones((8, SLOTS), BF16), slope[...])
        for block in range(BLOCKS):
            inside = slice(block * 128, block * 128 + 128)
            start = 3 * 128 * block + 128 * tile
            up_sum[:, start : start + 128] = total[:, inside]
        for pair in range(BLOCKS // 2):
            turned = dot_tn(second[...], slope[:, pair * 256 : pair * 256 + 256]).astype(BF16)
            unit[pair, :, :, 0:96, 0:256] = turned.reshape(4, 2, 96, 256)
        for pair in range(BLOCKS // 2):
            turned = dot_tn(outcome_change[...], active[:, pair * 256 : pair * 256 + 256]).astype(BF16)
            for side in range(2):
                inside = slice(side * 128, side * 128 + 128)
                for part in range(PARTS):
                    start = part * 192
                    unit[part, pair, side, 0:96, 256:384] = turned[start : start + 96, inside]
                    for third in range(3):
                        start = part * 192 + 96 + third * 32
                        unit[part, pair, side, 96:128, third * 128 : third * 128 + 128] = turned[start : start + 32, inside]
        after(tile)


def feed_end(upstream, middle, vec, output, outcome, feed_sums):
    scale, bias = vec[FEED_SCALE : FEED_SCALE + 1, :], vec[DOWN_BIAS : DOWN_BIAS + 1, :]

    def end(rows):
        value = outcome[rows, :] + bias
        output[rows, :] = (middle[rows, 0:MODEL] + scale * value).astype(BF16)
        feed_sums[0] += fold(upstream[rows, :].astype(F32) * value)

    chunks(end)


def pair_at(turn):
    late = turn // 4
    return (1 - late) * ((3 * turn + 1) // 2) + late * (3 * turn - 11)


def attend_back(query, keys, values, picks, query_codes, key_code, chance_of, change_low, attended, inverse, joined, band_sums, near_sums, weight_changes, score_changes, event, middle_event):
    def pair_step(turn, carry):
        pair = pair_at(turn)
        event(turn)
        chance = chance_of(turn)
        lanes = pl.ds(pl.multiple_of(pair * 128, 128), 128)
        lane = lax.broadcasted_iota(jnp.int32, (SLOTS, 128), 1)
        own_change = change_low[:, lanes].astype(F32)
        scale = inverse[:, lanes]
        terms = own_change * attended[:, lanes]
        high = terms.astype(BF16)
        low = (terms - high.astype(F32)).astype(BF16)
        block_row = lax.broadcasted_iota(jnp.int32, (128, 128), 0) // HEAD
        block_lane = lax.broadcasted_iota(jnp.int32, (128, 128), 1) // HEAD
        block = jnp.where(block_row == block_lane, 1.0, 0.0).astype(BF16)
        delta = (dot(high, block) + dot(low, block)) * -scale
        delta_high = delta.astype(BF16)
        delta_low = (delta - delta_high.astype(F32)).astype(BF16)
        scaled = (own_change * scale).astype(BF16)
        value_side = jnp.concatenate([values[:, lanes], jnp.ones((SLOTS, 128), BF16)], 1)
        query_total = jnp.zeros((SLOTS, 128), F32)
        key_total = jnp.zeros((SLOTS, 128), F32)
        value_total = jnp.zeros((SLOTS, 128), F32)
        for half in range(2):
            if half == 1:
                middle_event(turn)
            head = pair * 2 + half
            mask = half_mask(half)
            extra = jnp.where(
                lane == half * HEAD,
                delta_high,
                jnp.where(lane == half * HEAD + 1, delta_low, jnp.zeros_like(delta_low)),
            )
            own_scaled = keep(mask, scaled)
            weight_change, score_change = weight_changes[half], score_changes[half]
            weight_change[:, 0:SLOTS] = dot_nt(jnp.concatenate([own_scaled, extra], 1), value_side)
            kinds = [jnp.zeros((16, WIDE), F32), jnp.zeros((16, WIDE), F32)]
            for group in range(STRIP // 16 - 1, -1, -1):
                tiles = [[jnp.zeros((16, 128), F32)] * (WIDE // 128) for _ in range(2)]
                for major in range(-(-SLOTS // STRIP)):
                    start = major * STRIP + group * 16
                    if start >= SLOTS:
                        continue
                    rows = slice(start, start + 16)
                    low_code = query_codes[0, rows, :]
                    high_code = query_codes[1, rows, :]
                    for column in range(-(-SLOTS // 128)):
                        span = slice(column * 128, column * 128 + 128)
                        value = chance[half, rows, span].astype(F32) * weight_change[rows, span]
                        code = jnp.broadcast_to(key_code[0:1, span], (16, 128))
                        if column * 128 + 128 > SLOTS:
                            inside = lax.broadcasted_iota(jnp.int32, (16, 128), 1) < SLOTS - column * 128
                            value = jnp.where(inside, value, 0.0)
                        score_change[rows, span] = value.astype(BF16)
                        place = 4 - major + column
                        tiles[0][place] = tiles[0][place] + jnp.where(low_code >= code, value, 0.0)
                        tiles[1][place] = tiles[1][place] + jnp.where(code > high_code, value, 0.0)
                for which in range(2):
                    fresh = jnp.concatenate(tiles[which], 1)
                    if group == STRIP // 16 - 1:
                        kinds[which] = fresh
                    else:
                        kinds[which] = pltpu.roll(kinds[which], WIDE - 16, 1) + fresh
            for which in range(2):
                band_sums[head, which] = kinds[which][0:8] + pltpu.roll(kinds[which][8:16], WIDE - 8, 1)
            own_score = score_change[:, 0:SLOTS]
            key_side = jnp.concatenate([keep(mask, keys[:, lanes]), picks[...]], 1)
            both = dot(own_score, key_side)
            query_total = query_total + both[:, :128]
            near_sums[head] = dot_tn(picks[...], both[:, 128:].astype(BF16))
            key_total = key_total + dot_tn(own_score, keep(mask, query[:, lanes]))
            value_total = value_total + dot_tn(chance[half, :, 0:SLOTS], own_scaled)
        joined[0][:, lanes] = (query_total.astype(BF16).astype(F32) * HEAD**-0.5).astype(BF16)
        joined[1][:, lanes] = key_total.astype(BF16)
        joined[2][:, lanes] = value_total.astype(BF16)
        return carry

    lax.fori_loop(0, PAIRS, pair_step, 0)


def table_back(info, band_sums, near_sums, table_sum):
    kinds = []
    for which in range(2):
        total = jnp.zeros((16, WIDE), F32)
        for step in range(8):
            rows = jnp.concatenate(
                [band_sums[head, which, step : step + 1, :] for head in range(HEADS)]
                + [jnp.zeros((16 - HEADS, WIDE), F32)],
                0,
            )
            total = total + (rows if step == 0 else pltpu.roll(rows, WIDE - step, 1))
        kinds.append(total)
    low, high = kinds
    width = info["large_width"]
    entry = lax.broadcasted_iota(jnp.int32, (16, 128), 1)
    low_hit = (entry >= GRID - width) & (entry <= GRID - 1)
    high_hit = (entry >= GRID) & (entry <= GRID - 2 + width)

    table_sum[...] = jnp.zeros_like(table_sum)
    lane_wide = lax.broadcasted_iota(jnp.int32, (16, 256), 1)

    def line_step(line, carry):
        block, lane = line_place(line)
        back = WIDE - shift_of(info, line)
        low_part = pltpu.roll(low, back, 1)[:, :128]
        high_part = pltpu.roll(high, back, 1)[:, :128]
        part = jnp.where(low_hit, low_part, jnp.where(high_hit, high_part, 0.0))
        wide = pltpu.roll(jnp.concatenate([part, jnp.zeros((16, 128), F32)], 1), lane, 1)
        table_sum[block] += wide[:, :128]
        table_sum[block + 1] += wide[:, 128:]
        return carry

    lax.fori_loop(0, SPAN, line_step, 0)
    index = compact_index(info)
    head_row = lax.broadcasted_iota(jnp.int32, (16, 128), 0)
    centre = jnp.zeros((16, 128), F32)
    for head in range(HEADS):
        at = COMPACT + IMGS
        centre = jnp.where(head_row == head, near_sums[head, at : at + 1, :], centre)
    centre = jnp.sum(jnp.where(entry == COMPACT + IMGS, centre, 0.0), 1, keepdims=True)
    for number in range(25):
        hit = index == number
        column = jnp.zeros((16, 128), F32)
        for head in range(HEADS):
            part = jnp.sum(jnp.where(hit, near_sums[head, 0:COMPACT, :], 0.0), 0, keepdims=True)
            column = jnp.where(head_row == head, part, column)
        total = jnp.sum(column, 1, keepdims=True)
        if number == 12:
            total = total + centre
        at = LINES * 128 - 1 - (GRID - 3 + number // 5) * SPAN - (GRID - 3 + number % 5)
        table_sum[at // 128] += jnp.where(entry == at % 128, total, 0.0)


def remote(source, target, send, receive, device):
    return pltpu.make_async_remote_copy(
        src_ref=source,
        dst_ref=target,
        send_sem=send,
        recv_sem=receive,
        device_id=device,
        device_id_type=pl.DeviceIdType.MESH,
    )


def greet(devices):
    barrier = pltpu.get_barrier_semaphore()
    for device in devices:
        pl.semaphore_signal(barrier, inc=1, device_id=device, device_id_type=pl.DeviceIdType.MESH)
    pl.semaphore_wait(barrier, len(devices))


def group_peers(parts):
    row, me = lax.axis_index("rows"), lax.axis_index("seq")
    return row, me, [lax.rem(me + step, parts) for step in range(1, parts)]


def block_of(index, size):
    return pl.ds(pl.multiple_of(index * size, size), size)


def forward_kernel(heights, widths, order, table, *refs):
    rows_of, refs = refs[:11], refs[11:]
    forward_body(heights, widths, order, table, rows_of, *refs)


def stack_rows(rows_of, vec):
    vec[...] = jnp.zeros_like(vec)
    line = 0
    for item in rows_of:
        for start in range(0, item.shape[0], 128):
            where = start // MODEL + line
            lanes = slice(start % MODEL, start % MODEL + 128)
            vec[where : where + 1, lanes] = item[start : start + 128].astype(F32).reshape(1, 128)
        line += item.shape[0] // MODEL


def forward_body(heights, widths, order, table, rows_of, input_weight, output_weight, own_tokens, own_upstream, *rest):
    (tokens_far, upstream, first_far, query_far, keys_far, values_far, chance_far, attended_far, inverse_far, branch_far, middle_far, attended_low_far, second, picks, query_codes, key_code, vec), rest = rest[:17], rest[17:]
    (tokens, first, query, keys, values, attended, inverse, branch, middle, attended_low, chance, bands, near, score, other_score, low_strip, high_strip, other_low, other_high, flat, turned, columns, store_sems, chance_sems, send, receive, local) = rest
    parts, slots = own_tokens.shape[0], own_tokens.shape[1]
    row, me, peers = group_peers(parts)
    greet([(row, peer) for peer in peers])

    def exchange(which, source, target):
        mine = block_of(me, slots)
        copies = [
            remote(source.at[peer], target.at[mine], send.at[which, step], receive.at[which, step], (row, peer))
            for step, peer in enumerate(peers)
        ]
        return copies + [pltpu.make_async_copy(source.at[me], target.at[mine], local.at[which])]

    token_copies = exchange(0, own_tokens, tokens)
    upstream_copies = exchange(1, own_upstream, upstream)
    stores = {
        number: pltpu.make_async_copy(source, target, store_sems.at[number])
        for number, (source, target) in enumerate(
            (
                (tokens, tokens_far),
                (first, first_far),
                (query, query_far),
                (keys, keys_far),
                (values, values_far),
                (attended, attended_far),
                (inverse, inverse_far),
                (attended_low, attended_low_far),
                (branch, branch_far),
                (middle, middle_far),
            )
        )
    }
    for copy in token_copies:
        copy.start()
    stack_rows(rows_of, vec)
    info = row_scalars(heights, widths, order, me)
    prepare(info, table, flat, turned, columns, picks, query_codes, key_code, bands, near)
    for copy in token_copies:
        copy.wait()
    for copy in upstream_copies:
        copy.start()
    stores[0].start()
    project_in(tokens, vec, input_weight, first, query, keys, values)
    for number in range(1, 5):
        stores[number].start()

    def chance_copy(pair):
        slot = lax.rem(pair, 2)
        return pltpu.make_async_copy(chance.at[slot], chance_far.at[pl.ds(pair * 2, 2)], chance_sems.at[slot])

    def chance_of(pair):
        @pl.when(pair >= 2)
        def _():
            chance_copy(pair - 2).wait()

        return chance.at[lax.rem(pair, 2)]

    attend(query, keys, values, picks, query_codes, key_code, bands, near, chance_of, attended, inverse, (score, other_score), ((low_strip, high_strip), (other_low, other_high)), lambda pair: chance_copy(pair).start())
    for number in (5, 6):
        stores[number].start()
    project_out(tokens, attended, output_weight, vec, branch, middle, second, attended_low)
    for number in (7, 8, 9):
        stores[number].start()
    for pair in (PAIRS - 2, PAIRS - 1):
        chance_copy(jnp.int32(pair)).wait()
    for number in stores:
        stores[number].wait()
    for copy in upstream_copies:
        copy.wait()


UNITS = ((128, 384), (128, 384), (128, 384), (144, 384), (48, 384))
LATE = (
    (((0, 0, 128), (0, 256, 384), (0, 384, 512)), ((0, 640, 768), (1, 0, 128), (1, 256, 384)), ((1, 384, 512), (1, 640, 768), (2, 0, 128)), ((2, 256, 384), (2, 384, 512), (2, 640, 768))),
    (((0, 128, 256), (0, 512, 576)), ((1, 128, 256), (0, 576, 640)), ((1, 512, 640), (2, 128, 192)), ((2, 512, 640), (2, 192, 256))),
)


SPLITS = (80, 64, 80, 64, 32)
PLAN = {
    ("slab", 1, 3): (("first", 0),),
    ("slab", 2, 2): (("second_y", 0),),
    ("slab", 2, 3): (("first", 1),),
    "norm": (("first", 2),),
    ("middle", 0): (("second_y", 1), ("second_x", 0)),
    ("pair", 3): (("second_x", 1),),
    ("pair", 4): (("second_y", 2), ("second_x", 2), ("third", 0)),
    ("pair", 5): (("first", 3), ("third", 1), ("third", 2)),
    "products": (("second_x", 3),),
    "given": (("second_y", 3), ("fourth", 0)),
    ("small", 0): (("first", 4),),
    ("small", 1): (("third", 3),),
    ("small", 2): (("second_y", 4), ("second_x", 4)),
    ("small", 4): (("third", 4), ("fourth", 1), ("fourth", 2), ("fourth", 3)),
}


class Reduction:
    def __init__(self, sources, results, owns, core_in, x_in, y_in, late, line_in, send, receive, local):
        self.sources, self.results, self.owns = sources, results, owns
        self.core_in, self.x_in, self.y_in, self.late, self.line_in = core_in, x_in, y_in, late, line_in
        self.send, self.receive, self.local = send, receive, local
        rows, seq = lax.axis_index("rows"), lax.axis_index("seq")
        self.z, self.x, self.y, self.core = rows // 2, rows % 2, seq // 2, seq % 2
        z, x, y, core = self.z, self.x, self.y, self.core
        self.core_peer = (rows, y * 2 + 1 - core)
        self.x_peer = (z * 2 + 1 - x, seq)
        self.y_peer = (rows, (1 - y) * 2 + core)
        self.diagonal = (z * 2 + 1 - x, (1 - y) * 2 + core)
        self.z_peers = [(lax.rem(z + step, 4) * 2 + x, seq) for step in range(1, 4)]

    def cut(self, unit):
        return SPLITS[unit]

    def go(self, place):
        for name, unit in PLAN.get(place, ()):
            getattr(self, name)(unit)

    def peers(self):
        return [self.core_peer, self.x_peer, self.y_peer, self.diagonal] + self.z_peers

    def copy(self, unit, number, source, target, peer):
        return remote(source, target, self.send.at[unit, number], self.receive.at[unit, number], peer)

    def core_copies(self, unit):
        return [
            self.copy(unit, part, self.sources[unit].at[part * 2 + 1 - self.core], self.core_in[unit].at[part], self.core_peer)
            for part in range(2)
        ]

    def own_copies(self, unit):
        if self.owns[unit] is None:
            return []
        return [
            pltpu.make_async_copy(self.sources[unit].at[part * 2 + self.core], self.owns[unit].at[part], self.local.at[unit, part])
            for part in range(2)
        ]

    def x_copy(self, unit):
        return self.copy(unit, 2, self.core_in[unit].at[:, :, 1 - self.x, 0 : self.cut(unit)], self.x_in[unit], self.x_peer)

    def y_copy(self, unit):
        return self.copy(unit, 3, self.core_in[unit].at[1 - self.y, :, :, self.cut(unit) :], self.y_in[unit], self.y_peer)

    def again_y(self, unit):
        return self.copy(unit, 4, self.x_in[unit].at[1 - self.y], self.late[unit].at[:, 0 : self.cut(unit)], self.y_peer)

    def again_x(self, unit):
        return self.copy(unit, 5, self.y_in[unit].at[:, 1 - self.x], self.late[unit].at[:, self.cut(unit) :], self.x_peer)

    def line_copies(self, unit):
        return [
            self.copy(unit, 6 + step, self.late[unit].at[lax.rem(self.z + step + 1, 4)], self.line_in[unit].at[step], peer)
            for step, peer in enumerate(self.z_peers)
        ]

    def begin(self, unit):
        for copy in self.core_copies(unit):
            copy.start()

    def fetch(self, unit):
        for copy in self.own_copies(unit):
            copy.start()

    def first(self, unit):
        for copy in self.core_copies(unit) + self.own_copies(unit):
            copy.wait()
        held, own = self.core_in[unit], self.owns[unit]

        def add(line, carry):
            for part in range(2):
                for side in range(2):
                    if own is None:
                        term = self.sources[unit][part * 2 + self.core, line, side]
                    else:
                        term = own[part, line, side]
                    held[part, line, side] = held[part, line, side] + term
            return carry

        lax.fori_loop(0, 4, add, 0)
        self.x_copy(unit).start()
        self.y_copy(unit).start()

    def second_x(self, unit):
        x_in, held = self.x_in[unit], self.core_in[unit]
        self.x_copy(unit).wait()

        def add_x(line, carry):
            for part in range(2):
                x_in[part, line] = x_in[part, line] + held[part, line, self.x, 0 : self.cut(unit)]
            return carry

        lax.fori_loop(0, 4, add_x, 0)
        self.again_y(unit).start()

    def second_y(self, unit):
        y_in, held = self.y_in[unit], self.core_in[unit]
        self.y_copy(unit).wait()

        def add_y(line, carry):
            for side in range(2):
                y_in[line, side] = y_in[line, side] + held[self.y, line, side, self.cut(unit) :]
            return carry

        lax.fori_loop(0, 4, add_y, 0)
        self.again_x(unit).start()

    def third(self, unit):
        late, x_in, y_in = self.late[unit], self.x_in[unit], self.y_in[unit]
        self.again_y(unit).wait()
        self.again_x(unit).wait()

        def add(line, carry):
            late[line, 0 : self.cut(unit)] = late[line, 0 : self.cut(unit)] + x_in[self.y, line]
            late[line, self.cut(unit) :] = late[line, self.cut(unit) :] + y_in[line, self.x]
            return carry

        lax.fori_loop(0, 4, add, 0)
        for copy in self.line_copies(unit):
            copy.start()

    def fourth(self, unit):
        for copy in self.line_copies(unit):
            copy.wait()
        total = self.late[unit][self.z].astype(F32)
        for step in range(3):
            total = total + self.line_in[unit][step].astype(F32)
        self.results[unit](total)


class SmallSum:
    def __init__(self, link, small, out, core_in, plane_in, line_in, part, send, receive):
        self.link, self.small, self.out = link, small, out
        self.core_in, self.plane_in, self.line_in, self.part = core_in, plane_in, line_in, part
        self.send, self.receive = send, receive
        plane = link.x * 2 + link.y
        self.plane = plane
        self.plane_peers = (
            (link.x_peer, lax.rem(plane + 2, 4)),
            (link.y_peer, plane + 1 - 2 * link.y),
            (link.diagonal, 3 - plane),
        )

    def copy(self, number, source, target, peer):
        return remote(source, target, self.send.at[number], self.receive.at[number], peer)

    def core_copy(self):
        return self.copy(0, self.small.at[1 - self.link.core], self.core_in, self.link.core_peer)

    def plane_copies(self):
        return [
            self.copy(1 + step, self.core_in.at[index], self.plane_in.at[step], peer)
            for step, (peer, index) in enumerate(self.plane_peers)
        ]

    def line_copies(self):
        return [self.copy(4 + step, self.part, self.line_in.at[step], peer) for step, peer in enumerate(self.link.z_peers)]

    def plane_back(self):
        mine = self.out.at[self.link.core, self.plane]
        return [self.copy(10 + step, mine, mine, peer) for step, (peer, _) in enumerate(self.plane_peers)]

    def core_back(self):
        mine = self.out.at[self.link.core]
        return self.copy(13, mine, mine, self.link.core_peer)

    def steps(self):
        def one():
            self.core_copy().start()

        def two():
            self.core_copy().wait()
            self.core_in[...] += self.small[self.link.core]
            for copy in self.plane_copies():
                copy.start()

        def three():
            for copy in self.plane_copies():
                copy.wait()
            self.part[...] = self.core_in[self.plane] + self.plane_in[0] + self.plane_in[1] + self.plane_in[2]
            for copy in self.line_copies():
                copy.start()

        def four():
            for copy in self.line_copies():
                copy.wait()
            self.out[self.link.core, self.plane] = self.part[...] + self.line_in[0] + self.line_in[1] + self.line_in[2]
            for copy in self.plane_back():
                copy.start()

        def five():
            for copy in self.plane_back():
                copy.wait()
            self.core_back().start()

        def six():
            self.core_back().wait()

        return [one, two, three, four, five, six]


def pack_small(table_sum, sums, feed_sums, up_sum, vectors, small):
    for block in range(32):
        where = (block // 16, block // 4 % 4, block % 4)
        if block < LINES:
            small[where] = table_sum[block]
        elif block >= LINES + 6:
            small[where] = jnp.zeros((16, 128), F32)
    vectors[...] = jnp.zeros_like(vectors)
    for number in range(8):
        vectors[number : number + 1, :] = jnp.sum(sums[number], 0, keepdims=True)
    for number in range(2):
        vectors[8 + number : 9 + number, :] = jnp.sum(feed_sums[number], 0, keepdims=True)
    for number in range(PARTS):
        vectors[10 + number : 11 + number, :] = up_sum[0:1, number * MODEL : (number + 1) * MODEL]
    for number in range(6):
        block = LINES + number
        where = (block // 16, block // 4 % 4, block % 4)
        small[where] = vectors[:, number * 128 : (number + 1) * 128]


def backward_kernel(paired, heights, widths, order, vec, upstream, second, picks, query_codes, key_code, output_weight, up_far, down_far, weight_far, tokens_far, first_far, query_far, keys_far, values_far, attended_far, inverse_far, branch_far, middle_far, attended_low_far, chance_far, *rest):
    if paired:
        (own_output, own_gradient, up_result, down_result), late_results, small_out, rest = rest[:4], rest[4:7], rest[7], rest[8:]
    else:
        (own_output, own_gradient, feed_units), late_outs, small_out, rest = rest[:3], rest[3:5], rest[5], rest[6:]
    (hidden, change, active, slope, outcome_change, outcome, second_change, branch_change, change_low, attended_low, output, query, keys, values, first, up_tile, down_tile, chance, weight_change, score_change, band_sums, near_sums, table_sum, sums, feed_sums, up_sum, vectors, unit, small), rest = rest[:29], rest[29:]
    (tile_sems, load_sems, chance_sems, send, receive, local), rest = rest[:6], rest[6:]
    parts, slots = own_output.shape[0], own_output.shape[1]
    row, me, peers = group_peers(parts)
    feed_unit = unit.at[:, :, :, 0:128, :]
    if paired:
        count = len(UNITS)
        stages = [rest[i * count : (i + 1) * count] for i in range(5)]
        rest = rest[5 * count :]
        sources = [feed_unit] * TILES + [unit, unit.at[:, :, :, 0:48, :]]

        def feed_result(tile):
            def put(total):
                for half in range(2):
                    columns = slice(half * 384 + tile * 128, half * 384 + tile * 128 + 128)
                    up_result[:, columns] = total[0:96, half * 128 : half * 128 + 128]
                columns = slice(tile * 128, tile * 128 + 128)
                down_result[0:96, columns] = total[0:96, 256:384]
                for third in range(3):
                    lines = slice(96 + third * 32, 128 + third * 32)
                    down_result[lines, columns] = total[96:128, third * 128 : third * 128 + 128]

            return put

        def first_put(total):
            late_results[0][...] = total[0:96]
            for half in range(2):
                late_results[2][half * 48 : half * 48 + 48, :] = total[96:144, half * 192 : half * 192 + 192]

        def second_put(total):
            for half in range(2):
                late_results[1][half * 48 : half * 48 + 48, :] = total[:, half * 192 : half * 192 + 192]

        results = [feed_result(tile) for tile in range(TILES)] + [first_put, second_put]
        link = Reduction(sources, results, [None] * count, *stages, *rest[:2], None)
        small_sum = SmallSum(link, small, small_out, *rest[2:])
        greet(link.peers() + [(row, (1 - link.y) * 2 + 1 - link.core)])
    else:
        greet([(row, peer) for peer in peers])

    def give_back(which, source, target):
        copies = [
            remote(source.at[block_of(peer, slots)], target.at[me], send.at[which, step], receive.at[which, step], (row, peer))
            for step, peer in enumerate(peers)
        ]
        return copies + [pltpu.make_async_copy(source.at[block_of(me, slots)], target.at[me], local.at[which])]

    gradient = change_low
    output_copies = give_back(0, output, own_output)
    gradient_copies = give_back(1, gradient, own_gradient)
    wide = slice(0, MODEL)

    def load(number, source, target):
        return pltpu.make_async_copy(source, target, load_sems.at[number])

    load_query = load(0, query_far, query)
    load_keys = load(1, keys_far, keys)
    load_values = load(2, values_far, values)
    load_first = load(3, first_far, first)
    load_low = load(4, attended_low_far, attended_low)
    load_middle = load(5, middle_far, change.at[:, wide])
    load_branch = load(6, branch_far, hidden.at[:, wide])
    load_attended = load(7, attended_far, hidden.at[:, wide])
    load_inverse = load(8, inverse_far, change.at[:, wide])
    load_tokens = load(9, tokens_far, query)
    in_weights = (up_tile.at[0, :, wide], up_tile.at[1, :, wide], down_tile.at[0, wide, :])
    load_weights = [
        load(10 + number, weight_far.at[:, number * MODEL : (number + 1) * MODEL], target)
        for number, target in enumerate(in_weights)
    ]

    def chance_copy(turn):
        slot = lax.rem(turn, 2)
        return pltpu.make_async_copy(chance_far.at[pl.ds(pair_at(turn) * 2, 2)], chance.at[slot], chance_sems.at[slot])

    for copy in (load_query, load_keys, load_values, load_first, load_low):
        copy.start()
    chance_copy(jnp.int32(0)).start()

    def before(tile, pair):
        if tile == TILES - 1 and pair == 3:
            load_middle.start()
            load_branch.start()
        if paired:
            link.go(("slab", tile, pair))

    def after(tile):
        if paired:
            link.begin(tile)
        else:
            copy = load(13, feed_unit, feed_units.at[tile])
            copy.start()
            copy.wait()

    feed(second, upstream, up_far, down_far, vec, second_change, feed_unit, up_sum, feed_sums, outcome_change, outcome, active, slope, up_tile, down_tile, tile_sems, before, after)
    for copy in load_weights:
        copy.start()
    load_middle.wait()
    feed_end(upstream, change, vec, output, outcome, feed_sums)
    for copy in output_copies:
        copy.start()
    load_branch.wait()
    info = row_scalars(heights, widths, order, me)
    sums[...] = jnp.zeros_like(sums)
    middle_change = outcome
    gain, scale = vec[SECOND_GAIN : SECOND_GAIN + 1, :], vec[ATTENTION_SCALE : ATTENTION_SCALE + 1, :]

    def norm(rows):
        normal, spread = normal_of(change[rows, wide])
        back = second_change[rows, :]
        sums[6] += fold(back * normal)
        sums[7] += fold(back)
        value = upstream[rows, :].astype(F32) + normal_back(back, normal, spread, gain)
        middle_change[rows, :] = value
        sums[5] += fold(value * hidden[rows, wide])
        low = (value * scale).astype(BF16)
        branch_change[rows, :] = low
        sums[4] += fold(low.astype(F32))

    chunks(norm)
    load_attended.start()
    load_inverse.start()
    change_low[...] = dot_nt(branch_change[...], output_weight[...]).astype(BF16)
    if paired:
        link.go("norm")
    for copy in (load_query, load_keys, load_values, load_attended, load_inverse):
        copy.wait()

    joined = (active, slope, outcome_change)

    def packed(value):
        value = value.astype(BF16).reshape(4, 2, 2, 48, 192)
        return jnp.concatenate([value[:, :, 0], value[:, :, 1]], -1)

    def late_parts(number):
        for part in range(PARTS):
            pieces = [joined[which][:, low:high] for which, low, high in LATE[number][part]]
            value = dot_tn(first[...], jnp.concatenate(pieces, 1))
            if number == 1:
                unit[part, :, :, 0:48, 0:384] = packed(value)
            else:
                unit[part, :, :, 0:96, 0:384] = value.astype(BF16).reshape(4, 2, 96, 384)
                piece = branch_change[:, part * 192 : part * 192 + 192]
                unit[part, :, :, 96:144, 0:384] = packed(dot_tn(attended_low[...], piece))
        if paired:
            link.begin(TILES + number)
        else:
            source = unit if number == 0 else unit.at[:, :, :, 0:48, :]
            copy = load(13, source, late_outs[number])
            copy.start()
            copy.wait()

    def at_turn(name, turn):
        for number in range(PAIRS):
            if paired and (name, number) in PLAN:

                @pl.when(turn == number)
                def _(number=number):
                    link.go((name, number))

    def event(turn):
        @pl.when(turn + 1 < PAIRS)
        def _():
            chance_copy(turn + 1).start()

        chance_copy(turn).wait()

        @pl.when(turn == 4)
        def _():
            load_first.wait()
            load_low.wait()
            late_parts(0)

        at_turn("pair", turn)

    def middle_event(turn):
        at_turn("middle", turn)

    attend_back(query, keys, values, picks, query_codes, key_code, lambda turn: chance.at[lax.rem(turn, 2)], change_low, hidden, change, joined, band_sums, near_sums, (weight_change, weight_change), (score_change, score_change), event, middle_event)
    load_tokens.start()
    late_parts(1)
    for copy in load_weights:
        copy.wait()
    first_change = hidden
    for start in range(0, MODEL, 256):
        lanes = slice(start, start + 256)
        total = dot_nt(joined[0][:, wide], in_weights[0][lanes, :])
        total = total + dot_nt(joined[1][:, wide], in_weights[1][lanes, :])
        first_change[:, lanes] = total + dot_nt(joined[2][...], in_weights[2][lanes, :])
    load_tokens.wait()
    gain_first = vec[FIRST_GAIN : FIRST_GAIN + 1, :]
    if paired:
        link.go("products")

    def norm_first(rows):
        normal, spread = normal_of(query[rows, :].astype(F32))
        back = first_change[rows, wide]
        sums[0] += fold(back * normal)
        sums[1] += fold(back)
        sums[2] += fold(joined[0][rows, wide].astype(F32))
        sums[3] += fold(joined[2][rows, :].astype(F32))
        value = middle_change[rows, :] + normal_back(back, normal, spread, gain_first)
        gradient[rows, :] = value.astype(BF16)

    chunks(norm_first)
    for copy in gradient_copies:
        copy.start()
    if paired:
        link.go("given")
    table_back(info, band_sums, near_sums, table_sum)
    pack_small(table_sum, sums, feed_sums, up_sum, vectors, small)
    if paired:
        for number, step in enumerate(small_sum.steps()):
            step()
            link.go(("small", number))
        link.fourth(4)
    else:
        small_out[...] = small[...]
    for copy in output_copies + gradient_copies:
        copy.wait()


def whole():
    return pl.BlockSpec(memory_space=pltpu.VMEM)


def far():
    return pl.BlockSpec(memory_space=pl.ANY)


def scalars():
    return pl.BlockSpec(memory_space=pltpu.SMEM)


def shape(*dims, dtype=F32):
    return jax.ShapeDtypeStruct(dims, dtype)


def on_device(layer_input, first_gain, first_shift, input_weight, query_bias, value_bias, bias_table, output_weight, output_bias, attention_scale, second_gain, second_shift, up_weight, up_bias, down_weight, down_bias, feed_scale, upstream, grid_heights, grid_widths, packing_order):
    parts = lax.axis_size("seq")
    paired = (lax.axis_size("rows"), parts) == (8, 4)
    slots = layer_input.shape[1]
    hidden_units = up_weight.shape[1]

    rows_of = [first_gain, first_shift, query_bias, value_bias, output_bias, attention_scale, second_gain, second_shift, down_bias, feed_scale, up_bias]
    full = (SLOTS, MODEL)
    low_full, wide_full = shape(*full, dtype=BF16), shape(*full)
    dma = pltpu.SemaphoreType.DMA
    vmem = pltpu.VMEM
    exchange_sems = [dma((2, parts - 1)), dma((2, parts - 1)), dma((2,))]
    (tokens, own_upstream, first, query, keys, values, chance, attended, inverse, branch, middle, attended_low, second, picks, query_codes, key_code, vec) = pl.pallas_call(
        forward_kernel,
        out_shape=[low_full] * 6
        + [shape(HEADS, SLOTS, PADDED, dtype=BF16)]
        + [wide_full] * 4
        + [low_full] * 2
        + [shape(SLOTS, 128, dtype=BF16), shape(2, SLOTS, 128), shape(8, PADDED), shape(16, MODEL)],
        in_specs=[scalars()] * 3 + [whole()] * 14 + [far()] * 2,
        out_specs=[far()] * 12 + [whole()] * 5,
        scratch_shapes=[vmem(full, BF16)] * 5
        + [vmem(full, F32)] * 4
        + [
            vmem(full, BF16),
            vmem((2, 2, SLOTS, PADDED), BF16),
            vmem((HEADS, 2, 8, WIDE), F32),
            vmem((HEADS, 128, 128), BF16),
            vmem((SLOTS, SLOTS), F32),
            vmem((SLOTS, SLOTS), F32),
            vmem((STRIP, WIDE), F32),
            vmem((STRIP, WIDE), F32),
            vmem((STRIP, WIDE), F32),
            vmem((STRIP, WIDE), F32),
            vmem((16, LINES * 128), F32),
            vmem((LINES + 1, 16, 128), F32),
            vmem((25, 16, 128), F32),
            dma((10,)),
            dma((2,)),
        ]
        + exchange_sems,
        compiler_params=pltpu.CompilerParams(collective_id=0, has_side_effects=True, vmem_limit_bytes=VMEM_LIMIT),
        name="forward",
    )(
        grid_heights, grid_widths, packing_order, bias_table.T, *rows_of, input_weight, output_weight,
        layer_input, upstream,
    )

    outs = [(shape(parts, slots, MODEL, dtype=BF16), far())] * 2
    unit_shape, small_shape = (4, 4, 2, 144, 384), (2, 4, 4, 16, 128)
    scratch = [
        vmem(full, F32),
        vmem(full, F32),
        vmem((SLOTS, 1024), BF16),
        vmem((SLOTS, 1024), BF16),
        vmem(full, BF16),
        vmem(full, F32),
        vmem(full, F32),
    ]
    scratch += [vmem(full, BF16)] * 8
    scratch += [
        vmem((2, MODEL, 1024), BF16),
        vmem((2, 1024, MODEL), BF16),
        vmem((2, 2, SLOTS, PADDED), BF16),
        vmem((SLOTS, PADDED), F32),
        vmem((SLOTS, PADDED), BF16),
        vmem((HEADS, 2, 8, WIDE), F32),
        vmem((HEADS, 128, 128), F32),
        vmem((LINES + 1, 16, 128), F32),
        vmem((8, 8, MODEL), F32),
        vmem((2, 8, MODEL), F32),
        vmem((8, hidden_units), F32),
        vmem((16, MODEL), F32),
        vmem(unit_shape, BF16),
        vmem(small_shape, F32),
        dma((2, 2, BLOCKS)),
        dma((14,)),
        dma((2,)),
    ] + exchange_sems
    if paired:
        outs += [
            (shape(96, 768), whole()),
            (shape(192, 384), whole()),
            (shape(96, 384), whole()),
            (shape(96, 192), whole()),
            (shape(96, 192), whole()),
            (shape(*small_shape), whole()),
        ]
        for dims in (
            lambda r, c, cut: (2, 4, 2, r, c),
            lambda r, c, cut: (2, 4, cut, c),
            lambda r, c, cut: (4, 2, r - cut, c),
            lambda r, c, cut: (4, r, c),
            lambda r, c, cut: (3, r, c),
        ):
            scratch += [vmem(dims(*item, cut), BF16) for item, cut in zip(UNITS, SPLITS)]
        count = len(UNITS)
        scratch += [dma((count, 9)), dma((count, 9))]
        scratch += [
            vmem((4, 4, 16, 128), F32),
            vmem((3, 4, 16, 128), F32),
            vmem((3, 4, 16, 128), F32),
            vmem((4, 16, 128), F32),
            dma((14,)),
            dma((14,)),
        ]
    else:
        outs += [
            (shape(TILES, 4, 4, 2, 128, 384, dtype=BF16), far()),
            (shape(4, 4, 2, 144, 384, dtype=BF16), far()),
            (shape(4, 4, 2, 48, 384, dtype=BF16), far()),
            (shape(*small_shape), whole()),
        ]
    results = pl.pallas_call(
        functools.partial(backward_kernel, paired),
        out_shape=[item[0] for item in outs],
        in_specs=[scalars()] * 3 + [whole()] * 7 + [far()] * 14,
        out_specs=[item[1] for item in outs],
        scratch_shapes=scratch,
        compiler_params=pltpu.CompilerParams(collective_id=1, has_side_effects=True, vmem_limit_bytes=VMEM_LIMIT),
        name="backward",
    )(
        grid_heights, grid_widths, packing_order, vec, own_upstream, second, picks, query_codes, key_code, output_weight,
        up_weight, down_weight, input_weight, tokens, first, query, keys, values, attended, inverse, branch, middle,
        attended_low, chance,
    )
    own_output, own_gradient = results[:2]
    if paired:
        up_result, down_result, late_first, late_second, output_part, small = results[2:]
    else:
        feed_units, late_first, late_second, small = results[2:]
        up_unit, down_unit = restore_feed(feed_units)
        up_result, down_result = reduce_any_mesh(up_unit), reduce_any_mesh(down_unit)
        packed = jnp.concatenate([late_first[:, :, :, 96:144], late_second], 4).reshape(PARTS, BLOCKS, 48, 2, 2, 192)
        packed = jnp.transpose(packed, (3, 0, 1, 4, 2, 5)).reshape(2, PARTS, MODEL, 192)
        output_part, late_second = reduce_any_mesh(packed[0]), reduce_any_mesh(packed[1])
        late_first = reduce_any_mesh(late_first[:, :, :, 0:96].reshape(PARTS, MODEL, 384))
        small = lax.psum(small, ("rows", "seq"))
    lines = late_first.shape[0]
    done = pl.pallas_call(
        finish_kernel,
        out_shape=[
            shape(parts, slots, MODEL, dtype=BF16),
            shape(parts, slots, MODEL),
            shape(lines, 576),
            shape(lines, 192),
            shape(HEADS, SPAN * SPAN),
        ]
        + [shape(MODEL)] * 10
        + [shape(hidden_units)],
        in_specs=[whole()] * 6,
        out_specs=[whole()] * 16,
        scratch_shapes=[vmem((16, LINES * 128), F32)],
        compiler_params=pltpu.CompilerParams(vmem_limit_bytes=VMEM_LIMIT),
        name="finish",
    )(own_output, own_gradient, late_first, late_second, output_part, small.reshape(32, 16, 128))
    own_output, own_gradient, input_result, output_result, table = done[:5]
    vectors = done[5:]
    return (
        own_output,
        own_gradient,
        vectors[0],
        vectors[1],
        input_result,
        vectors[2],
        vectors[3],
        table.T,
        output_result,
        vectors[4],
        vectors[5],
        vectors[6],
        vectors[7],
        up_result,
        vectors[10],
        down_result if down_result.shape[1] == 192 else down_result.T,
        vectors[9],
        vectors[8],
    )


def finish_kernel(output_in, gradient_in, late_first, late_second, output_part, small, output, gradient, input_result, output_result, table, *rest):
    vectors, flat = rest[:-1], rest[-1]
    output[...] = output_in[...]
    for part in range(gradient.shape[0]):
        gradient[part] = gradient_in[part].astype(F32)
    first, second = late_first[...], late_second[...]
    pieces = [first[:, 0:128], first[:, 128:256], first[:, 256:384], second[:, 0:128], second[:, 128:192]]
    even = jnp.concatenate([pieces[0], pieces[3], pieces[1], pieces[2], pieces[4]], 1)
    odd = jnp.concatenate([pieces[4], pieces[0], pieces[1], pieces[3], pieces[2]], 1)
    side = jnp.full(even.shape, lax.rem(lax.axis_index("seq"), 2), jnp.int32)
    input_result[...] = jnp.where(side == 0, even, odd)
    output_result[...] = output_part[...]
    mirror = flip()
    for block in range(LINES):
        rest = small[block]
        total = jnp.zeros((16, 128), F32)
        for _ in range(3):
            low = rest.astype(BF16)
            total = total + dot(low, mirror)
            rest = rest - low.astype(F32)
        lanes = slice((LINES - 1 - block) * 128, (LINES - block) * 128)
        flat[:, lanes] = total
    table[...] = flat[0:HEADS, 0 : SPAN * SPAN]
    for number in range(14):
        target, start = vectors[min(number, 10)], max(number - 10, 0) * MODEL
        for block in range(6):
            row = small[LINES + block, number : number + 1, :]
            target[start + block * 128 : start + block * 128 + 128] = row.reshape(128)


def restore_feed(units):
    up = units[..., :96, :256].reshape(TILES, PARTS, BLOCKS, 96, 2, 128)
    up = jnp.transpose(up, (1, 2, 3, 4, 0, 5)).reshape(PARTS, MODEL, MODEL)
    low = units[..., :96, 256:].reshape(TILES, PARTS, BLOCKS, 96, 128)
    high = units[..., 96:, :].reshape(TILES, PARTS, BLOCKS, 32, 3, 128)
    high = jnp.transpose(high, (0, 1, 2, 4, 3, 5)).reshape(TILES, PARTS, BLOCKS, 96, 128)
    down = jnp.concatenate([low, high], 3)
    down = jnp.transpose(down, (1, 2, 0, 4, 3)).reshape(PARTS, BLOCKS * TILES * 128, 192)
    return up, down


def reduce_any_mesh(item):
    part = lax.psum_scatter(item, "seq", scatter_dimension=0, tiled=True)
    part = lax.psum_scatter(part.reshape(part.shape[1:]), "rows", scatter_dimension=0, tiled=True)
    return part.astype(F32)


def solution(mesh):
    split = P("rows", "seq", None)
    lines = P("rows", None)
    block = P("rows", "seq")
    in_specs = (split,) + (P(),) * 16 + (split, lines, lines, lines)
    out_specs = (split, split, P(), P(), block, P(), P(), P(), block, P(), P(), P(), P(), block, P(), block, P(), P())
    return jax.shard_map(on_device, mesh=mesh, in_specs=in_specs, out_specs=out_specs, check_vma=False)
```

```python
import functools
import math

import jax
import jax.numpy as jnp
from jax import lax
from jax.experimental import pallas as pl
from jax.experimental.pallas import tpu as pltpu
from jax.sharding import PartitionSpec as P

HEADS = 12
HEAD = 64
GRID = 24
SPAN = 2 * GRID - 1
SLOTS = 576
PADDED = 640
MODEL = 768
PAIRS = HEADS // 2
WIDE = 1152
STRIP = 128
BASE = 489
COMPACT = 32
LINES = 2304 // 128
IMGS = 4
EPS = 1e-06
NEGATIVE = -1e30
CHUNK = 96
PARTS = 4
BLOCKS = 8
TILES = 3
F32 = jnp.float32
BF16 = jnp.bfloat16
VMEM_LIMIT = 63 * 2**20
FIRST_GAIN, FIRST_SHIFT, QUERY_BIAS, VALUE_BIAS, OUTPUT_BIAS, ATTENTION_SCALE = range(6)
SECOND_GAIN, SECOND_SHIFT, DOWN_BIAS, FEED_SCALE, UP_BIAS = range(6, 11)


def dot(left, right):
    return lax.dot_general(left, right, (((1,), (0,)), ((), ())), preferred_element_type=F32)


def dot_nt(left, right):
    return lax.dot_general(left, right, (((1,), (1,)), ((), ())), preferred_element_type=F32)


def dot_tn(left, right):
    return lax.dot_general(left, right, (((0,), (0,)), ((), ())), preferred_element_type=F32)


def chunks(body):
    def step(index, carry):
        body(pl.ds(pl.multiple_of(index * CHUNK, CHUNK), CHUNK))
        return carry

    lax.fori_loop(0, SLOTS // CHUNK, step, 0)


def fold(value):
    return jnp.sum(value.reshape(value.shape[0] // 8, 8, value.shape[1]), 0)


def normal_of(values):
    center = values - jnp.mean(values, -1, keepdims=True)
    spread = lax.rsqrt(jnp.mean(center * center, -1, keepdims=True) + EPS)
    return center * spread, spread


def normal_back(change, normal, spread, gain):
    scaled = change * gain
    inner = (
        scaled
        - jnp.mean(scaled, -1, keepdims=True)
        - normal * jnp.mean(scaled * normal, -1, keepdims=True)
    )
    return inner * spread


def row_scalars(heights, widths, order, row):
    sizes, breadths, large = [], [], []
    for place in range(IMGS):
        picked = order[row, place]
        size, breadth = jnp.int32(0), jnp.int32(0)
        for image in range(IMGS):
            hit = picked == image
            size = size + jnp.where(hit, heights[row, image] * widths[row, image], 0)
            breadth = breadth + jnp.where(hit, widths[row, image], 0)
        sizes.append(size)
        breadths.append(breadth)
        large.append(jnp.where(picked == 0, 1, 0))
    begins = [jnp.int32(0)]
    for place in range(IMGS - 1):
        begins.append(begins[-1] + sizes[place])
    large_begin = sum(begins[p] * large[p] for p in range(IMGS))
    return dict(
        sizes=sizes,
        breadths=breadths,
        large=large,
        begins=begins,
        large_begin=large_begin,
        large_size=heights[row, 0] * widths[row, 0],
        large_width=widths[row, 0],
    )


def place_info(info, slot):
    segment = jnp.full(slot.shape, IMGS, jnp.int32)
    across = jnp.zeros(slot.shape, jnp.int32)
    down = jnp.zeros(slot.shape, jnp.int32)
    large = jnp.zeros(slot.shape, jnp.int32)
    for place in range(IMGS):
        offset = slot - info["begins"][place]
        inside = (offset >= 0) & (offset < info["sizes"][place])
        breadth = jnp.full(slot.shape, info["breadths"][place], jnp.int32)
        line = ((offset.astype(F32) + 0.5) / breadth.astype(F32)).astype(jnp.int32)
        segment = jnp.where(inside, place, segment)
        down = jnp.where(inside, line, down)
        across = jnp.where(inside, offset - line * breadth, across)
        large = jnp.where(inside, info["large"][place], large)
    return segment, down, across, large


def compact_index(info):
    found = []
    for axis in (0, 1):
        number = lax.broadcasted_iota(jnp.int32, (COMPACT, 128), axis)
        slot = number + jnp.where(number >= info["large_begin"], info["large_size"], 0)
        segment, down, across, large = place_info(info, slot)
        small = (segment < IMGS) & (large == 0) & (number < COMPACT)
        found.append((jnp.where(small, segment, -1 - axis), down, across))
    same = found[0][0] == found[1][0]
    row_step = found[0][1] - found[1][1] + 2
    column_step = found[0][2] - found[1][2] + 2
    return jnp.where(same, row_step * 5 + column_step, -1)


def shift_of(info, line):
    shift = BASE - (line - (GRID - 1)) * info["large_width"]
    return jnp.where(shift < 0, shift + WIDE, shift)


def flip():
    down = lax.broadcasted_iota(jnp.int32, (128, 128), 0)
    across = lax.broadcasted_iota(jnp.int32, (128, 128), 1)
    return jnp.where(down + across == 127, 1.0, 0.0).astype(BF16)


def line_place(line):
    start = LINES * 128 - SPAN - SPAN * line
    return start // 128, lax.rem(start, 128)


def prepare(info, table, flat, turned, columns, picks, query_codes, key_code, bands, near):
    flat[...] = jnp.zeros_like(flat)
    flat[0:HEADS, 0 : SPAN * SPAN] = table[...].astype(F32)
    turned[LINES] = jnp.zeros((16, 128), F32)
    for block in range(LINES):
        turned[LINES - 1 - block] = dot(flat[:, block * 128 : block * 128 + 128].astype(BF16), flip())
    for entry in range(25):
        at = (GRID - 3 + entry // 5) * SPAN + GRID - 3 + entry % 5
        columns[entry] = jnp.broadcast_to(flat[:, at : at + 1], (16, 128))

    def rows(index, carry):
        start = pl.multiple_of(index * 64, 64)
        slot = lax.broadcasted_iota(jnp.int32, (64, 128), 0) + start
        lane = lax.broadcasted_iota(jnp.int32, (64, 128), 1)
        segment, _, across, large = place_info(info, slot)
        rank = slot - jnp.where(slot >= info["large_begin"], info["large_size"], 0)
        small = (segment < IMGS) & (large == 0)
        target = jnp.where(small, rank, -1)
        pick = (lane == target) | (lane == segment + COMPACT)
        picks[pl.ds(start, 64), :] = jnp.where(pick, 1.0, 0.0).astype(BF16)
        code = across.astype(F32)
        query_codes[0, pl.ds(start, 64), :] = jnp.where(large == 1, code, -1e9)
        query_codes[1, pl.ds(start, 64), :] = jnp.where(large == 1, code, 1e9)
        return carry

    lax.fori_loop(0, SLOTS // 64, rows, 0)
    slot = lax.broadcasted_iota(jnp.int32, (8, PADDED), 1)
    key_code[...] = place_info(info, slot)[2].astype(F32)

    lanes = lax.broadcasted_iota(jnp.int32, (16, WIDE), 1)
    width = info["large_width"]

    def line_step(line, carry):
        low, high = carry
        shift = shift_of(info, line)
        block, lane = line_place(line)
        wide = jnp.concatenate([turned[block], turned[block + 1], jnp.zeros((16, WIDE - 256), F32)], 1)
        move = shift - lane
        rolled = pltpu.roll(wide, jnp.where(move < 0, move + WIDE, move), 1)
        entry = lanes - shift
        entry = jnp.where(entry < 0, entry + WIDE, entry)
        low = jnp.where((entry >= GRID - width) & (entry <= GRID - 1), rolled, low)
        high = jnp.where((entry >= GRID) & (entry <= GRID - 2 + width), rolled, high)
        return low, high

    zero = jnp.zeros((16, WIDE), F32)
    low, high = lax.fori_loop(0, SPAN, line_step, (zero, zero))
    for head in range(HEADS):
        bands[head, 0] = jnp.broadcast_to(low[head : head + 1], (8, WIDE))
        bands[head, 1] = jnp.broadcast_to(high[head : head + 1], (8, WIDE))

    index = compact_index(info)
    across = lax.broadcasted_iota(jnp.int32, (128 - COMPACT, 128), 1) - COMPACT
    down = lax.broadcasted_iota(jnp.int32, (128 - COMPACT, 128), 0)
    inside = (across >= 0) & (across <= IMGS) & (down <= IMGS)
    for head in range(HEADS):
        value = jnp.zeros((COMPACT, 128), F32)
        for entry in range(25):
            value = jnp.where(index == entry, columns[entry, head : head + 1, :], value)
        near[head, 0:COMPACT, :] = value.astype(BF16)
        own = jnp.where(down == IMGS, columns[12, head : head + 1, :], 0.0)
        lower = jnp.where(inside, jnp.where(across == down, own, NEGATIVE), 0.0)
        near[head, COMPACT:128, :] = lower.astype(BF16)


def project_in(tokens, vec, weight, first, query, keys, values, begin, count):
    gain, shift = vec[FIRST_GAIN : FIRST_GAIN + 1, :], vec[FIRST_SHIFT : FIRST_SHIFT + 1, :]

    def norm(index, carry):
        rows = pl.ds(pl.multiple_of(begin + index * CHUNK, CHUNK), CHUNK)
        normal, _ = normal_of(tokens[rows, :].astype(F32))
        first[rows, :] = (normal * gain + shift).astype(BF16)
        return carry

    lax.fori_loop(0, count // CHUNK, norm, 0)
    rows = pl.ds(pl.multiple_of(begin, CHUNK), count)
    step = 256
    for part, out in enumerate((query, keys, values)):
        for block in range(MODEL // step):
            lanes = slice(block * step, (block + 1) * step)
            columns = slice(part * MODEL + block * step, part * MODEL + (block + 1) * step)
            mixed = dot(first[rows, :], weight[:, columns])
            if part == 0:
                mixed = (mixed + vec[QUERY_BIAS : QUERY_BIAS + 1, lanes]) * HEAD**-0.5
            if part == 2:
                mixed = mixed + vec[VALUE_BIAS : VALUE_BIAS + 1, lanes]
            out[rows, lanes] = mixed.astype(BF16)


def half_mask(half):
    lane = lax.broadcasted_iota(jnp.int32, (SLOTS, 128), 1)
    return (lane < HEAD) if half == 0 else (lane >= HEAD)


def keep(mask, value):
    return jnp.where(mask, value, jnp.zeros_like(value))


def attend(query, keys, values, picks, query_codes, key_code, bands, near, chance_of, attended, inverse, strips, done):
    def pair_step(pair, carry):
        chance = chance_of(pair)
        lanes = pl.ds(pl.multiple_of(pair * 128, 128), 128)
        key_side = jnp.concatenate([keys[:, lanes], picks[...]], 1)
        totals = [None] * (SLOTS // 192)
        for half in range(2):
            head = pair * 2 + half
            mask = half_mask(half)
            near_side = dot(picks[...], near[head]).astype(BF16)
            query_side = jnp.concatenate([keep(mask, query[:, lanes]), near_side], 1)
            low_strip, high_strip = strips[half]
            for which, strip in enumerate((low_strip, high_strip)):
                band = jnp.concatenate([bands[head, which]] * (STRIP // 8), 0)
                strip[...] = pltpu.roll(band, 0, 1, stride=1, stride_axis=0)
            chance[half, :, SLOTS:] = jnp.zeros((SLOTS, PADDED - SLOTS), BF16)
            value_side = jnp.concatenate(
                [keep(mask, values[:, lanes]), keep(mask, jnp.ones((SLOTS, 128), BF16))], 1
            )
            for slab in range(SLOTS // 192):
                score = dot_nt(query_side[slab * 192 : slab * 192 + 192], key_side)
                weights = []
                for block in range(slab * 3, slab * 3 + 3):
                    rows = slice(block * 64, (block + 1) * 64)
                    strip_rows = slice(block % 2 * 64, block % 2 * 64 + 64)
                    start = 512 - block // 2 * 128
                    strip_lanes = slice(start, start + SLOTS)
                    code = key_code[0:1, 0:SLOTS]
                    low_hit = query_codes[0, rows, 0:1] >= code
                    high_hit = code > query_codes[1, rows, 0:1]
                    bias = jnp.where(
                        low_hit,
                        low_strip[strip_rows, strip_lanes],
                        jnp.where(high_hit, high_strip[strip_rows, strip_lanes], 0.0),
                    )
                    inside = (block - slab * 3) * 64
                    part = score[inside : inside + 64] + bias
                    top = jnp.max(part, -1, keepdims=True)
                    weight = jnp.exp(part - top).astype(BF16)
                    chance[half, rows, 0:SLOTS] = weight
                    weights.append(weight)
                added = dot(jnp.concatenate(weights, 0), value_side)
                totals[slab] = added if half == 0 else totals[slab] + added
        result = jnp.concatenate(totals, 0)
        scale = 1.0 / result[:, 128:]
        inverse[:, lanes] = scale
        attended[:, lanes] = result[:, :128] * scale
        done(pair)
        return carry

    lax.fori_loop(0, PAIRS, pair_step, 0)


def project_out(tokens, attended, weight, vec, branch, middle, second, attended_low):
    attended_low[...] = attended[...].astype(BF16)
    step = 256
    for block in range(MODEL // step):
        lanes = slice(block * step, (block + 1) * step)
        branch[:, lanes] = dot(attended_low[...], weight[:, lanes]) + vec[OUTPUT_BIAS : OUTPUT_BIAS + 1, lanes]
    scale = vec[ATTENTION_SCALE : ATTENTION_SCALE + 1, :]
    gain, shift = vec[SECOND_GAIN : SECOND_GAIN + 1, :], vec[SECOND_SHIFT : SECOND_SHIFT + 1, :]

    def norm(rows):
        value = tokens[rows, :].astype(F32) + scale * branch[rows, :]
        middle[rows, :] = value
        normal, _ = normal_of(value)
        second[rows, :] = (normal * gain + shift).astype(BF16)

    chunks(norm)


def gelu_parts(value):
    bell = jnp.exp2(value * value * (-0.5 * math.log2(math.e)))
    base = 1.0 + (0.3275911 / math.sqrt(2.0)) * jnp.abs(value)
    guess = pl.reciprocal(base, approx=True)
    inner = guess * (2.0 - base * guess)
    poly = 0.5 * 1.061405429
    for coefficient in (-1.453152027, 1.421413741, -0.284496736, 0.254829592):
        poly = poly * inner + 0.5 * coefficient
    tail = poly * inner * bell
    share = jnp.where(value >= 0.0, 1.0 - tail, tail)
    return value * share, share + value * bell * (1.0 / math.sqrt(2.0 * math.pi))


def feed(second, upstream, up, down, vec, second_change, unit, up_sum, feed_sums, outcome_change, outcome, active, slope, up_tile, down_tile, sems, before, after):
    def loads(tile):
        slot = tile % 2
        copies = []
        for block in range(BLOCKS):
            start = 3 * 128 * block + 128 * tile
            inside = slice(block * 128, block * 128 + 128)
            copies.append(
                pltpu.make_async_copy(
                    up.at[:, start : start + 128], up_tile.at[slot, :, inside], sems.at[slot, 0, block]
                )
            )
            copies.append(
                pltpu.make_async_copy(
                    down.at[start : start + 128], down_tile.at[slot, inside], sems.at[slot, 1, block]
                )
            )
        return copies

    for copy in loads(0):
        copy.start()
    feed_sums[...] = jnp.zeros_like(feed_sums)
    scale = vec[FEED_SCALE : FEED_SCALE + 1, :]

    def begin(rows):
        value = (upstream[rows, :].astype(F32) * scale).astype(BF16)
        outcome_change[rows, :] = value
        feed_sums[1] += fold(value.astype(F32))

    chunks(begin)
    for tile in range(TILES):
        slot = tile % 2
        if tile + 1 < TILES:
            for copy in loads(tile + 1):
                copy.start()
        for copy in loads(tile):
            copy.wait()
        for pair in range(BLOCKS // 2):
            wide = slice(pair * 256, pair * 256 + 256)
            line = slice(UP_BIAS + pair, UP_BIAS + pair + 1)
            ends = [slice(start + 128 * tile, start + 128 * tile + 128) for start in (0, 384)]
            bias = jnp.concatenate([vec[line, end] for end in ends], 1)
            for start in range(0, SLOTS, 192):
                rows = slice(start, start + 192)
                value, gradient = gelu_parts(dot(second[rows, :], up_tile[slot, :, wide]) + bias)
                active[rows, wide] = value.astype(BF16)
                back = dot_nt(outcome_change[rows, :], down_tile[slot, wide, :])
                slope[rows, wide] = (back * gradient).astype(BF16)
            before(tile, pair)
        for start in range(0, MODEL, 256):
            lanes = slice(start, start + 256)
            result = dot(active[...], down_tile[slot, :, lanes])
            back = dot_nt(slope[...], up_tile[slot, lanes, :])
            if tile == 0:
                outcome[:, lanes] = result
                second_change[:, lanes] = back
            else:
                outcome[:, lanes] += result
                second_change[:, lanes] += back
        total = dot(jnp.ones((8, SLOTS), BF16), slope[...])
        for block in range(BLOCKS):
            inside = slice(block * 128, block * 128 + 128)
            start = 3 * 128 * block + 128 * tile
            up_sum[:, start : start + 128] = total[:, inside]
        for pair in range(BLOCKS // 2):
            turned = dot_tn(second[...], slope[:, pair * 256 : pair * 256 + 256]).astype(BF16)
            unit[pair, :, :, 0:96, 0:256] = turned.reshape(4, 2, 96, 256)
        for pair in range(BLOCKS // 2):
            turned = dot_tn(outcome_change[...], active[:, pair * 256 : pair * 256 + 256]).astype(BF16)
            for side in range(2):
                inside = slice(side * 128, side * 128 + 128)
                for part in range(PARTS):
                    start = part * 192
                    unit[part, pair, side, 0:96, 256:384] = turned[start : start + 96, inside]
                    for third in range(3):
                        start = part * 192 + 96 + third * 32
                        unit[part, pair, side, 96:128, third * 128 : third * 128 + 128] = turned[start : start + 32, inside]
        after(tile)


def feed_end(upstream, middle, vec, output, outcome, feed_sums):
    scale, bias = vec[FEED_SCALE : FEED_SCALE + 1, :], vec[DOWN_BIAS : DOWN_BIAS + 1, :]

    def end(rows):
        value = outcome[rows, :] + bias
        output[rows, :] = (middle[rows, 0:MODEL] + scale * value).astype(BF16)
        feed_sums[0] += fold(upstream[rows, :].astype(F32) * value)

    chunks(end)


def pair_at(turn):
    late = turn // 4
    return (1 - late) * ((3 * turn + 1) // 2) + late * (3 * turn - 11)


def attend_back(query, keys, values, picks, query_codes, key_code, chance_of, change_low, attended, inverse, joined, band_sums, near_sums, score_changes, event, middle_event):
    for score_change in score_changes:
        score_change[:, SLOTS:] = jnp.zeros((SLOTS, PADDED - SLOTS), BF16)

    def pair_step(turn, carry):
        pair = pair_at(turn)
        event(turn)
        chance = chance_of(turn)
        lanes = pl.ds(pl.multiple_of(pair * 128, 128), 128)
        lane = lax.broadcasted_iota(jnp.int32, (SLOTS, 128), 1)
        own_change = change_low[:, lanes].astype(F32)
        scale = inverse[:, lanes]
        terms = own_change * attended[:, lanes]
        high = terms.astype(BF16)
        low = (terms - high.astype(F32)).astype(BF16)
        block_row = lax.broadcasted_iota(jnp.int32, (128, 128), 0) // HEAD
        block_lane = lax.broadcasted_iota(jnp.int32, (128, 128), 1) // HEAD
        block = jnp.where(block_row == block_lane, 1.0, 0.0).astype(BF16)
        delta = (dot(high, block) + dot(low, block)) * -scale
        delta_high = delta.astype(BF16)
        delta_low = (delta - delta_high.astype(F32)).astype(BF16)
        scaled = (own_change * scale).astype(BF16)
        value_side = jnp.concatenate([values[:, lanes], jnp.ones((SLOTS, 128), BF16)], 1)
        query_total = jnp.zeros((SLOTS, 128), F32)
        key_total = jnp.zeros((SLOTS, 128), F32)
        value_total = jnp.zeros((SLOTS, 128), F32)
        for half in range(2):
            if half == 1:
                middle_event(turn)
            head = pair * 2 + half
            mask = half_mask(half)
            extra = jnp.where(
                lane == half * HEAD,
                delta_high,
                jnp.where(lane == half * HEAD + 1, delta_low, jnp.zeros_like(delta_low)),
            )
            own_scaled = keep(mask, scaled)
            score_change = score_changes[half]
            change_side = jnp.concatenate([own_scaled, extra], 1)
            for start in range(0, SLOTS, 192):
                rows = slice(start, start + 192)
                weight_change = dot_nt(change_side[rows], value_side)
                value = chance[half, rows, 0:SLOTS].astype(F32) * weight_change
                score_change[rows, 0:SLOTS] = value.astype(BF16)
            kinds = [None, None]
            own_score = score_change[:, 0:SLOTS]
            key_side = jnp.concatenate([keep(mask, keys[:, lanes]), picks[...]], 1)
            both = dot(own_score, key_side)
            query_total = query_total + both[:, :128]
            near_sums[head] = dot_tn(picks[...], both[:, 128:].astype(BF16))
            key_total = key_total + dot_tn(own_score, keep(mask, query[:, lanes]))
            value_total = value_total + dot_tn(chance[half, :, 0:SLOTS], own_scaled)
            for group in range(STRIP // 16 - 1, -1, -1):
                tiles = [[jnp.zeros((16, 128), F32)] * (WIDE // 128) for _ in range(2)]
                for major in range(-(-SLOTS // STRIP)):
                    start = major * STRIP + group * 16
                    if start >= SLOTS:
                        continue
                    rows = slice(start, start + 16)
                    low_code = query_codes[0, rows, :]
                    high_code = query_codes[1, rows, :]
                    for column in range(PADDED // 128):
                        span = slice(column * 128, column * 128 + 128)
                        value = score_change[rows, span].astype(F32)
                        code = jnp.broadcast_to(key_code[0:1, span], (16, 128))
                        place = 4 - major + column
                        tiles[0][place] = tiles[0][place] + jnp.where(low_code >= code, value, 0.0)
                        tiles[1][place] = tiles[1][place] + jnp.where(code > high_code, value, 0.0)
                for which in range(2):
                    fresh = jnp.concatenate(tiles[which], 1)
                    if group == STRIP // 16 - 1:
                        kinds[which] = fresh
                    else:
                        kinds[which] = pltpu.roll(kinds[which], WIDE - 16, 1) + fresh
            for which in range(2):
                band_sums[head, which] = kinds[which][0:8] + pltpu.roll(kinds[which][8:16], WIDE - 8, 1)
        joined[0][:, lanes] = (query_total.astype(BF16).astype(F32) * HEAD**-0.5).astype(BF16)
        joined[1][:, lanes] = key_total.astype(BF16)
        joined[2][:, lanes] = value_total.astype(BF16)
        return carry

    lax.fori_loop(0, PAIRS, pair_step, 0)


def table_back(info, band_sums, near_sums, table_sum):
    kinds = []
    for which in range(2):
        total = jnp.zeros((16, WIDE), F32)
        for step in range(8):
            rows = jnp.concatenate(
                [band_sums[head, which, step : step + 1, :] for head in range(HEADS)]
                + [jnp.zeros((16 - HEADS, WIDE), F32)],
                0,
            )
            total = total + (rows if step == 0 else pltpu.roll(rows, WIDE - step, 1))
        kinds.append(total)
    low, high = kinds
    width = info["large_width"]
    entry = lax.broadcasted_iota(jnp.int32, (16, 128), 1)
    low_hit = (entry >= GRID - width) & (entry <= GRID - 1)
    high_hit = (entry >= GRID) & (entry <= GRID - 2 + width)

    table_sum[...] = jnp.zeros_like(table_sum)
    lane_wide = lax.broadcasted_iota(jnp.int32, (16, 256), 1)

    def line_step(line, carry):
        block, lane = line_place(line)
        back = WIDE - shift_of(info, line)
        low_part = pltpu.roll(low, back, 1)[:, :128]
        high_part = pltpu.roll(high, back, 1)[:, :128]
        part = jnp.where(low_hit, low_part, jnp.where(high_hit, high_part, 0.0))
        wide = pltpu.roll(jnp.concatenate([part, jnp.zeros((16, 128), F32)], 1), lane, 1)
        table_sum[block] += wide[:, :128]
        table_sum[block + 1] += wide[:, 128:]
        return carry

    lax.fori_loop(0, SPAN, line_step, 0)
    index = compact_index(info)
    head_row = lax.broadcasted_iota(jnp.int32, (16, 128), 0)
    centre = jnp.zeros((16, 128), F32)
    for head in range(HEADS):
        at = COMPACT + IMGS
        centre = jnp.where(head_row == head, near_sums[head, at : at + 1, :], centre)
    centre = jnp.sum(jnp.where(entry == COMPACT + IMGS, centre, 0.0), 1, keepdims=True)
    for number in range(25):
        hit = index == number
        column = jnp.zeros((16, 128), F32)
        for head in range(HEADS):
            part = jnp.sum(jnp.where(hit, near_sums[head, 0:COMPACT, :], 0.0), 0, keepdims=True)
            column = jnp.where(head_row == head, part, column)
        total = jnp.sum(column, 1, keepdims=True)
        if number == 12:
            total = total + centre
        at = LINES * 128 - 1 - (GRID - 3 + number // 5) * SPAN - (GRID - 3 + number % 5)
        table_sum[at // 128] += jnp.where(entry == at % 128, total, 0.0)


def remote(source, target, send, receive, device):
    return pltpu.make_async_remote_copy(
        src_ref=source,
        dst_ref=target,
        send_sem=send,
        recv_sem=receive,
        device_id=device,
        device_id_type=pl.DeviceIdType.MESH,
    )


def greet(devices):
    barrier = pltpu.get_barrier_semaphore()
    for device in devices:
        pl.semaphore_signal(barrier, inc=1, device_id=device, device_id_type=pl.DeviceIdType.MESH)
    pl.semaphore_wait(barrier, len(devices))


def group_peers(parts):
    row, me = lax.axis_index("rows"), lax.axis_index("seq")
    near = 1 - 2 * (me % 2)
    far = 2 - 4 * (me // 2)
    return row, me, [me + near, me + far, me + near + far]


def block_of(index, size):
    return pl.ds(pl.multiple_of(index * size, size), size)


def forward_kernel(heights, widths, order, table, *refs):
    rows_of, refs = refs[:11], refs[11:]
    forward_body(heights, widths, order, table, rows_of, *refs)


def stack_rows(rows_of, vec):
    vec[...] = jnp.zeros_like(vec)
    line = 0
    for item in rows_of:
        for start in range(0, item.shape[0], 128):
            where = start // MODEL + line
            lanes = slice(start % MODEL, start % MODEL + 128)
            vec[where : where + 1, lanes] = item[start : start + 128].astype(F32).reshape(1, 128)
        line += item.shape[0] // MODEL


def forward_body(heights, widths, order, table, rows_of, input_weight, output_weight, own_tokens, own_upstream, *rest):
    (tokens_far, upstream, first_far, query_far, keys_far, values_far, chance_far, attended_far, inverse_far, branch_far, middle_far, attended_low_far, second, picks, query_codes, key_code, vec), rest = rest[:17], rest[17:]
    (tokens, first, query, keys, values, attended, inverse, branch, middle, attended_low, chance, bands, near, low_strip, high_strip, other_low, other_high, flat, turned, columns, store_sems, chance_sems, send, receive, local) = rest
    parts, slots = own_tokens.shape[0], own_tokens.shape[1]
    row, me, peers = group_peers(parts)
    greet([(row, peer) for peer in peers])

    def exchange(which, source, target):
        mine = block_of(me, slots)
        copies = [
            remote(source.at[peer], target.at[mine], send.at[which, step], receive.at[which, step], (row, peer))
            for step, peer in enumerate(peers)
        ]
        return copies + [pltpu.make_async_copy(source.at[me], target.at[mine], local.at[which])]

    token_copies = exchange(0, own_tokens, tokens)
    upstream_copies = exchange(1, own_upstream, upstream)
    stores = {
        number: pltpu.make_async_copy(source, target, store_sems.at[number])
        for number, (source, target) in enumerate(
            (
                (tokens, tokens_far),
                (first, first_far),
                (query, query_far),
                (keys, keys_far),
                (values, values_far),
                (attended, attended_far),
                (inverse, inverse_far),
                (attended_low, attended_low_far),
                (branch, branch_far),
                (middle, middle_far),
            )
        )
    }
    for copy in token_copies:
        copy.start()
    stack_rows(rows_of, vec)
    info = row_scalars(heights, widths, order, me)
    prepare(info, table, flat, turned, columns, picks, query_codes, key_code, bands, near)
    half = SLOTS // 2
    own_half = me // 2
    token_copies[0].wait()
    token_copies[3].wait()
    project_in(tokens, vec, input_weight, first, query, keys, values, own_half * half, half)
    token_copies[1].wait()
    token_copies[2].wait()
    for copy in upstream_copies:
        copy.start()
    stores[0].start()
    project_in(tokens, vec, input_weight, first, query, keys, values, (1 - own_half) * half, half)
    for number in range(1, 5):
        stores[number].start()

    def chance_copy(pair):
        slot = lax.rem(pair, 2)
        return pltpu.make_async_copy(chance.at[slot], chance_far.at[pl.ds(pair * 2, 2)], chance_sems.at[slot])

    def chance_of(pair):
        @pl.when(pair >= 2)
        def _():
            chance_copy(pair - 2).wait()

        return chance.at[lax.rem(pair, 2)]

    attend(query, keys, values, picks, query_codes, key_code, bands, near, chance_of, attended, inverse, ((low_strip, high_strip), (other_low, other_high)), lambda pair: chance_copy(pair).start())
    for number in (5, 6):
        stores[number].start()
    project_out(tokens, attended, output_weight, vec, branch, middle, second, attended_low)
    for number in (7, 8, 9):
        stores[number].start()
    for pair in (PAIRS - 2, PAIRS - 1):
        chance_copy(jnp.int32(pair)).wait()
    for number in stores:
        stores[number].wait()
    for copy in upstream_copies:
        copy.wait()


UNITS = ((128, 384), (128, 384), (128, 384), (144, 384), (48, 384))
LATE = (
    (((0, 0, 128), (0, 256, 384), (0, 384, 512)), ((0, 640, 768), (1, 0, 128), (1, 256, 384)), ((1, 384, 512), (1, 640, 768), (2, 0, 128)), ((2, 256, 384), (2, 384, 512), (2, 640, 768))),
    (((0, 128, 256), (0, 512, 576)), ((1, 128, 256), (0, 576, 640)), ((1, 512, 640), (2, 128, 192)), ((2, 512, 640), (2, 192, 256))),
)


SPLITS = (64, 64, 64, 64, 32)
PLAN = {
    ("slab", 1, 3): (("first", 0),),
    ("slab", 2, 3): (("first", 1),),
    "norm": (("first", 2),),
    ("middle", 0): (("second_y", 1),),
    ("pair", 2): (("second_x", 1),),
    ("middle", 2): (("second_x", 0),),
    ("pair", 3): (("second_y", 0),),
    ("pair", 4): (("second_x", 2),),
    ("middle", 4): (("second_y", 2), ("third", 1),),
    ("pair", 5): (("first", 3), ("third", 0),),
    ("middle", 5): (("third", 2),),
    "late": (("first", 4), ("second_y", 3), ("second_x", 3),),
    "given": (("second_y", 4), ("second_x", 4), ("third", 3),),
    ("small", 0): (("fourth", 0),),
    ("small", 1): (("third", 4),),
    ("small", 2): (("fourth", 2),),
    "end": (("fourth", 1), ("fourth", 3), ("fourth", 4),),
}


class Reduction:
    def __init__(self, sources, results, owns, core_in, x_in, y_in, late, line_in, send, receive, local):
        self.sources, self.results, self.owns = sources, results, owns
        self.core_in, self.x_in, self.y_in, self.late, self.line_in = core_in, x_in, y_in, late, line_in
        self.send, self.receive, self.local = send, receive, local
        rows, seq = lax.axis_index("rows"), lax.axis_index("seq")
        self.z, self.x, self.y, self.core = rows // 2, rows % 2, seq // 2, seq % 2
        z, x, y, core = self.z, self.x, self.y, self.core
        self.core_peer = (rows, y * 2 + 1 - core)
        self.x_peer = (z * 2 + 1 - x, seq)
        self.y_peer = (rows, (1 - y) * 2 + core)
        self.diagonal = (z * 2 + 1 - x, (1 - y) * 2 + core)
        self.z_peers = [(lax.rem(z + step, 4) * 2 + x, seq) for step in range(1, 4)]

    def cut(self, unit):
        return SPLITS[unit]

    def go(self, place):
        for name, unit in PLAN.get(place, ()):
            getattr(self, name)(unit)

    def peers(self):
        return [self.core_peer, self.x_peer, self.y_peer, self.diagonal] + self.z_peers

    def copy(self, unit, number, source, target, peer):
        return remote(source, target, self.send.at[unit, number], self.receive.at[unit, number], peer)

    def core_copies(self, unit):
        return [
            self.copy(unit, part, self.sources[unit].at[part * 2 + 1 - self.core], self.core_in[unit].at[part], self.core_peer)
            for part in range(2)
        ]

    def own_copies(self, unit):
        if self.owns[unit] is None:
            return []
        return [
            pltpu.make_async_copy(self.sources[unit].at[part * 2 + self.core], self.owns[unit].at[part], self.local.at[unit, part])
            for part in range(2)
        ]

    def x_copy(self, unit):
        return self.copy(unit, 2, self.core_in[unit].at[:, :, 1 - self.x, 0 : self.cut(unit)], self.x_in[unit], self.x_peer)

    def y_copy(self, unit):
        return self.copy(unit, 3, self.core_in[unit].at[1 - self.y, :, :, self.cut(unit) :], self.y_in[unit], self.y_peer)

    def again_y(self, unit):
        return self.copy(unit, 4, self.x_in[unit].at[1 - self.y], self.late[unit].at[:, 0 : self.cut(unit)], self.y_peer)

    def again_x(self, unit):
        return self.copy(unit, 5, self.y_in[unit].at[:, 1 - self.x], self.late[unit].at[:, self.cut(unit) :], self.x_peer)

    def line_copies(self, unit):
        return [
            self.copy(unit, 6 + step, self.late[unit].at[lax.rem(self.z + step + 1, 4)], self.line_in[unit].at[step], peer)
            for step, peer in enumerate(self.z_peers)
        ]

    def begin(self, unit):
        for copy in self.core_copies(unit):
            copy.start()

    def fetch(self, unit):
        for copy in self.own_copies(unit):
            copy.start()

    def first(self, unit):
        for copy in self.core_copies(unit) + self.own_copies(unit):
            copy.wait()
        held, own = self.core_in[unit], self.owns[unit]

        def add(line, carry):
            for part in range(2):
                for side in range(2):
                    if own is None:
                        term = self.sources[unit][part * 2 + self.core, line, side]
                    else:
                        term = own[part, line, side]
                    held[part, line, side] = held[part, line, side] + term
            return carry

        lax.fori_loop(0, 4, add, 0)
        self.x_copy(unit).start()
        self.y_copy(unit).start()

    def second_x(self, unit):
        x_in, held = self.x_in[unit], self.core_in[unit]
        self.x_copy(unit).wait()

        def add_x(line, carry):
            for part in range(2):
                x_in[part, line] = x_in[part, line] + held[part, line, self.x, 0 : self.cut(unit)]
            return carry

        lax.fori_loop(0, 4, add_x, 0)
        self.again_y(unit).start()

    def second_y(self, unit):
        y_in, held = self.y_in[unit], self.core_in[unit]
        self.y_copy(unit).wait()

        def add_y(line, carry):
            for side in range(2):
                y_in[line, side] = y_in[line, side] + held[self.y, line, side, self.cut(unit) :]
            return carry

        lax.fori_loop(0, 4, add_y, 0)
        self.again_x(unit).start()

    def third(self, unit):
        late, x_in, y_in = self.late[unit], self.x_in[unit], self.y_in[unit]
        self.again_y(unit).wait()
        self.again_x(unit).wait()

        def add(line, carry):
            late[line, 0 : self.cut(unit)] = late[line, 0 : self.cut(unit)] + x_in[self.y, line]
            late[line, self.cut(unit) :] = late[line, self.cut(unit) :] + y_in[line, self.x]
            return carry

        lax.fori_loop(0, 4, add, 0)
        for copy in self.line_copies(unit):
            copy.start()

    def fourth(self, unit):
        for copy in self.line_copies(unit):
            copy.wait()
        total = self.late[unit][self.z].astype(F32)
        for step in range(3):
            total = total + self.line_in[unit][step].astype(F32)
        self.results[unit](total)


class SmallSum:
    def __init__(self, link, small, out, plane_in, line_in, part, send, receive):
        self.link, self.small, self.out = link, small, out
        self.plane_in, self.line_in, self.part = plane_in, line_in, part
        self.send, self.receive = send, receive
        self.mine = self.place(link.core, link.x, link.y)
        self.plane_peers = []
        for flips in range(1, 8):
            core = 1 - link.core if flips & 4 else link.core
            x = 1 - link.x if flips & 2 else link.x
            y = 1 - link.y if flips & 1 else link.y
            self.plane_peers.append(((link.z * 2 + x, y * 2 + core), self.place(core, x, y)))

    def place(self, core, x, y):
        return core * 4 + x * 2 + y

    def copy(self, number, source, target, peer):
        return remote(source, target, self.send.at[number], self.receive.at[number], peer)

    def plane_copies(self):
        return [
            self.copy(step, self.small.at[index], self.plane_in.at[step], peer)
            for step, (peer, index) in enumerate(self.plane_peers)
        ]

    def line_copies(self):
        return [self.copy(7 + step, self.part, self.line_in.at[step], peer) for step, peer in enumerate(self.link.z_peers)]

    def plane_back(self):
        mine = self.out.at[self.mine]
        return [self.copy(10 + step, mine, mine, peer) for step, (peer, _) in enumerate(self.plane_peers)]

    def steps(self):
        def one():
            for copy in self.plane_copies():
                copy.start()

        def two():
            for copy in self.plane_copies():
                copy.wait()
            total = self.small[self.mine]
            for step in range(7):
                total = total + self.plane_in[step]
            self.part[...] = total
            for copy in self.line_copies():
                copy.start()

        def three():
            for copy in self.line_copies():
                copy.wait()
            self.out[self.mine] = self.part[...] + self.line_in[0] + self.line_in[1] + self.line_in[2]
            for copy in self.plane_back():
                copy.start()

        def four():
            for copy in self.plane_back():
                copy.wait()

        return [one, two, three, four]


def pack_small(table_sum, sums, feed_sums, up_sum, vectors, small):
    for block in range(LINES):
        small[block // 3, block % 3] = table_sum[block]
    vectors[...] = jnp.zeros_like(vectors)
    for number in range(8):
        vectors[number : number + 1, :] = jnp.sum(sums[number], 0, keepdims=True)
    for number in range(2):
        vectors[8 + number : 9 + number, :] = jnp.sum(feed_sums[number], 0, keepdims=True)
    for number in range(PARTS):
        vectors[10 + number : 11 + number, :] = up_sum[0:1, number * MODEL : (number + 1) * MODEL]
    for number in range(6):
        block = LINES + number
        small[block // 3, block % 3] = vectors[:, number * 128 : (number + 1) * 128]


def backward_kernel(paired, heights, widths, order, vec, upstream, second, picks, query_codes, key_code, output_weight, up_far, down_far, weight_far, tokens_far, first_far, query_far, keys_far, values_far, attended_far, inverse_far, branch_far, middle_far, attended_low_far, chance_far, *rest):
    if paired:
        (own_output, own_gradient, up_result, down_result), late_results, small_out, rest = rest[:4], rest[4:7], rest[7], rest[8:]
    else:
        (own_output, own_gradient, feed_units), late_outs, small_out, rest = rest[:3], rest[3:5], rest[5], rest[6:]
    (hidden, change, active, slope, outcome_change, outcome, second_change, branch_change, change_low, attended_low, output, query, keys, values, first, up_tile, down_tile, chance, score_change, other_change, band_sums, near_sums, table_sum, sums, feed_sums, up_sum, vectors, unit, small), rest = rest[:29], rest[29:]
    (tile_sems, load_sems, chance_sems, send, receive, local), rest = rest[:6], rest[6:]
    parts, slots = own_output.shape[0], own_output.shape[1]
    row, me, peers = group_peers(parts)
    feed_unit = unit.at[:, :, :, 0:128, :]
    if paired:
        count = len(UNITS)
        stages = [rest[i * count : (i + 1) * count] for i in range(5)]
        rest = rest[5 * count :]
        sources = [feed_unit] * TILES + [unit, unit.at[:, :, :, 0:48, :]]

        def feed_result(tile):
            def put(total):
                for half in range(2):
                    columns = slice(half * 384 + tile * 128, half * 384 + tile * 128 + 128)
                    up_result[:, columns] = total[0:96, half * 128 : half * 128 + 128]
                columns = slice(tile * 128, tile * 128 + 128)
                down_result[0:96, columns] = total[0:96, 256:384]
                for third in range(3):
                    lines = slice(96 + third * 32, 128 + third * 32)
                    down_result[lines, columns] = total[96:128, third * 128 : third * 128 + 128]

            return put

        def first_put(total):
            late_results[0][...] = total[0:96]
            for half in range(2):
                late_results[2][half * 48 : half * 48 + 48, :] = total[96:144, half * 192 : half * 192 + 192]

        def second_put(total):
            for half in range(2):
                late_results[1][half * 48 : half * 48 + 48, :] = total[:, half * 192 : half * 192 + 192]

        results = [feed_result(tile) for tile in range(TILES)] + [first_put, second_put]
        link = Reduction(sources, results, [None] * count, *stages, *rest[:2], None)
        small_sum = SmallSum(link, small, small_out, *rest[2:])
        greet([peer for peer, _ in small_sum.plane_peers] + link.z_peers)
    else:
        greet([(row, peer) for peer in peers])

    def give_back(which, source, target):
        copies = [
            remote(source.at[block_of(peer, slots)], target.at[me], send.at[which, step], receive.at[which, step], (row, peer))
            for step, peer in enumerate(peers)
        ]
        return copies + [pltpu.make_async_copy(source.at[block_of(me, slots)], target.at[me], local.at[which])]

    gradient = change_low
    output_copies = give_back(0, output, own_output)
    gradient_copies = give_back(1, gradient, own_gradient)
    wide = slice(0, MODEL)

    def load(number, source, target):
        return pltpu.make_async_copy(source, target, load_sems.at[number])

    load_query = load(0, query_far, query)
    load_keys = load(1, keys_far, keys)
    load_values = load(2, values_far, values)
    load_first = load(3, first_far, first)
    load_low = load(4, attended_low_far, attended_low)
    load_middle = load(5, middle_far, change.at[:, wide])
    load_branch = load(6, branch_far, hidden.at[:, wide])
    load_attended = load(7, attended_far, hidden.at[:, wide])
    load_inverse = load(8, inverse_far, change.at[:, wide])
    load_tokens = load(9, tokens_far, query)
    in_weights = (up_tile.at[0, :, wide], up_tile.at[1, :, wide], down_tile.at[0, wide, :])
    load_weights = [
        load(10 + number, weight_far.at[:, number * MODEL : (number + 1) * MODEL], target)
        for number, target in enumerate(in_weights)
    ]

    def chance_copy(turn):
        slot = lax.rem(turn, 2)
        return pltpu.make_async_copy(chance_far.at[pl.ds(pair_at(turn) * 2, 2)], chance.at[slot], chance_sems.at[slot])

    for copy in (load_query, load_keys, load_values, load_first, load_low):
        copy.start()
    chance_copy(jnp.int32(0)).start()

    def before(tile, pair):
        if tile == TILES - 1 and pair == 3:
            load_middle.start()
            load_branch.start()
        if paired:
            link.go(("slab", tile, pair))

    def after(tile):
        if paired:
            link.begin(tile)
        else:
            copy = load(13, feed_unit, feed_units.at[tile])
            copy.start()
            copy.wait()

    feed(second, upstream, up_far, down_far, vec, second_change, feed_unit, up_sum, feed_sums, outcome_change, outcome, active, slope, up_tile, down_tile, tile_sems, before, after)
    for copy in load_weights:
        copy.start()
    load_middle.wait()
    feed_end(upstream, change, vec, output, outcome, feed_sums)
    for copy in output_copies:
        copy.start()
    load_branch.wait()
    info = row_scalars(heights, widths, order, me)
    sums[...] = jnp.zeros_like(sums)
    middle_change = outcome
    gain, scale = vec[SECOND_GAIN : SECOND_GAIN + 1, :], vec[ATTENTION_SCALE : ATTENTION_SCALE + 1, :]

    def norm(rows):
        normal, spread = normal_of(change[rows, wide])
        back = second_change[rows, :]
        sums[6] += fold(back * normal)
        sums[7] += fold(back)
        value = upstream[rows, :].astype(F32) + normal_back(back, normal, spread, gain)
        middle_change[rows, :] = value
        sums[5] += fold(value * hidden[rows, wide])
        low = (value * scale).astype(BF16)
        branch_change[rows, :] = low
        sums[4] += fold(low.astype(F32))

    chunks(norm)
    load_attended.start()
    load_inverse.start()
    change_low[...] = dot_nt(branch_change[...], output_weight[...]).astype(BF16)
    if paired:
        link.go("norm")
    for copy in (load_query, load_keys, load_values, load_attended, load_inverse):
        copy.wait()

    joined = (active, slope, outcome_change)

    def packed(value):
        value = value.astype(BF16).reshape(4, 2, 2, 48, 192)
        return jnp.concatenate([value[:, :, 0], value[:, :, 1]], -1)

    def late_parts(number):
        for part in range(PARTS):
            pieces = [joined[which][:, low:high] for which, low, high in LATE[number][part]]
            value = dot_tn(first[...], jnp.concatenate(pieces, 1))
            if number == 1:
                unit[part, :, :, 0:48, 0:384] = packed(value)
            else:
                unit[part, :, :, 0:96, 0:384] = value.astype(BF16).reshape(4, 2, 96, 384)
                piece = branch_change[:, part * 192 : part * 192 + 192]
                unit[part, :, :, 96:144, 0:384] = packed(dot_tn(attended_low[...], piece))
        if paired:
            link.begin(TILES + number)
        else:
            source = unit if number == 0 else unit.at[:, :, :, 0:48, :]
            copy = load(13, source, late_outs[number])
            copy.start()
            copy.wait()

    def at_turn(name, turn):
        for number in range(PAIRS):
            if paired and (name, number) in PLAN:

                @pl.when(turn == number)
                def _(number=number):
                    link.go((name, number))

    def event(turn):
        @pl.when(turn + 1 < PAIRS)
        def _():
            chance_copy(turn + 1).start()

        chance_copy(turn).wait()

        @pl.when(turn == 4)
        def _():
            load_first.wait()
            load_low.wait()
            late_parts(0)

        at_turn("pair", turn)

    def middle_event(turn):
        at_turn("middle", turn)

    attend_back(query, keys, values, picks, query_codes, key_code, lambda turn: chance.at[lax.rem(turn, 2)], change_low, hidden, change, joined, band_sums, near_sums, (score_change, other_change), event, middle_event)
    load_tokens.start()
    late_parts(1)
    if paired:
        link.go("late")
    for copy in load_weights:
        copy.wait()
    first_change = hidden
    for start in range(0, MODEL, 256):
        lanes = slice(start, start + 256)
        total = dot_nt(joined[0][:, wide], in_weights[0][lanes, :])
        total = total + dot_nt(joined[1][:, wide], in_weights[1][lanes, :])
        first_change[:, lanes] = total + dot_nt(joined[2][...], in_weights[2][lanes, :])
    load_tokens.wait()
    gain_first = vec[FIRST_GAIN : FIRST_GAIN + 1, :]
    if paired:
        link.go("products")

    def norm_first(rows):
        normal, spread = normal_of(query[rows, :].astype(F32))
        back = first_change[rows, wide]
        sums[0] += fold(back * normal)
        sums[1] += fold(back)
        sums[2] += fold(joined[0][rows, wide].astype(F32))
        sums[3] += fold(joined[2][rows, :].astype(F32))
        value = middle_change[rows, :] + normal_back(back, normal, spread, gain_first)
        gradient[rows, :] = value.astype(BF16)

    chunks(norm_first)
    for copy in gradient_copies:
        copy.start()
    if paired:
        link.go("given")
    table_back(info, band_sums, near_sums, table_sum)
    pack_small(table_sum, sums, feed_sums, up_sum, vectors, small)
    if paired:
        link.go("tabled")
        for number, step in enumerate(small_sum.steps()):
            step()
            link.go(("small", number))
        link.go("end")
    else:
        small_out[...] = small[...]
    for copy in output_copies + gradient_copies:
        copy.wait()


def whole():
    return pl.BlockSpec(memory_space=pltpu.VMEM)


def far():
    return pl.BlockSpec(memory_space=pl.ANY)


def scalars():
    return pl.BlockSpec(memory_space=pltpu.SMEM)


def shape(*dims, dtype=F32):
    return jax.ShapeDtypeStruct(dims, dtype)


def on_device(layer_input, first_gain, first_shift, input_weight, query_bias, value_bias, bias_table, output_weight, output_bias, attention_scale, second_gain, second_shift, up_weight, up_bias, down_weight, down_bias, feed_scale, upstream, grid_heights, grid_widths, packing_order):
    parts = lax.axis_size("seq")
    paired = (lax.axis_size("rows"), parts) == (8, 4)
    slots = layer_input.shape[1]
    hidden_units = up_weight.shape[1]

    rows_of = [first_gain, first_shift, query_bias, value_bias, output_bias, attention_scale, second_gain, second_shift, down_bias, feed_scale, up_bias]
    full = (SLOTS, MODEL)
    low_full, wide_full = shape(*full, dtype=BF16), shape(*full)
    dma = pltpu.SemaphoreType.DMA
    vmem = pltpu.VMEM
    exchange_sems = [dma((2, parts - 1)), dma((2, parts - 1)), dma((2,))]
    (tokens, own_upstream, first, query, keys, values, chance, attended, inverse, branch, middle, attended_low, second, picks, query_codes, key_code, vec) = pl.pallas_call(
        forward_kernel,
        out_shape=[low_full] * 6
        + [shape(HEADS, SLOTS, PADDED, dtype=BF16)]
        + [wide_full] * 4
        + [low_full] * 2
        + [shape(SLOTS, 128, dtype=BF16), shape(2, SLOTS, 128), shape(8, PADDED), shape(16, MODEL)],
        in_specs=[scalars()] * 3 + [whole()] * 14 + [far()] * 2,
        out_specs=[far()] * 12 + [whole()] * 5,
        scratch_shapes=[vmem(full, BF16)] * 5
        + [vmem(full, F32)] * 4
        + [
            vmem(full, BF16),
            vmem((2, 2, SLOTS, PADDED), BF16),
            vmem((HEADS, 2, 8, WIDE), F32),
            vmem((HEADS, 128, 128), BF16),
            vmem((STRIP, WIDE), F32),
            vmem((STRIP, WIDE), F32),
            vmem((STRIP, WIDE), F32),
            vmem((STRIP, WIDE), F32),
            vmem((16, LINES * 128), F32),
            vmem((LINES + 1, 16, 128), F32),
            vmem((25, 16, 128), F32),
            dma((10,)),
            dma((2,)),
        ]
        + exchange_sems,
        compiler_params=pltpu.CompilerParams(collective_id=0, has_side_effects=True, vmem_limit_bytes=VMEM_LIMIT),
        name="forward",
    )(
        grid_heights, grid_widths, packing_order, bias_table.T, *rows_of, input_weight, output_weight,
        layer_input, upstream,
    )

    outs = [(shape(parts, slots, MODEL, dtype=BF16), far())] * 2
    unit_shape, small_shape = (4, 4, 2, 144, 384), (8, 3, 16, 128)
    scratch = [
        vmem(full, F32),
        vmem(full, F32),
        vmem((SLOTS, 1024), BF16),
        vmem((SLOTS, 1024), BF16),
        vmem(full, BF16),
        vmem(full, F32),
        vmem(full, F32),
    ]
    scratch += [vmem(full, BF16)] * 8
    scratch += [
        vmem((2, MODEL, 1024), BF16),
        vmem((2, 1024, MODEL), BF16),
        vmem((2, 2, SLOTS, PADDED), BF16),
        vmem((SLOTS, PADDED), BF16),
        vmem((SLOTS, PADDED), BF16),
        vmem((HEADS, 2, 8, WIDE), F32),
        vmem((HEADS, 128, 128), F32),
        vmem((LINES + 1, 16, 128), F32),
        vmem((8, 8, MODEL), F32),
        vmem((2, 8, MODEL), F32),
        vmem((8, hidden_units), F32),
        vmem((16, MODEL), F32),
        vmem(unit_shape, BF16),
        vmem(small_shape, F32),
        dma((2, 2, BLOCKS)),
        dma((14,)),
        dma((2,)),
    ] + exchange_sems
    if paired:
        outs += [
            (shape(96, 768), whole()),
            (shape(192, 384), whole()),
            (shape(96, 384), whole()),
            (shape(96, 192), whole()),
            (shape(96, 192), whole()),
            (shape(*small_shape), whole()),
        ]
        for dims in (
            lambda r, c, cut: (2, 4, 2, r, c),
            lambda r, c, cut: (2, 4, cut, c),
            lambda r, c, cut: (4, 2, r - cut, c),
            lambda r, c, cut: (4, r, c),
            lambda r, c, cut: (3, r, c),
        ):
            scratch += [vmem(dims(*item, cut), BF16) for item, cut in zip(UNITS, SPLITS)]
        count = len(UNITS)
        scratch += [dma((count, 9)), dma((count, 9))]
        scratch += [
            vmem((7, 3, 16, 128), F32),
            vmem((3, 3, 16, 128), F32),
            vmem((3, 16, 128), F32),
            dma((17,)),
            dma((17,)),
        ]
    else:
        outs += [
            (shape(TILES, 4, 4, 2, 128, 384, dtype=BF16), far()),
            (shape(4, 4, 2, 144, 384, dtype=BF16), far()),
            (shape(4, 4, 2, 48, 384, dtype=BF16), far()),
            (shape(*small_shape), whole()),
        ]
    results = pl.pallas_call(
        functools.partial(backward_kernel, paired),
        out_shape=[item[0] for item in outs],
        in_specs=[scalars()] * 3 + [whole()] * 7 + [far()] * 14,
        out_specs=[item[1] for item in outs],
        scratch_shapes=scratch,
        compiler_params=pltpu.CompilerParams(collective_id=1, has_side_effects=True, vmem_limit_bytes=VMEM_LIMIT),
        name="backward",
    )(
        grid_heights, grid_widths, packing_order, vec, own_upstream, second, picks, query_codes, key_code, output_weight,
        up_weight, down_weight, input_weight, tokens, first, query, keys, values, attended, inverse, branch, middle,
        attended_low, chance,
    )
    own_output, own_gradient = results[:2]
    if paired:
        up_result, down_result, late_first, late_second, output_part, small = results[2:]
    else:
        feed_units, late_first, late_second, small = results[2:]
        up_unit, down_unit = restore_feed(feed_units)
        up_result, down_result = reduce_any_mesh(up_unit), reduce_any_mesh(down_unit)
        packed = jnp.concatenate([late_first[:, :, :, 96:144], late_second], 4).reshape(PARTS, BLOCKS, 48, 2, 2, 192)
        packed = jnp.transpose(packed, (3, 0, 1, 4, 2, 5)).reshape(2, PARTS, MODEL, 192)
        output_part, late_second = reduce_any_mesh(packed[0]), reduce_any_mesh(packed[1])
        late_first = reduce_any_mesh(late_first[:, :, :, 0:96].reshape(PARTS, MODEL, 384))
        small = lax.psum(small, ("rows", "seq"))
    lines = late_first.shape[0]
    done = pl.pallas_call(
        finish_kernel,
        out_shape=[
            shape(parts, slots, MODEL, dtype=BF16),
            shape(parts, slots, MODEL),
            shape(lines, 576),
            shape(lines, 192),
            shape(HEADS, SPAN * SPAN),
        ]
        + [shape(MODEL)] * 10
        + [shape(hidden_units)],
        in_specs=[whole()] * 6,
        out_specs=[whole()] * 16,
        scratch_shapes=[vmem((16, LINES * 128), F32)],
        compiler_params=pltpu.CompilerParams(vmem_limit_bytes=VMEM_LIMIT),
        name="finish",
    )(own_output, own_gradient, late_first, late_second, output_part, small.reshape(24, 16, 128))
    own_output, own_gradient, input_result, output_result, table = done[:5]
    vectors = done[5:]
    return (
        own_output,
        own_gradient,
        vectors[0],
        vectors[1],
        input_result,
        vectors[2],
        vectors[3],
        table.T,
        output_result,
        vectors[4],
        vectors[5],
        vectors[6],
        vectors[7],
        up_result,
        vectors[10],
        down_result if down_result.shape[1] == 192 else down_result.T,
        vectors[9],
        vectors[8],
    )


def finish_kernel(output_in, gradient_in, late_first, late_second, output_part, small, output, gradient, input_result, output_result, table, *rest):
    vectors, flat = rest[:-1], rest[-1]
    output[...] = output_in[...]
    for part in range(gradient.shape[0]):
        gradient[part] = gradient_in[part].astype(F32)
    first, second = late_first[...], late_second[...]
    pieces = [first[:, 0:128], first[:, 128:256], first[:, 256:384], second[:, 0:128], second[:, 128:192]]
    even = jnp.concatenate([pieces[0], pieces[3], pieces[1], pieces[2], pieces[4]], 1)
    odd = jnp.concatenate([pieces[4], pieces[0], pieces[1], pieces[3], pieces[2]], 1)
    side = jnp.full(even.shape, lax.rem(lax.axis_index("seq"), 2), jnp.int32)
    input_result[...] = jnp.where(side == 0, even, odd)
    output_result[...] = output_part[...]
    mirror = flip()
    for block in range(LINES):
        rest = small[block]
        total = jnp.zeros((16, 128), F32)
        for _ in range(3):
            low = rest.astype(BF16)
            total = total + dot(low, mirror)
            rest = rest - low.astype(F32)
        lanes = slice((LINES - 1 - block) * 128, (LINES - block) * 128)
        flat[:, lanes] = total
    table[...] = flat[0:HEADS, 0 : SPAN * SPAN]
    for number in range(14):
        target, start = vectors[min(number, 10)], max(number - 10, 0) * MODEL
        for block in range(6):
            row = small[LINES + block, number : number + 1, :]
            target[start + block * 128 : start + block * 128 + 128] = row.reshape(128)


def restore_feed(units):
    up = units[..., :96, :256].reshape(TILES, PARTS, BLOCKS, 96, 2, 128)
    up = jnp.transpose(up, (1, 2, 3, 4, 0, 5)).reshape(PARTS, MODEL, MODEL)
    low = units[..., :96, 256:].reshape(TILES, PARTS, BLOCKS, 96, 128)
    high = units[..., 96:, :].reshape(TILES, PARTS, BLOCKS, 32, 3, 128)
    high = jnp.transpose(high, (0, 1, 2, 4, 3, 5)).reshape(TILES, PARTS, BLOCKS, 96, 128)
    down = jnp.concatenate([low, high], 3)
    down = jnp.transpose(down, (1, 2, 0, 4, 3)).reshape(PARTS, BLOCKS * TILES * 128, 192)
    return up, down


def reduce_any_mesh(item):
    part = lax.psum_scatter(item, "seq", scatter_dimension=0, tiled=True)
    part = lax.psum_scatter(part.reshape(part.shape[1:]), "rows", scatter_dimension=0, tiled=True)
    return part.astype(F32)


def solution(mesh):
    split = P("rows", "seq", None)
    lines = P("rows", None)
    block = P("rows", "seq")
    in_specs = (split,) + (P(),) * 16 + (split, lines, lines, lines)
    out_specs = (split, split, P(), P(), block, P(), P(), P(), block, P(), P(), P(), P(), block, P(), block, P(), P())
    return jax.shard_map(on_device, mesh=mesh, in_specs=in_specs, out_specs=out_specs, check_vma=False)
```

```python
import functools
import math

import jax
import jax.numpy as jnp
from jax import lax
from jax.experimental import pallas as pl
from jax.experimental.pallas import tpu as pltpu
from jax.sharding import PartitionSpec as P

HEADS = 12
HEAD = 64
GRID = 24
SPAN = 2 * GRID - 1
SLOTS = 576
PADDED = 640
MODEL = 768
PAIRS = HEADS // 2
WIDE = 1152
STRIP = 128
BASE = 489
COMPACT = 32
LINES = 2304 // 128
IMGS = 4
EPS = 1e-06
NEGATIVE = -1e30
CHUNK = 144
PARTS = 4
BLOCKS = 8
TILES = 3
F32 = jnp.float32
BF16 = jnp.bfloat16
VMEM_LIMIT = 63 * 2**20
FIRST_GAIN, FIRST_SHIFT, QUERY_BIAS, VALUE_BIAS, OUTPUT_BIAS, ATTENTION_SCALE = range(6)
SECOND_GAIN, SECOND_SHIFT, DOWN_BIAS, FEED_SCALE, UP_BIAS = range(6, 11)


def dot(left, right):
    return lax.dot_general(left, right, (((1,), (0,)), ((), ())), preferred_element_type=F32)


def dot_nt(left, right):
    return lax.dot_general(left, right, (((1,), (1,)), ((), ())), preferred_element_type=F32)


def dot_tn(left, right):
    return lax.dot_general(left, right, (((0,), (0,)), ((), ())), preferred_element_type=F32)


def chunks(body):
    def step(index, carry):
        body(pl.ds(pl.multiple_of(index * CHUNK, CHUNK), CHUNK))
        return carry

    lax.fori_loop(0, SLOTS // CHUNK, step, 0)


def fold(value):
    return jnp.sum(value.reshape(value.shape[0] // 8, 8, value.shape[1]), 0)


def normal_of(values):
    center = values - jnp.mean(values, -1, keepdims=True)
    spread = lax.rsqrt(jnp.mean(center * center, -1, keepdims=True) + EPS)
    return center * spread, spread


def normal_back(change, normal, spread, gain):
    scaled = change * gain
    inner = (
        scaled
        - jnp.mean(scaled, -1, keepdims=True)
        - normal * jnp.mean(scaled * normal, -1, keepdims=True)
    )
    return inner * spread


def row_scalars(heights, widths, order, row):
    sizes, breadths, large = [], [], []
    for place in range(IMGS):
        picked = order[row, place]
        size, breadth = jnp.int32(0), jnp.int32(0)
        for image in range(IMGS):
            hit = picked == image
            size = size + jnp.where(hit, heights[row, image] * widths[row, image], 0)
            breadth = breadth + jnp.where(hit, widths[row, image], 0)
        sizes.append(size)
        breadths.append(breadth)
        large.append(jnp.where(picked == 0, 1, 0))
    begins = [jnp.int32(0)]
    for place in range(IMGS - 1):
        begins.append(begins[-1] + sizes[place])
    large_begin = sum(begins[p] * large[p] for p in range(IMGS))
    return dict(
        sizes=sizes,
        breadths=breadths,
        large=large,
        begins=begins,
        large_begin=large_begin,
        large_size=heights[row, 0] * widths[row, 0],
        large_width=widths[row, 0],
    )


def place_info(info, slot):
    segment = jnp.full(slot.shape, IMGS, jnp.int32)
    across = jnp.zeros(slot.shape, jnp.int32)
    down = jnp.zeros(slot.shape, jnp.int32)
    large = jnp.zeros(slot.shape, jnp.int32)
    for place in range(IMGS):
        offset = slot - info["begins"][place]
        inside = (offset >= 0) & (offset < info["sizes"][place])
        breadth = jnp.full(slot.shape, info["breadths"][place], jnp.int32)
        line = ((offset.astype(F32) + 0.5) / breadth.astype(F32)).astype(jnp.int32)
        segment = jnp.where(inside, place, segment)
        down = jnp.where(inside, line, down)
        across = jnp.where(inside, offset - line * breadth, across)
        large = jnp.where(inside, info["large"][place], large)
    return segment, down, across, large


def compact_index(info):
    found = []
    for axis in (0, 1):
        number = lax.broadcasted_iota(jnp.int32, (COMPACT, 128), axis)
        slot = number + jnp.where(number >= info["large_begin"], info["large_size"], 0)
        segment, down, across, large = place_info(info, slot)
        small = (segment < IMGS) & (large == 0) & (number < COMPACT)
        found.append((jnp.where(small, segment, -1 - axis), down, across))
    same = found[0][0] == found[1][0]
    row_step = found[0][1] - found[1][1] + 2
    column_step = found[0][2] - found[1][2] + 2
    return jnp.where(same, row_step * 5 + column_step, -1)


def shift_of(info, line):
    shift = BASE - (line - (GRID - 1)) * info["large_width"]
    return jnp.where(shift < 0, shift + WIDE, shift)


def flip():
    down = lax.broadcasted_iota(jnp.int32, (128, 128), 0)
    across = lax.broadcasted_iota(jnp.int32, (128, 128), 1)
    return jnp.where(down + across == 127, 1.0, 0.0).astype(BF16)


def line_place(line):
    start = LINES * 128 - SPAN - SPAN * line
    return start // 128, lax.rem(start, 128)


def prepare(info, table, flat, turned, columns, picks, query_codes, key_code, bands, near):
    flat[...] = jnp.zeros_like(flat)
    flat[0:HEADS, 0 : SPAN * SPAN] = table[...].astype(F32)
    turned[LINES] = jnp.zeros((16, 128), F32)
    for block in range(LINES):
        turned[LINES - 1 - block] = dot(flat[:, block * 128 : block * 128 + 128].astype(BF16), flip())
    for entry in range(25):
        at = (GRID - 3 + entry // 5) * SPAN + GRID - 3 + entry % 5
        columns[entry] = jnp.broadcast_to(flat[:, at : at + 1], (16, 128))

    def rows(index, carry):
        start = pl.multiple_of(index * 64, 64)
        slot = lax.broadcasted_iota(jnp.int32, (64, 128), 0) + start
        lane = lax.broadcasted_iota(jnp.int32, (64, 128), 1)
        segment, _, across, large = place_info(info, slot)
        rank = slot - jnp.where(slot >= info["large_begin"], info["large_size"], 0)
        small = (segment < IMGS) & (large == 0)
        target = jnp.where(small, rank, -1)
        pick = (lane == target) | (lane == segment + COMPACT)
        picks[pl.ds(start, 64), :] = jnp.where(pick, 1.0, 0.0).astype(BF16)
        code = across.astype(F32)
        query_codes[0, pl.ds(start, 64), :] = jnp.where(large == 1, code, -1e9)
        query_codes[1, pl.ds(start, 64), :] = jnp.where(large == 1, code, 1e9)
        return carry

    lax.fori_loop(0, SLOTS // 64, rows, 0)
    slot = lax.broadcasted_iota(jnp.int32, (8, PADDED), 1)
    key_code[...] = place_info(info, slot)[2].astype(F32)

    lanes = lax.broadcasted_iota(jnp.int32, (16, WIDE), 1)
    width = info["large_width"]

    def line_step(line, carry):
        low, high = carry
        shift = shift_of(info, line)
        block, lane = line_place(line)
        wide = jnp.concatenate([turned[block], turned[block + 1], jnp.zeros((16, WIDE - 256), F32)], 1)
        move = shift - lane
        rolled = pltpu.roll(wide, jnp.where(move < 0, move + WIDE, move), 1)
        entry = lanes - shift
        entry = jnp.where(entry < 0, entry + WIDE, entry)
        low = jnp.where((entry >= GRID - width) & (entry <= GRID - 1), rolled, low)
        high = jnp.where((entry >= GRID) & (entry <= GRID - 2 + width), rolled, high)
        return low, high

    zero = jnp.zeros((16, WIDE), F32)
    low, high = lax.fori_loop(0, SPAN, line_step, (zero, zero))
    for head in range(HEADS):
        bands[head, 0] = jnp.broadcast_to(low[head : head + 1], (8, WIDE))
        bands[head, 1] = jnp.broadcast_to(high[head : head + 1], (8, WIDE))

    index = compact_index(info)
    across = lax.broadcasted_iota(jnp.int32, (128 - COMPACT, 128), 1) - COMPACT
    down = lax.broadcasted_iota(jnp.int32, (128 - COMPACT, 128), 0)
    inside = (across >= 0) & (across <= IMGS) & (down <= IMGS)
    for head in range(HEADS):
        value = jnp.zeros((COMPACT, 128), F32)
        for entry in range(25):
            value = jnp.where(index == entry, columns[entry, head : head + 1, :], value)
        near[head, 0:COMPACT, :] = value.astype(BF16)
        own = jnp.where(down == IMGS, columns[12, head : head + 1, :], 0.0)
        lower = jnp.where(inside, jnp.where(across == down, own, NEGATIVE), 0.0)
        near[head, COMPACT:128, :] = lower.astype(BF16)


def project_in(tokens, vec, weight, first, query, keys, values, begin, count):
    gain, shift = vec[FIRST_GAIN : FIRST_GAIN + 1, :], vec[FIRST_SHIFT : FIRST_SHIFT + 1, :]

    def norm(index, carry):
        rows = pl.ds(pl.multiple_of(begin + index * CHUNK, CHUNK), CHUNK)
        normal, _ = normal_of(tokens[rows, :].astype(F32))
        first[rows, :] = (normal * gain + shift).astype(BF16)
        return carry

    lax.fori_loop(0, count // CHUNK, norm, 0)
    rows = pl.ds(pl.multiple_of(begin, CHUNK), count)
    step = 256
    for part, out in enumerate((query, keys, values)):
        for block in range(MODEL // step):
            lanes = slice(block * step, (block + 1) * step)
            columns = slice(part * MODEL + block * step, part * MODEL + (block + 1) * step)
            mixed = dot(first[rows, :], weight[:, columns])
            if part == 0:
                mixed = (mixed + vec[QUERY_BIAS : QUERY_BIAS + 1, lanes]) * HEAD**-0.5
            if part == 2:
                mixed = mixed + vec[VALUE_BIAS : VALUE_BIAS + 1, lanes]
            out[rows, lanes] = mixed.astype(BF16)


def half_mask(half):
    lane = lax.broadcasted_iota(jnp.int32, (SLOTS, 128), 1)
    return (lane < HEAD) if half == 0 else (lane >= HEAD)


def keep(mask, value):
    return jnp.where(mask, value, jnp.zeros_like(value))


def attend(query, keys, values, picks, query_codes, key_code, bands, near, chance_of, attended, inverse, strips, done):
    def pair_step(pair, carry):
        chance = chance_of(pair)
        lanes = pl.ds(pl.multiple_of(pair * 128, 128), 128)
        key_side = jnp.concatenate([keys[:, lanes], picks[...]], 1)
        totals = [None] * (SLOTS // 192)
        for half in range(2):
            head = pair * 2 + half
            mask = half_mask(half)
            near_side = dot(picks[...], near[head]).astype(BF16)
            query_side = jnp.concatenate([keep(mask, query[:, lanes]), near_side], 1)
            low_strip, high_strip = strips[half]
            for which, strip in enumerate((low_strip, high_strip)):
                band = jnp.concatenate([bands[head, which]] * (STRIP // 8), 0)
                strip[...] = pltpu.roll(band, 0, 1, stride=1, stride_axis=0)
            chance[half, :, SLOTS:] = jnp.zeros((SLOTS, PADDED - SLOTS), BF16)
            value_side = jnp.concatenate(
                [keep(mask, values[:, lanes]), keep(mask, jnp.ones((SLOTS, 128), BF16))], 1
            )
            for slab in range(SLOTS // 192):
                score = dot_nt(query_side[slab * 192 : slab * 192 + 192], key_side)
                weights = []
                for block in range(slab * 3, slab * 3 + 3):
                    rows = slice(block * 64, (block + 1) * 64)
                    strip_rows = slice(block % 2 * 64, block % 2 * 64 + 64)
                    start = 512 - block // 2 * 128
                    strip_lanes = slice(start, start + SLOTS)
                    code = key_code[0:1, 0:SLOTS]
                    low_hit = query_codes[0, rows, 0:1] >= code
                    high_hit = code > query_codes[1, rows, 0:1]
                    bias = jnp.where(
                        low_hit,
                        low_strip[strip_rows, strip_lanes],
                        jnp.where(high_hit, high_strip[strip_rows, strip_lanes], 0.0),
                    )
                    inside = (block - slab * 3) * 64
                    part = score[inside : inside + 64] + bias
                    top = jnp.max(part, -1, keepdims=True)
                    weight = jnp.exp(part - top).astype(BF16)
                    chance[half, rows, 0:SLOTS] = weight
                    weights.append(weight)
                added = dot(jnp.concatenate(weights, 0), value_side)
                totals[slab] = added if half == 0 else totals[slab] + added
        result = jnp.concatenate(totals, 0)
        scale = 1.0 / result[:, 128:]
        inverse[:, lanes] = scale
        attended[:, lanes] = result[:, :128] * scale
        done(pair)
        return carry

    lax.fori_loop(0, PAIRS, pair_step, 0)


def project_out(tokens, attended, weight, vec, branch, middle, second, attended_low):
    attended_low[...] = attended[...].astype(BF16)
    step = 256
    for block in range(MODEL // step):
        lanes = slice(block * step, (block + 1) * step)
        branch[:, lanes] = dot(attended_low[...], weight[:, lanes]) + vec[OUTPUT_BIAS : OUTPUT_BIAS + 1, lanes]
    scale = vec[ATTENTION_SCALE : ATTENTION_SCALE + 1, :]
    gain, shift = vec[SECOND_GAIN : SECOND_GAIN + 1, :], vec[SECOND_SHIFT : SECOND_SHIFT + 1, :]

    def norm(rows):
        value = tokens[rows, :].astype(F32) + scale * branch[rows, :]
        middle[rows, :] = value
        normal, _ = normal_of(value)
        second[rows, :] = (normal * gain + shift).astype(BF16)

    chunks(norm)


def gelu_parts(value):
    bell = jnp.exp2(value * value * (-0.5 * math.log2(math.e)))
    base = 1.0 + (0.3275911 / math.sqrt(2.0)) * jnp.abs(value)
    guess = pl.reciprocal(base, approx=True)
    inner = guess * (2.0 - base * guess)
    poly = 0.5 * 1.061405429
    for coefficient in (-1.453152027, 1.421413741, -0.284496736, 0.254829592):
        poly = poly * inner + 0.5 * coefficient
    tail = poly * inner * bell
    share = jnp.where(value >= 0.0, 1.0 - tail, tail)
    return value * share, share + value * bell * (1.0 / math.sqrt(2.0 * math.pi))


def feed(second, upstream, up, down, vec, second_change, unit, up_sum, feed_sums, outcome_change, outcome, active, slope, up_tile, down_tile, sems, before, after):
    def loads(tile):
        slot = tile % 2
        copies = []
        for block in range(BLOCKS):
            start = 3 * 128 * block + 128 * tile
            inside = slice(block * 128, block * 128 + 128)
            copies.append(
                pltpu.make_async_copy(
                    up.at[:, start : start + 128], up_tile.at[slot, :, inside], sems.at[slot, 0, block]
                )
            )
            copies.append(
                pltpu.make_async_copy(
                    down.at[start : start + 128], down_tile.at[slot, inside], sems.at[slot, 1, block]
                )
            )
        return copies

    for copy in loads(0):
        copy.start()
    feed_sums[...] = jnp.zeros_like(feed_sums)
    scale = vec[FEED_SCALE : FEED_SCALE + 1, :]

    def begin(rows):
        value = (upstream[rows, :].astype(F32) * scale).astype(BF16)
        outcome_change[rows, :] = value
        feed_sums[1] += fold(value.astype(F32))

    chunks(begin)
    for tile in range(TILES):
        slot = tile % 2
        if tile + 1 < TILES:
            for copy in loads(tile + 1):
                copy.start()
        for copy in loads(tile):
            copy.wait()
        for pair in range(BLOCKS // 2):
            wide = slice(pair * 256, pair * 256 + 256)
            line = slice(UP_BIAS + pair, UP_BIAS + pair + 1)
            ends = [slice(start + 128 * tile, start + 128 * tile + 128) for start in (0, 384)]
            bias = jnp.concatenate([vec[line, end] for end in ends], 1)
            for start in range(0, SLOTS, 192):
                rows = slice(start, start + 192)
                value, gradient = gelu_parts(dot(second[rows, :], up_tile[slot, :, wide]) + bias)
                active[rows, wide] = value.astype(BF16)
                back = dot_nt(outcome_change[rows, :], down_tile[slot, wide, :])
                slope[rows, wide] = (back * gradient).astype(BF16)
            before(tile, pair)
        for start in range(0, MODEL, 256):
            lanes = slice(start, start + 256)
            result = dot(active[...], down_tile[slot, :, lanes])
            back = dot_nt(slope[...], up_tile[slot, lanes, :])
            if tile == 0:
                outcome[:, lanes] = result
                second_change[:, lanes] = back
            else:
                outcome[:, lanes] += result
                second_change[:, lanes] += back
        total = dot(jnp.ones((8, SLOTS), BF16), slope[...])
        for block in range(BLOCKS):
            inside = slice(block * 128, block * 128 + 128)
            start = 3 * 128 * block + 128 * tile
            up_sum[:, start : start + 128] = total[:, inside]
        for pair in range(BLOCKS // 2):
            turned = dot_tn(second[...], slope[:, pair * 256 : pair * 256 + 256]).astype(BF16)
            unit[pair, :, :, 0:96, 0:256] = turned.reshape(4, 2, 96, 256)
        for pair in range(BLOCKS // 2):
            turned = dot_tn(outcome_change[...], active[:, pair * 256 : pair * 256 + 256]).astype(BF16)
            for side in range(2):
                inside = slice(side * 128, side * 128 + 128)
                for part in range(PARTS):
                    start = part * 192
                    unit[part, pair, side, 0:96, 256:384] = turned[start : start + 96, inside]
                    for third in range(3):
                        start = part * 192 + 96 + third * 32
                        unit[part, pair, side, 96:128, third * 128 : third * 128 + 128] = turned[start : start + 32, inside]
        after(tile)


def feed_end(upstream, middle, vec, output, outcome, feed_sums):
    scale, bias = vec[FEED_SCALE : FEED_SCALE + 1, :], vec[DOWN_BIAS : DOWN_BIAS + 1, :]

    def end(rows):
        value = outcome[rows, :] + bias
        output[rows, :] = (middle[rows, 0:MODEL] + scale * value).astype(BF16)
        feed_sums[0] += fold(upstream[rows, :].astype(F32) * value)

    chunks(end)


def pair_at(turn):
    late = turn // 4
    return (1 - late) * ((3 * turn + 1) // 2) + late * (3 * turn - 11)


def attend_back(query, keys, values, picks, query_codes, key_code, chance_of, change_low, attended, inverse, joined, band_sums, near_sums, score_changes, event, middle_event):
    for score_change in score_changes:
        score_change[:, SLOTS:] = jnp.zeros((SLOTS, PADDED - SLOTS), BF16)

    def pair_step(turn, carry):
        pair = pair_at(turn)
        event(turn)
        chance = chance_of(turn)
        lanes = pl.ds(pl.multiple_of(pair * 128, 128), 128)
        lane = lax.broadcasted_iota(jnp.int32, (SLOTS, 128), 1)
        own_change = change_low[:, lanes].astype(F32)
        scale = inverse[:, lanes]
        terms = own_change * attended[:, lanes]
        high = terms.astype(BF16)
        low = (terms - high.astype(F32)).astype(BF16)
        block_row = lax.broadcasted_iota(jnp.int32, (128, 128), 0) // HEAD
        block_lane = lax.broadcasted_iota(jnp.int32, (128, 128), 1) // HEAD
        block = jnp.where(block_row == block_lane, 1.0, 0.0).astype(BF16)
        delta = (dot(high, block) + dot(low, block)) * -scale
        delta_high = delta.astype(BF16)
        delta_low = (delta - delta_high.astype(F32)).astype(BF16)
        scaled = (own_change * scale).astype(BF16)
        value_side = jnp.concatenate([values[:, lanes], jnp.ones((SLOTS, 128), BF16)], 1)
        query_total = jnp.zeros((SLOTS, 128), F32)
        key_total = jnp.zeros((SLOTS, 128), F32)
        value_total = jnp.zeros((SLOTS, 128), F32)
        for half in range(2):
            if half == 1:
                middle_event(turn)
            head = pair * 2 + half
            mask = half_mask(half)
            extra = jnp.where(
                lane == half * HEAD,
                delta_high,
                jnp.where(lane == half * HEAD + 1, delta_low, jnp.zeros_like(delta_low)),
            )
            own_scaled = keep(mask, scaled)
            score_change = score_changes[half]
            change_side = jnp.concatenate([own_scaled, extra], 1)
            for start in range(0, SLOTS, 192):
                rows = slice(start, start + 192)
                weight_change = dot_nt(change_side[rows], value_side)
                value = chance[half, rows, 0:SLOTS].astype(F32) * weight_change
                score_change[rows, 0:SLOTS] = value.astype(BF16)
            kinds = [None, None]
            own_score = score_change[:, 0:SLOTS]
            key_side = jnp.concatenate([keep(mask, keys[:, lanes]), picks[...]], 1)
            both = dot(own_score, key_side)
            query_total = query_total + both[:, :128]
            near_sums[head] = dot_tn(picks[...], both[:, 128:].astype(BF16))
            key_total = key_total + dot_tn(own_score, keep(mask, query[:, lanes]))
            value_total = value_total + dot_tn(chance[half, :, 0:SLOTS], own_scaled)
            for group in range(STRIP // 16 - 1, -1, -1):
                tiles = [[jnp.zeros((16, 128), F32)] * (WIDE // 128) for _ in range(2)]
                for major in range(-(-SLOTS // STRIP)):
                    start = major * STRIP + group * 16
                    if start >= SLOTS:
                        continue
                    rows = slice(start, start + 16)
                    low_code = query_codes[0, rows, :]
                    high_code = query_codes[1, rows, :]
                    for column in range(PADDED // 128):
                        span = slice(column * 128, column * 128 + 128)
                        value = score_change[rows, span].astype(F32)
                        code = jnp.broadcast_to(key_code[0:1, span], (16, 128))
                        place = 4 - major + column
                        tiles[0][place] = tiles[0][place] + jnp.where(low_code >= code, value, 0.0)
                        tiles[1][place] = tiles[1][place] + jnp.where(code > high_code, value, 0.0)
                for which in range(2):
                    fresh = jnp.concatenate(tiles[which], 1)
                    if group == STRIP // 16 - 1:
                        kinds[which] = fresh
                    else:
                        kinds[which] = pltpu.roll(kinds[which], WIDE - 16, 1) + fresh
            for which in range(2):
                band_sums[head, which] = kinds[which][0:8] + pltpu.roll(kinds[which][8:16], WIDE - 8, 1)
        joined[0][:, lanes] = (query_total.astype(BF16).astype(F32) * HEAD**-0.5).astype(BF16)
        joined[1][:, lanes] = key_total.astype(BF16)
        joined[2][:, lanes] = value_total.astype(BF16)
        return carry

    lax.fori_loop(0, PAIRS, pair_step, 0)


def table_back(info, band_sums, near_sums, table_sum):
    kinds = []
    for which in range(2):
        total = jnp.zeros((16, WIDE), F32)
        for step in range(8):
            rows = jnp.concatenate(
                [band_sums[head, which, step : step + 1, :] for head in range(HEADS)]
                + [jnp.zeros((16 - HEADS, WIDE), F32)],
                0,
            )
            total = total + (rows if step == 0 else pltpu.roll(rows, WIDE - step, 1))
        kinds.append(total)
    low, high = kinds
    width = info["large_width"]
    entry = lax.broadcasted_iota(jnp.int32, (16, 128), 1)
    low_hit = (entry >= GRID - width) & (entry <= GRID - 1)
    high_hit = (entry >= GRID) & (entry <= GRID - 2 + width)

    table_sum[...] = jnp.zeros_like(table_sum)
    lane_wide = lax.broadcasted_iota(jnp.int32, (16, 256), 1)

    def line_step(line, carry):
        block, lane = line_place(line)
        back = WIDE - shift_of(info, line)
        low_part = pltpu.roll(low, back, 1)[:, :128]
        high_part = pltpu.roll(high, back, 1)[:, :128]
        part = jnp.where(low_hit, low_part, jnp.where(high_hit, high_part, 0.0))
        wide = pltpu.roll(jnp.concatenate([part, jnp.zeros((16, 128), F32)], 1), lane, 1)
        table_sum[block] += wide[:, :128]
        table_sum[block + 1] += wide[:, 128:]
        return carry

    lax.fori_loop(0, SPAN, line_step, 0)
    index = compact_index(info)
    head_row = lax.broadcasted_iota(jnp.int32, (16, 128), 0)
    centre = jnp.zeros((16, 128), F32)
    for head in range(HEADS):
        at = COMPACT + IMGS
        centre = jnp.where(head_row == head, near_sums[head, at : at + 1, :], centre)
    centre = jnp.sum(jnp.where(entry == COMPACT + IMGS, centre, 0.0), 1, keepdims=True)
    for number in range(25):
        hit = index == number
        column = jnp.zeros((16, 128), F32)
        for head in range(HEADS):
            part = jnp.sum(jnp.where(hit, near_sums[head, 0:COMPACT, :], 0.0), 0, keepdims=True)
            column = jnp.where(head_row == head, part, column)
        total = jnp.sum(column, 1, keepdims=True)
        if number == 12:
            total = total + centre
        at = LINES * 128 - 1 - (GRID - 3 + number // 5) * SPAN - (GRID - 3 + number % 5)
        table_sum[at // 128] += jnp.where(entry == at % 128, total, 0.0)


def remote(source, target, send, receive, device):
    return pltpu.make_async_remote_copy(
        src_ref=source,
        dst_ref=target,
        send_sem=send,
        recv_sem=receive,
        device_id=device,
        device_id_type=pl.DeviceIdType.MESH,
    )


def greet(devices):
    barrier = pltpu.get_barrier_semaphore()
    for device in devices:
        pl.semaphore_signal(barrier, inc=1, device_id=device, device_id_type=pl.DeviceIdType.MESH)
    pl.semaphore_wait(barrier, len(devices))


def group_peers(parts):
    row, me = lax.axis_index("rows"), lax.axis_index("seq")
    near = 1 - 2 * (me % 2)
    far = 2 - 4 * (me // 2)
    return row, me, [me + near, me + far, me + near + far]


def block_of(index, size):
    return pl.ds(pl.multiple_of(index * size, size), size)


def forward_kernel(heights, widths, order, table, *refs):
    rows_of, refs = refs[:11], refs[11:]
    forward_body(heights, widths, order, table, rows_of, *refs)


def stack_rows(rows_of, vec):
    vec[...] = jnp.zeros_like(vec)
    line = 0
    for item in rows_of:
        for start in range(0, item.shape[0], 128):
            where = start // MODEL + line
            lanes = slice(start % MODEL, start % MODEL + 128)
            vec[where : where + 1, lanes] = item[start : start + 128].astype(F32).reshape(1, 128)
        line += item.shape[0] // MODEL


def forward_body(heights, widths, order, table, rows_of, input_weight, output_weight, own_tokens, own_upstream, *rest):
    (tokens_far, upstream, first_far, query_far, keys_far, values_far, chance_far, attended_far, inverse_far, branch_far, middle_far, attended_low_far, second, picks, query_codes, key_code, vec), rest = rest[:17], rest[17:]
    (tokens, first, query, keys, values, attended, inverse, branch, middle, attended_low, chance, bands, near, low_strip, high_strip, other_low, other_high, flat, turned, columns, store_sems, chance_sems, send, receive, local) = rest
    parts, slots = own_tokens.shape[0], own_tokens.shape[1]
    row, me, peers = group_peers(parts)
    greet([(row, peer) for peer in peers])

    def exchange(which, source, target):
        mine = block_of(me, slots)
        copies = [
            remote(source.at[peer], target.at[mine], send.at[which, step], receive.at[which, step], (row, peer))
            for step, peer in enumerate(peers)
        ]
        return copies + [pltpu.make_async_copy(source.at[me], target.at[mine], local.at[which])]

    token_copies = exchange(0, own_tokens, tokens)
    upstream_copies = exchange(1, own_upstream, upstream)
    stores = {
        number: pltpu.make_async_copy(source, target, store_sems.at[number])
        for number, (source, target) in enumerate(
            (
                (tokens, tokens_far),
                (first, first_far),
                (query, query_far),
                (keys, keys_far),
                (values, values_far),
                (attended, attended_far),
                (inverse, inverse_far),
                (attended_low, attended_low_far),
                (branch, branch_far),
                (middle, middle_far),
            )
        )
    }
    for copy in token_copies:
        copy.start()
    stack_rows(rows_of, vec)
    info = row_scalars(heights, widths, order, me)
    prepare(info, table, flat, turned, columns, picks, query_codes, key_code, bands, near)
    half = SLOTS // 2
    own_half = me // 2
    token_copies[0].wait()
    token_copies[3].wait()
    project_in(tokens, vec, input_weight, first, query, keys, values, own_half * half, half)
    token_copies[1].wait()
    token_copies[2].wait()
    for copy in upstream_copies:
        copy.start()
    stores[0].start()
    project_in(tokens, vec, input_weight, first, query, keys, values, (1 - own_half) * half, half)
    for number in range(1, 5):
        stores[number].start()

    def chance_copy(pair):
        slot = lax.rem(pair, 2)
        return pltpu.make_async_copy(chance.at[slot], chance_far.at[pl.ds(pair * 2, 2)], chance_sems.at[slot])

    def chance_of(pair):
        @pl.when(pair >= 2)
        def _():
            chance_copy(pair - 2).wait()

        return chance.at[lax.rem(pair, 2)]

    attend(query, keys, values, picks, query_codes, key_code, bands, near, chance_of, attended, inverse, ((low_strip, high_strip), (other_low, other_high)), lambda pair: chance_copy(pair).start())
    for number in (5, 6):
        stores[number].start()
    project_out(tokens, attended, output_weight, vec, branch, middle, second, attended_low)
    for number in (7, 8, 9):
        stores[number].start()
    for pair in (PAIRS - 2, PAIRS - 1):
        chance_copy(jnp.int32(pair)).wait()
    for number in stores:
        stores[number].wait()
    for copy in upstream_copies:
        copy.wait()


UNITS = ((128, 384), (128, 384), (128, 384), (144, 384), (48, 384))
LATE = (
    (((0, 0, 128), (0, 256, 384), (0, 384, 512)), ((0, 640, 768), (1, 0, 128), (1, 256, 384)), ((1, 384, 512), (1, 640, 768), (2, 0, 128)), ((2, 256, 384), (2, 384, 512), (2, 640, 768))),
    (((0, 128, 256), (0, 512, 576)), ((1, 128, 256), (0, 576, 640)), ((1, 512, 640), (2, 128, 192)), ((2, 512, 640), (2, 192, 256))),
)


SPLITS = (64, 64, 64, 64, 32)
PLAN = {
    ("slab", 1, 3): (("first", 0),),
    ("slab", 2, 3): (("first", 1),),
    "norm": (("first", 2),),
    ("middle", 0): (("second_y", 1),),
    ("pair", 2): (("second_x", 1),),
    ("middle", 2): (("second_x", 0),),
    ("pair", 3): (("second_y", 0),),
    ("pair", 4): (("second_x", 2),),
    ("middle", 4): (("second_y", 2), ("third", 1),),
    ("pair", 5): (("first", 3), ("third", 0),),
    ("middle", 5): (("third", 2),),
    "late": (("first", 4), ("second_y", 3), ("second_x", 3),),
    "given": (("second_y", 4), ("second_x", 4), ("third", 3),),
    ("small", 0): (("fourth", 0),),
    ("small", 1): (("third", 4),),
    ("small", 2): (("fourth", 2),),
    "end": (("fourth", 1), ("fourth", 3), ("fourth", 4),),
}


class Reduction:
    def __init__(self, sources, results, owns, core_in, x_in, y_in, late, line_in, send, receive, local):
        self.sources, self.results, self.owns = sources, results, owns
        self.core_in, self.x_in, self.y_in, self.late, self.line_in = core_in, x_in, y_in, late, line_in
        self.send, self.receive, self.local = send, receive, local
        rows, seq = lax.axis_index("rows"), lax.axis_index("seq")
        self.z, self.x, self.y, self.core = rows // 2, rows % 2, seq // 2, seq % 2
        z, x, y, core = self.z, self.x, self.y, self.core
        self.core_peer = (rows, y * 2 + 1 - core)
        self.x_peer = (z * 2 + 1 - x, seq)
        self.y_peer = (rows, (1 - y) * 2 + core)
        self.diagonal = (z * 2 + 1 - x, (1 - y) * 2 + core)
        self.z_peers = [(lax.rem(z + step, 4) * 2 + x, seq) for step in range(1, 4)]

    def cut(self, unit):
        return SPLITS[unit]

    def go(self, place):
        for name, unit in PLAN.get(place, ()):
            getattr(self, name)(unit)

    def peers(self):
        return [self.core_peer, self.x_peer, self.y_peer, self.diagonal] + self.z_peers

    def copy(self, unit, number, source, target, peer):
        return remote(source, target, self.send.at[unit, number], self.receive.at[unit, number], peer)

    def core_copies(self, unit):
        return [
            self.copy(unit, part, self.sources[unit].at[part * 2 + 1 - self.core], self.core_in[unit].at[part], self.core_peer)
            for part in range(2)
        ]

    def own_copies(self, unit):
        if self.owns[unit] is None:
            return []
        return [
            pltpu.make_async_copy(self.sources[unit].at[part * 2 + self.core], self.owns[unit].at[part], self.local.at[unit, part])
            for part in range(2)
        ]

    def x_copy(self, unit):
        return self.copy(unit, 2, self.core_in[unit].at[:, :, 1 - self.x, 0 : self.cut(unit)], self.x_in[unit], self.x_peer)

    def y_copy(self, unit):
        return self.copy(unit, 3, self.core_in[unit].at[1 - self.y, :, :, self.cut(unit) :], self.y_in[unit], self.y_peer)

    def again_y(self, unit):
        return self.copy(unit, 4, self.x_in[unit].at[1 - self.y], self.late[unit].at[:, 0 : self.cut(unit)], self.y_peer)

    def again_x(self, unit):
        return self.copy(unit, 5, self.y_in[unit].at[:, 1 - self.x], self.late[unit].at[:, self.cut(unit) :], self.x_peer)

    def line_copies(self, unit):
        return [
            self.copy(unit, 6 + step, self.late[unit].at[lax.rem(self.z + step + 1, 4)], self.line_in[unit].at[step], peer)
            for step, peer in enumerate(self.z_peers)
        ]

    def begin(self, unit):
        for copy in self.core_copies(unit):
            copy.start()

    def fetch(self, unit):
        for copy in self.own_copies(unit):
            copy.start()

    def first(self, unit):
        for copy in self.core_copies(unit) + self.own_copies(unit):
            copy.wait()
        held, own = self.core_in[unit], self.owns[unit]

        def add(line, carry):
            for part in range(2):
                for side in range(2):
                    if own is None:
                        term = self.sources[unit][part * 2 + self.core, line, side]
                    else:
                        term = own[part, line, side]
                    held[part, line, side] = held[part, line, side] + term
            return carry

        lax.fori_loop(0, 4, add, 0)
        self.x_copy(unit).start()
        self.y_copy(unit).start()

    def second_x(self, unit):
        x_in, held = self.x_in[unit], self.core_in[unit]
        self.x_copy(unit).wait()

        def add_x(line, carry):
            for part in range(2):
                x_in[part, line] = x_in[part, line] + held[part, line, self.x, 0 : self.cut(unit)]
            return carry

        lax.fori_loop(0, 4, add_x, 0)
        self.again_y(unit).start()

    def second_y(self, unit):
        y_in, held = self.y_in[unit], self.core_in[unit]
        self.y_copy(unit).wait()

        def add_y(line, carry):
            for side in range(2):
                y_in[line, side] = y_in[line, side] + held[self.y, line, side, self.cut(unit) :]
            return carry

        lax.fori_loop(0, 4, add_y, 0)
        self.again_x(unit).start()

    def third(self, unit):
        late, x_in, y_in = self.late[unit], self.x_in[unit], self.y_in[unit]
        self.again_y(unit).wait()
        self.again_x(unit).wait()

        def add(line, carry):
            late[line, 0 : self.cut(unit)] = late[line, 0 : self.cut(unit)] + x_in[self.y, line]
            late[line, self.cut(unit) :] = late[line, self.cut(unit) :] + y_in[line, self.x]
            return carry

        lax.fori_loop(0, 4, add, 0)
        for copy in self.line_copies(unit):
            copy.start()

    def fourth(self, unit):
        for copy in self.line_copies(unit):
            copy.wait()
        total = self.late[unit][self.z].astype(F32)
        for step in range(3):
            total = total + self.line_in[unit][step].astype(F32)
        self.results[unit](total)


class SmallSum:
    def __init__(self, link, small, out, plane_in, line_in, part, send, receive):
        self.link, self.small, self.out = link, small, out
        self.plane_in, self.line_in, self.part = plane_in, line_in, part
        self.send, self.receive = send, receive
        self.mine = self.place(link.core, link.x, link.y)
        self.plane_peers = []
        for flips in range(1, 8):
            core = 1 - link.core if flips & 4 else link.core
            x = 1 - link.x if flips & 2 else link.x
            y = 1 - link.y if flips & 1 else link.y
            self.plane_peers.append(((link.z * 2 + x, y * 2 + core), self.place(core, x, y)))

    def place(self, core, x, y):
        return core * 4 + x * 2 + y

    def copy(self, number, source, target, peer):
        return remote(source, target, self.send.at[number], self.receive.at[number], peer)

    def plane_copies(self):
        return [
            self.copy(step, self.small.at[index], self.plane_in.at[step], peer)
            for step, (peer, index) in enumerate(self.plane_peers)
        ]

    def line_copies(self):
        return [self.copy(7 + step, self.part, self.line_in.at[step], peer) for step, peer in enumerate(self.link.z_peers)]

    def plane_back(self):
        mine = self.out.at[self.mine]
        return [self.copy(10 + step, mine, mine, peer) for step, (peer, _) in enumerate(self.plane_peers)]

    def steps(self):
        def one():
            for copy in self.plane_copies():
                copy.start()

        def two():
            for copy in self.plane_copies():
                copy.wait()
            total = self.small[self.mine]
            for step in range(7):
                total = total + self.plane_in[step]
            self.part[...] = total
            for copy in self.line_copies():
                copy.start()

        def three():
            for copy in self.line_copies():
                copy.wait()
            self.out[self.mine] = self.part[...] + self.line_in[0] + self.line_in[1] + self.line_in[2]
            for copy in self.plane_back():
                copy.start()

        def four():
            for copy in self.plane_back():
                copy.wait()

        return [one, two, three, four]


def pack_small(table_sum, sums, feed_sums, up_sum, vectors, small):
    for block in range(LINES):
        small[block // 3, block % 3] = table_sum[block]
    vectors[...] = jnp.zeros_like(vectors)
    for number in range(8):
        vectors[number : number + 1, :] = jnp.sum(sums[number], 0, keepdims=True)
    for number in range(2):
        vectors[8 + number : 9 + number, :] = jnp.sum(feed_sums[number], 0, keepdims=True)
    for number in range(PARTS):
        vectors[10 + number : 11 + number, :] = up_sum[0:1, number * MODEL : (number + 1) * MODEL]
    for number in range(6):
        block = LINES + number
        small[block // 3, block % 3] = vectors[:, number * 128 : (number + 1) * 128]


def backward_kernel(paired, heights, widths, order, vec, upstream, second, picks, query_codes, key_code, output_weight, up_far, down_far, weight_far, tokens_far, first_far, query_far, keys_far, values_far, attended_far, inverse_far, branch_far, middle_far, attended_low_far, chance_far, *rest):
    if paired:
        (own_output, own_gradient, up_result, down_result), late_results, small_out, rest = rest[:4], rest[4:7], rest[7], rest[8:]
    else:
        (own_output, own_gradient, feed_units), late_outs, small_out, rest = rest[:3], rest[3:5], rest[5], rest[6:]
    (hidden, change, active, slope, outcome_change, outcome, second_change, branch_change, change_low, attended_low, output, query, keys, values, first, up_tile, down_tile, chance, score_change, other_change, band_sums, near_sums, table_sum, sums, feed_sums, up_sum, vectors, unit, small), rest = rest[:29], rest[29:]
    (tile_sems, load_sems, chance_sems, send, receive, local), rest = rest[:6], rest[6:]
    parts, slots = own_output.shape[0], own_output.shape[1]
    row, me, peers = group_peers(parts)
    feed_unit = unit.at[:, :, :, 0:128, :]
    if paired:
        count = len(UNITS)
        stages = [rest[i * count : (i + 1) * count] for i in range(5)]
        rest = rest[5 * count :]
        sources = [feed_unit] * TILES + [unit, unit.at[:, :, :, 0:48, :]]

        def feed_result(tile):
            def put(total):
                for half in range(2):
                    columns = slice(half * 384 + tile * 128, half * 384 + tile * 128 + 128)
                    up_result[:, columns] = total[0:96, half * 128 : half * 128 + 128]
                columns = slice(tile * 128, tile * 128 + 128)
                down_result[0:96, columns] = total[0:96, 256:384]
                for third in range(3):
                    lines = slice(96 + third * 32, 128 + third * 32)
                    down_result[lines, columns] = total[96:128, third * 128 : third * 128 + 128]

            return put

        def first_put(total):
            late_results[0][...] = total[0:96]
            for half in range(2):
                late_results[2][half * 48 : half * 48 + 48, :] = total[96:144, half * 192 : half * 192 + 192]

        def second_put(total):
            for half in range(2):
                late_results[1][half * 48 : half * 48 + 48, :] = total[:, half * 192 : half * 192 + 192]

        results = [feed_result(tile) for tile in range(TILES)] + [first_put, second_put]
        link = Reduction(sources, results, [None] * count, *stages, *rest[:2], None)
        small_sum = SmallSum(link, small, small_out, *rest[2:])
        greet([peer for peer, _ in small_sum.plane_peers] + link.z_peers)
    else:
        greet([(row, peer) for peer in peers])

    def give_back(which, source, target):
        copies = [
            remote(source.at[block_of(peer, slots)], target.at[me], send.at[which, step], receive.at[which, step], (row, peer))
            for step, peer in enumerate(peers)
        ]
        return copies + [pltpu.make_async_copy(source.at[block_of(me, slots)], target.at[me], local.at[which])]

    gradient = change_low
    output_copies = give_back(0, output, own_output)
    gradient_copies = give_back(1, gradient, own_gradient)
    wide = slice(0, MODEL)

    def load(number, source, target):
        return pltpu.make_async_copy(source, target, load_sems.at[number])

    load_query = load(0, query_far, query)
    load_keys = load(1, keys_far, keys)
    load_values = load(2, values_far, values)
    load_first = load(3, first_far, first)
    load_low = load(4, attended_low_far, attended_low)
    load_middle = load(5, middle_far, change.at[:, wide])
    load_branch = load(6, branch_far, hidden.at[:, wide])
    load_attended = load(7, attended_far, hidden.at[:, wide])
    load_inverse = load(8, inverse_far, change.at[:, wide])
    load_tokens = load(9, tokens_far, query)
    in_weights = (up_tile.at[0, :, wide], up_tile.at[1, :, wide], down_tile.at[0, wide, :])
    load_weights = [
        load(10 + number, weight_far.at[:, number * MODEL : (number + 1) * MODEL], target)
        for number, target in enumerate(in_weights)
    ]

    def chance_copy(turn):
        slot = lax.rem(turn, 2)
        return pltpu.make_async_copy(chance_far.at[pl.ds(pair_at(turn) * 2, 2)], chance.at[slot], chance_sems.at[slot])

    for copy in (load_query, load_keys, load_values, load_first, load_low):
        copy.start()
    chance_copy(jnp.int32(0)).start()

    def before(tile, pair):
        if tile == TILES - 1 and pair == 3:
            load_middle.start()
            load_branch.start()
        if paired:
            link.go(("slab", tile, pair))

    def after(tile):
        if paired:
            link.begin(tile)
        else:
            copy = load(13, feed_unit, feed_units.at[tile])
            copy.start()
            copy.wait()

    feed(second, upstream, up_far, down_far, vec, second_change, feed_unit, up_sum, feed_sums, outcome_change, outcome, active, slope, up_tile, down_tile, tile_sems, before, after)
    for copy in load_weights:
        copy.start()
    load_middle.wait()
    feed_end(upstream, change, vec, output, outcome, feed_sums)
    for copy in output_copies:
        copy.start()
    load_branch.wait()
    info = row_scalars(heights, widths, order, me)
    sums[...] = jnp.zeros_like(sums)
    middle_change = outcome
    gain, scale = vec[SECOND_GAIN : SECOND_GAIN + 1, :], vec[ATTENTION_SCALE : ATTENTION_SCALE + 1, :]

    def norm(rows):
        normal, spread = normal_of(change[rows, wide])
        back = second_change[rows, :]
        sums[6] += fold(back * normal)
        sums[7] += fold(back)
        value = upstream[rows, :].astype(F32) + normal_back(back, normal, spread, gain)
        middle_change[rows, :] = value
        sums[5] += fold(value * hidden[rows, wide])
        low = (value * scale).astype(BF16)
        branch_change[rows, :] = low
        sums[4] += fold(low.astype(F32))

    chunks(norm)
    load_attended.start()
    load_inverse.start()
    change_low[...] = dot_nt(branch_change[...], output_weight[...]).astype(BF16)
    if paired:
        link.go("norm")
    for copy in (load_query, load_keys, load_values, load_attended, load_inverse):
        copy.wait()

    joined = (active, slope, outcome_change)

    def packed(value):
        value = value.astype(BF16).reshape(4, 2, 2, 48, 192)
        return jnp.concatenate([value[:, :, 0], value[:, :, 1]], -1)

    def late_parts(number):
        for part in range(PARTS):
            pieces = [joined[which][:, low:high] for which, low, high in LATE[number][part]]
            value = dot_tn(first[...], jnp.concatenate(pieces, 1))
            if number == 1:
                unit[part, :, :, 0:48, 0:384] = packed(value)
            else:
                unit[part, :, :, 0:96, 0:384] = value.astype(BF16).reshape(4, 2, 96, 384)
                piece = branch_change[:, part * 192 : part * 192 + 192]
                unit[part, :, :, 96:144, 0:384] = packed(dot_tn(attended_low[...], piece))
        if paired:
            link.begin(TILES + number)
        else:
            source = unit if number == 0 else unit.at[:, :, :, 0:48, :]
            copy = load(13, source, late_outs[number])
            copy.start()
            copy.wait()

    def at_turn(name, turn):
        for number in range(PAIRS):
            if paired and (name, number) in PLAN:

                @pl.when(turn == number)
                def _(number=number):
                    link.go((name, number))

    def event(turn):
        @pl.when(turn + 1 < PAIRS)
        def _():
            chance_copy(turn + 1).start()

        chance_copy(turn).wait()

        @pl.when(turn == 4)
        def _():
            load_first.wait()
            load_low.wait()
            late_parts(0)

        at_turn("pair", turn)

    def middle_event(turn):
        at_turn("middle", turn)

    attend_back(query, keys, values, picks, query_codes, key_code, lambda turn: chance.at[lax.rem(turn, 2)], change_low, hidden, change, joined, band_sums, near_sums, (score_change, other_change), event, middle_event)
    load_tokens.start()
    late_parts(1)
    if paired:
        link.go("late")
    for copy in load_weights:
        copy.wait()
    first_change = hidden
    for start in range(0, MODEL, 256):
        lanes = slice(start, start + 256)
        total = dot_nt(joined[0][:, wide], in_weights[0][lanes, :])
        total = total + dot_nt(joined[1][:, wide], in_weights[1][lanes, :])
        first_change[:, lanes] = total + dot_nt(joined[2][...], in_weights[2][lanes, :])
    load_tokens.wait()
    gain_first = vec[FIRST_GAIN : FIRST_GAIN + 1, :]
    if paired:
        link.go("products")

    def norm_first(rows):
        normal, spread = normal_of(query[rows, :].astype(F32))
        back = first_change[rows, wide]
        sums[0] += fold(back * normal)
        sums[1] += fold(back)
        value = middle_change[rows, :] + normal_back(back, normal, spread, gain_first)
        gradient[rows, :] = value.astype(BF16)

    chunks(norm_first)
    line = lax.broadcasted_iota(jnp.int32, (8, SLOTS), 0)
    one = jnp.where(line == 0, 1.0, 0.0).astype(BF16)
    sums[2] = dot(one, joined[0][:, wide])
    sums[3] = dot(one, joined[2][...])
    for copy in gradient_copies:
        copy.start()
    if paired:
        link.go("given")
    table_back(info, band_sums, near_sums, table_sum)
    pack_small(table_sum, sums, feed_sums, up_sum, vectors, small)
    if paired:
        link.go("tabled")
        for number, step in enumerate(small_sum.steps()):
            step()
            link.go(("small", number))
        link.go("end")
    else:
        small_out[...] = small[...]
    for copy in output_copies + gradient_copies:
        copy.wait()


def whole():
    return pl.BlockSpec(memory_space=pltpu.VMEM)


def far():
    return pl.BlockSpec(memory_space=pl.ANY)


def scalars():
    return pl.BlockSpec(memory_space=pltpu.SMEM)


def shape(*dims, dtype=F32):
    return jax.ShapeDtypeStruct(dims, dtype)


def on_device(layer_input, first_gain, first_shift, input_weight, query_bias, value_bias, bias_table, output_weight, output_bias, attention_scale, second_gain, second_shift, up_weight, up_bias, down_weight, down_bias, feed_scale, upstream, grid_heights, grid_widths, packing_order):
    parts = lax.axis_size("seq")
    paired = (lax.axis_size("rows"), parts) == (8, 4)
    slots = layer_input.shape[1]
    hidden_units = up_weight.shape[1]

    rows_of = [first_gain, first_shift, query_bias, value_bias, output_bias, attention_scale, second_gain, second_shift, down_bias, feed_scale, up_bias]
    full = (SLOTS, MODEL)
    low_full, wide_full = shape(*full, dtype=BF16), shape(*full)
    dma = pltpu.SemaphoreType.DMA
    vmem = pltpu.VMEM
    exchange_sems = [dma((2, parts - 1)), dma((2, parts - 1)), dma((2,))]
    (tokens, own_upstream, first, query, keys, values, chance, attended, inverse, branch, middle, attended_low, second, picks, query_codes, key_code, vec) = pl.pallas_call(
        forward_kernel,
        out_shape=[low_full] * 6
        + [shape(HEADS, SLOTS, PADDED, dtype=BF16)]
        + [wide_full] * 4
        + [low_full] * 2
        + [shape(SLOTS, 128, dtype=BF16), shape(2, SLOTS, 128), shape(8, PADDED), shape(16, MODEL)],
        in_specs=[scalars()] * 3 + [whole()] * 14 + [far()] * 2,
        out_specs=[far()] * 12 + [whole()] * 5,
        scratch_shapes=[vmem(full, BF16)] * 5
        + [vmem(full, F32)] * 4
        + [
            vmem(full, BF16),
            vmem((2, 2, SLOTS, PADDED), BF16),
            vmem((HEADS, 2, 8, WIDE), F32),
            vmem((HEADS, 128, 128), BF16),
            vmem((STRIP, WIDE), F32),
            vmem((STRIP, WIDE), F32),
            vmem((STRIP, WIDE), F32),
            vmem((STRIP, WIDE), F32),
            vmem((16, LINES * 128), F32),
            vmem((LINES + 1, 16, 128), F32),
            vmem((25, 16, 128), F32),
            dma((10,)),
            dma((2,)),
        ]
        + exchange_sems,
        compiler_params=pltpu.CompilerParams(collective_id=0, has_side_effects=True, vmem_limit_bytes=VMEM_LIMIT),
        name="forward",
    )(
        grid_heights, grid_widths, packing_order, bias_table.T, *rows_of, input_weight, output_weight,
        layer_input, upstream,
    )

    outs = [(shape(parts, slots, MODEL, dtype=BF16), far())] * 2
    unit_shape, small_shape = (4, 4, 2, 144, 384), (8, 3, 16, 128)
    scratch = [
        vmem(full, F32),
        vmem(full, F32),
        vmem((SLOTS, 1024), BF16),
        vmem((SLOTS, 1024), BF16),
        vmem(full, BF16),
        vmem(full, F32),
        vmem(full, F32),
    ]
    scratch += [vmem(full, BF16)] * 8
    scratch += [
        vmem((2, MODEL, 1024), BF16),
        vmem((2, 1024, MODEL), BF16),
        vmem((2, 2, SLOTS, PADDED), BF16),
        vmem((SLOTS, PADDED), BF16),
        vmem((SLOTS, PADDED), BF16),
        vmem((HEADS, 2, 8, WIDE), F32),
        vmem((HEADS, 128, 128), F32),
        vmem((LINES + 1, 16, 128), F32),
        vmem((8, 8, MODEL), F32),
        vmem((2, 8, MODEL), F32),
        vmem((8, hidden_units), F32),
        vmem((16, MODEL), F32),
        vmem(unit_shape, BF16),
        vmem(small_shape, F32),
        dma((2, 2, BLOCKS)),
        dma((14,)),
        dma((2,)),
    ] + exchange_sems
    if paired:
        outs += [
            (shape(96, 768), whole()),
            (shape(192, 384), whole()),
            (shape(96, 384), whole()),
            (shape(96, 192), whole()),
            (shape(96, 192), whole()),
            (shape(*small_shape), whole()),
        ]
        for dims in (
            lambda r, c, cut: (2, 4, 2, r, c),
            lambda r, c, cut: (2, 4, cut, c),
            lambda r, c, cut: (4, 2, r - cut, c),
            lambda r, c, cut: (4, r, c),
            lambda r, c, cut: (3, r, c),
        ):
            scratch += [vmem(dims(*item, cut), BF16) for item, cut in zip(UNITS, SPLITS)]
        count = len(UNITS)
        scratch += [dma((count, 9)), dma((count, 9))]
        scratch += [
            vmem((7, 3, 16, 128), F32),
            vmem((3, 3, 16, 128), F32),
            vmem((3, 16, 128), F32),
            dma((17,)),
            dma((17,)),
        ]
    else:
        outs += [
            (shape(TILES, 4, 4, 2, 128, 384, dtype=BF16), far()),
            (shape(4, 4, 2, 144, 384, dtype=BF16), far()),
            (shape(4, 4, 2, 48, 384, dtype=BF16), far()),
            (shape(*small_shape), whole()),
        ]
    results = pl.pallas_call(
        functools.partial(backward_kernel, paired),
        out_shape=[item[0] for item in outs],
        in_specs=[scalars()] * 3 + [whole()] * 7 + [far()] * 14,
        out_specs=[item[1] for item in outs],
        scratch_shapes=scratch,
        compiler_params=pltpu.CompilerParams(collective_id=1, has_side_effects=True, vmem_limit_bytes=VMEM_LIMIT),
        name="backward",
    )(
        grid_heights, grid_widths, packing_order, vec, own_upstream, second, picks, query_codes, key_code, output_weight,
        up_weight, down_weight, input_weight, tokens, first, query, keys, values, attended, inverse, branch, middle,
        attended_low, chance,
    )
    own_output, own_gradient = results[:2]
    if paired:
        up_result, down_result, late_first, late_second, output_part, small = results[2:]
    else:
        feed_units, late_first, late_second, small = results[2:]
        up_unit, down_unit = restore_feed(feed_units)
        up_result, down_result = reduce_any_mesh(up_unit), reduce_any_mesh(down_unit)
        packed = jnp.concatenate([late_first[:, :, :, 96:144], late_second], 4).reshape(PARTS, BLOCKS, 48, 2, 2, 192)
        packed = jnp.transpose(packed, (3, 0, 1, 4, 2, 5)).reshape(2, PARTS, MODEL, 192)
        output_part, late_second = reduce_any_mesh(packed[0]), reduce_any_mesh(packed[1])
        late_first = reduce_any_mesh(late_first[:, :, :, 0:96].reshape(PARTS, MODEL, 384))
        small = lax.psum(small, ("rows", "seq"))
    lines = late_first.shape[0]
    done = pl.pallas_call(
        finish_kernel,
        out_shape=[
            shape(parts, slots, MODEL, dtype=BF16),
            shape(parts, slots, MODEL),
            shape(lines, 576),
            shape(lines, 192),
            shape(HEADS, SPAN * SPAN),
            shape(*up_result.shape),
            shape(*down_result.shape),
        ]
        + [shape(MODEL)] * 10
        + [shape(hidden_units)],
        in_specs=[whole()] * 8,
        out_specs=[whole()] * 18,
        scratch_shapes=[vmem((16, LINES * 128), F32)],
        compiler_params=pltpu.CompilerParams(vmem_limit_bytes=VMEM_LIMIT),
        name="finish",
    )(own_output, own_gradient, late_first, late_second, output_part, up_result, down_result, small.reshape(24, 16, 128))
    own_output, own_gradient, input_result, output_result, table, up_result, down_result = done[:7]
    vectors = done[7:]
    return (
        own_output,
        own_gradient,
        vectors[0],
        vectors[1],
        input_result,
        vectors[2],
        vectors[3],
        table.T,
        output_result,
        vectors[4],
        vectors[5],
        vectors[6],
        vectors[7],
        up_result,
        vectors[10],
        down_result if down_result.shape[1] == 192 else down_result.T,
        vectors[9],
        vectors[8],
    )


def finish_kernel(output_in, gradient_in, late_first, late_second, output_part, up_in, down_in, small, output, gradient, input_result, output_result, table, up_result, down_result, *rest):
    vectors, flat = rest[:-1], rest[-1]
    output[...] = output_in[...]
    for part in range(gradient.shape[0]):
        gradient[part] = gradient_in[part].astype(F32)
    first, second = late_first[...], late_second[...]
    pieces = [first[:, 0:128], first[:, 128:256], first[:, 256:384], second[:, 0:128], second[:, 128:192]]
    even = jnp.concatenate([pieces[0], pieces[3], pieces[1], pieces[2], pieces[4]], 1)
    odd = jnp.concatenate([pieces[4], pieces[0], pieces[1], pieces[3], pieces[2]], 1)
    side = jnp.full(even.shape, lax.rem(lax.axis_index("seq"), 2), jnp.int32)
    input_result[...] = jnp.where(side == 0, even, odd)
    output_result[...] = output_part[...]
    up_result[...] = up_in[...]
    down_result[...] = down_in[...]
    mirror = flip()
    for block in range(LINES):
        rest = small[block]
        total = jnp.zeros((16, 128), F32)
        for _ in range(3):
            low = rest.astype(BF16)
            total = total + dot(low, mirror)
            rest = rest - low.astype(F32)
        lanes = slice((LINES - 1 - block) * 128, (LINES - block) * 128)
        flat[:, lanes] = total
    table[...] = flat[0:HEADS, 0 : SPAN * SPAN]
    for number in range(14):
        target, start = vectors[min(number, 10)], max(number - 10, 0) * MODEL
        for block in range(6):
            row = small[LINES + block, number : number + 1, :]
            target[start + block * 128 : start + block * 128 + 128] = row.reshape(128)


def restore_feed(units):
    up = units[..., :96, :256].reshape(TILES, PARTS, BLOCKS, 96, 2, 128)
    up = jnp.transpose(up, (1, 2, 3, 4, 0, 5)).reshape(PARTS, MODEL, MODEL)
    low = units[..., :96, 256:].reshape(TILES, PARTS, BLOCKS, 96, 128)
    high = units[..., 96:, :].reshape(TILES, PARTS, BLOCKS, 32, 3, 128)
    high = jnp.transpose(high, (0, 1, 2, 4, 3, 5)).reshape(TILES, PARTS, BLOCKS, 96, 128)
    down = jnp.concatenate([low, high], 3)
    down = jnp.transpose(down, (1, 2, 0, 4, 3)).reshape(PARTS, BLOCKS * TILES * 128, 192)
    return up, down


def reduce_any_mesh(item):
    part = lax.psum_scatter(item, "seq", scatter_dimension=0, tiled=True)
    part = lax.psum_scatter(part.reshape(part.shape[1:]), "rows", scatter_dimension=0, tiled=True)
    return part.astype(F32)


def solution(mesh):
    split = P("rows", "seq", None)
    lines = P("rows", None)
    block = P("rows", "seq")
    in_specs = (split,) + (P(),) * 16 + (split, lines, lines, lines)
    out_specs = (split, split, P(), P(), block, P(), P(), P(), block, P(), P(), P(), P(), block, P(), block, P(), P())
    return jax.shard_map(on_device, mesh=mesh, in_specs=in_specs, out_specs=out_specs, check_vma=False)
```
